256 devices in a mesh: grp: 8 (over y, core), cand: 32 (over z, x).
Axes of the slice: x: 4, y: 4, z: 8, core: 2. Of those that a mesh axis runs over, the one named last changes fastest.
Arguments:
- history: bfloat16 [32, 512, 256], P('grp', 'cand'), parts along dimension 0, may hold values from -6 to 6
- cands: bfloat16 [32, 8192, 256], P('grp', 'cand'), parts along dimension 0, may hold values from -400 to 400, as said below
- surv_count: int32 [32, 32], P('grp', 'cand'), parts along dimension 0, may hold values from 1 to 256, 4096 in all within a row
- surv_index: int32 [32, 8192], P('grp', 'cand'), parts along dimension 0, may hold values from 0 to 255
- pre_wq: bfloat16 [256, 256], replicated, may hold values from -0.375 to 0.375
- pre_wkv: bfloat16 [256, 512], replicated, may hold values from -0.375 to 0.375
- rank_wq: bfloat16 [256, 1024], replicated, may hold values from -0.375 to 0.375
- rank_wkv: bfloat16 [256, 2048], replicated, may hold values from -0.375 to 0.375
- norm_gain: float32 [1024], replicated, may hold values from 0.1 to 1.9
- mlp_up: bfloat16 [1024, 4096], replicated, may hold values from -0.1875 to 0.1875
- score_w: bfloat16 [4096], replicated, may hold values from -0.09375 to 0.09375
Outputs:
- pre_score: float32 [32, 8192], P('grp', 'cand'), parts along dimension 0
- rank_score: float32 [32, 8192], P('grp', 'cand'), parts along dimension 0
The draws below stay inside these ranges and needn't reach their ends.
There are 8 independent parts, one for each index of `grp`. The reference program is written for one: setup_inputs(seed, part) draws one part's arguments, and reference() takes and returns one part's arrays. A program takes and returns all parts, laid end to end along the dimension named above; an argument that names none is the same for every part. Nothing has to cross between parts.
Inputs may be any that keep to these rules, and one draw needn't show every extreme that they name: `cands`: feature values of candidates lie within the stated range.
All inputs are finite; a program needn't handle non-finite values. No bound on the sum of `surv_count` on one device may be relied on, other than what follows from the above.
Results may differ from the reference program's by a relative error of at most 0.01.
The reference program's roundings to bfloat16 on the way count: a program that leaves them out, or rounds other values in their place, can miss the bound.
Values may be sent and summed in bfloat16 or wider, within the bound.
No kernel may reach another device: no remote copies, remote signals or barrier semaphores. Data moves between devices by JAX's collectives and lax.ppermute only.
A program may use at most 128 MiB of HBM per device.

```python
import math
import jax
import jax.numpy as jnp
import numpy as np
from jax import lax

E = 256
W = 1024
HEADS = 8
FF = 4096
REQ = 4
CPR = 256
HIST = 512
CAND = 8192
TOTAL = 4096
MOST = 256
SLOTS = 8192
N_CAND = 32


def draw_cands(key, part):
    key = jax.random.fold_in(key, 7)
    base = jax.random.normal(key, (REQ, CAND, E), jnp.float32)
    values = jnp.clip(base, -6.0, 6.0)
    return values.astype(jnp.bfloat16)


def place_ends(values, rng, low, top_value):
    dims = values.shape
    spot = [jax.random.randint(jax.random.fold_in(rng, axis), (), 0, dims[axis]) for axis in range(len(dims))]
    values = values.at[tuple(spot)].set(low)
    longest = dims.index(max(dims))
    spot[longest] = (spot[longest] + 1) % dims[longest]
    return values.at[tuple(spot)].set(top_value)


def block_levels(stream_key, dims, shards, low, largest):
    gain = 1.0
    for position, blocks in shards:
        steps = jax.random.uniform(jax.random.fold_in(jax.random.fold_in(stream_key, 6), position), (blocks,), jnp.float32, low / len(shards), largest / len(shards))
        gain = gain * jnp.repeat(jnp.exp(steps), dims[position] // blocks).reshape((-1,) + (1,) * (len(dims) - 1 - position))
    return gain


def length_profile(number_of, total, limit, lean):
    weights = [(1 << 20) // math.isqrt(standing ** lean) + 1 for standing in range(2, number_of + 1)]
    surplus, counts = total - limit - (number_of - 1), [1] * (number_of - 1)
    while surplus > 0:
        movable = [i for i in range(number_of - 1) if counts[i] < limit]
        whole, budget = sum([weights[i] for i in movable]), surplus
        for i in movable:
            addition = min(limit - counts[i], max(1, budget * weights[i] // whole), surplus)
            counts[i] = counts[i] + addition
            surplus = surplus - addition
    return np.array([limit] + counts)


def uneven(own_key, amount, total, limit, lean):
    if amount == 2:
        one = jax.random.randint(own_key, (), max(1, total - limit), min(limit, total - 1) + 1)
        return jnp.stack([one, total - one])
    tallies = jnp.asarray(length_profile(amount, total, limit, lean), jnp.int32)
    twos = (amount - 1) // 2
    donor, receiver = tallies[1:1 + 2 * twos:2], tallies[2:2 + 2 * twos:2]
    margin = jnp.minimum(donor - 1, limit - receiver)
    moved = jax.random.randint(jax.random.fold_in(own_key, 1), (twos,), 0, 1 << 20) % (margin + 1)
    tallies = tallies.at[1:1 + 2 * twos:2].set(donor - moved).at[2:2 + 2 * twos:2].set(receiver + moved)
    return tallies[jax.random.permutation(jax.random.fold_in(own_key, 2), amount)]


def noise(own_key, shape, scale, bound, cuts=(), kind=jnp.bfloat16):
    entries = scale * jax.random.normal(own_key, shape, jnp.float32)
    if cuts:
        entries = entries * block_levels(own_key, shape, cuts, -0.22, 0.18)
    return jnp.clip(entries, -bound, bound).astype(kind)


def setup_inputs(seed: int = 0, part: int = 0) -> dict:
    splits = jax.random.split(jax.random.key(seed), 12)
    part_keys = jax.random.split(jax.random.fold_in(splits[11], part), 12)
    history = noise(part_keys[0], (REQ, HIST, E), 1.0, 6.0, ((1, 32),))
    cands = draw_cands(jax.random.fold_in(jax.random.fold_in(splits[11], part), 71), part)
    surv_count = jax.vmap(lambda own: uneven(own, N_CAND, TOTAL, MOST, 2))(jax.random.split(part_keys[2], REQ)).reshape((REQ, N_CAND)).astype(jnp.int32)
    surv_index = place_ends(jax.random.randint(part_keys[3], (REQ, SLOTS), 0, CPR), jax.random.fold_in(part_keys[3], 1), 0, CPR - 1).astype(jnp.int32)
    pre_wq = noise(splits[4], (E, E), E ** -0.5, 0.375)
    pre_wkv = noise(splits[5], (E, 2 * E), E ** -0.5, 0.375)
    rank_wq = noise(splits[6], (E, W), E ** -0.5, 0.375)
    rank_wkv = noise(splits[7], (E, 2 * W), E ** -0.5, 0.375)
    norm_gain = jnp.clip(1.0 + 0.18 * jax.random.normal(splits[8], (W,), jnp.float32), 0.1, 1.9)
    mlp_up = noise(splits[9], (W, FF), W ** -0.5, 0.1875)
    score_w = noise(splits[10], (FF,), FF ** -0.5, 0.09375)
    return dict(history=history, cands=cands, surv_count=surv_count, surv_index=surv_index, pre_wq=pre_wq, pre_wkv=pre_wkv, rank_wq=rank_wq, rank_wkv=rank_wkv, norm_gain=norm_gain, mlp_up=mlp_up, score_w=score_w)


def rank_rows(rows, rank_kv, rank_wq, norm_gain, mlp_up, score_w):
    width = rank_wq.shape[1]
    head_size = width // HEADS
    count = rows.shape[0]
    query = jnp.dot(rows, rank_wq, preferred_element_type=jnp.float32).astype(jnp.bfloat16)
    query_heads = query.astype(jnp.float32).reshape(count, HEADS, head_size)
    keys = rank_kv[:, :width].astype(jnp.float32).reshape(-1, HEADS, head_size)
    values = rank_kv[:, width:].astype(jnp.float32).reshape(-1, HEADS, head_size)
    logits = jnp.einsum('nhd,khd->hnk', query_heads, keys) / math.sqrt(head_size)
    weights = jax.nn.softmax(logits, axis=-1).astype(jnp.bfloat16)
    attended = jnp.einsum('hnk,khd->nhd', weights.astype(jnp.float32), values).reshape(count, width)
    mixed = query.astype(jnp.float32) + attended
    center = lax.optimization_barrier(jnp.mean(mixed, axis=-1, keepdims=True))
    spread = lax.optimization_barrier(jnp.mean((mixed - center) ** 2, axis=-1, keepdims=True))
    normed = ((mixed - center) * lax.rsqrt(spread + 1e-05) * norm_gain).astype(jnp.bfloat16)
    hidden = jax.nn.gelu(jnp.dot(normed, mlp_up, preferred_element_type=jnp.float32)).astype(jnp.bfloat16)
    return jnp.dot(hidden, score_w, preferred_element_type=jnp.float32)

def reference(history, cands, surv_count, surv_index, pre_wq, pre_wkv, rank_wq, rank_wkv, norm_gain, mlp_up, score_w):
    width_pre = pre_wq.shape[0]

    def pre_one(pair):
        events, candidates = pair
        query = jnp.dot(candidates, pre_wq, preferred_element_type=jnp.float32).astype(jnp.bfloat16)
        pairs = jnp.dot(events, pre_wkv, preferred_element_type=jnp.float32).astype(jnp.bfloat16)
        keys = pairs[:, :width_pre]
        values = pairs[:, width_pre:]
        logits = jnp.dot(query, keys.T, preferred_element_type=jnp.float32) / math.sqrt(width_pre)
        weights = jax.nn.softmax(logits, axis=-1).astype(jnp.bfloat16)
        pooled = jnp.dot(weights, values, preferred_element_type=jnp.float32)
        query_f = query.astype(jnp.float32)
        length = jnp.sqrt(lax.optimization_barrier(jnp.sum(query_f * query_f, axis=-1)))
        return lax.optimization_barrier(jnp.sum(pooled * query_f, axis=-1)) / (1.0 + length)
    pre_score = lax.map(pre_one, (history, cands))
    slot = jnp.arange(MOST, dtype=jnp.int32)
    offsets = jnp.cumsum(surv_count, axis=1).astype(jnp.int32) - surv_count
    lists = surv_index.reshape(REQ, N_CAND, MOST)
    global_index = lists + (jnp.arange(N_CAND, dtype=jnp.int32) * CPR)[None, :, None]
    valid = slot[None, None, :] < surv_count[:, :, None]
    place = jnp.where(valid, offsets[:, :, None] + slot[None, None, :], TOTAL).astype(jnp.int32)

    def rank_one(group):
        events, candidates, picks, spots = group
        rows = candidates[picks.reshape(-1)]
        packed = jnp.zeros((TOTAL, candidates.shape[1]), jnp.bfloat16).at[spots.reshape(-1)].set(rows, mode='drop')
        pairs = jnp.dot(events, rank_wkv, preferred_element_type=jnp.float32).astype(jnp.bfloat16)
        ranked = rank_rows(packed, pairs, rank_wq, norm_gain, mlp_up, score_w)
        return ranked[jnp.minimum(spots, TOTAL - 1)]
    ranked = lax.map(rank_one, (history, cands, global_index, place))
    rank_score = jnp.where(valid, ranked, 0.0).reshape(REQ, SLOTS)
    return (pre_score, rank_score)
```

```python
import functools
import math

import jax
import jax.numpy as jnp
from jax import lax
from jax.experimental import pallas as pl
from jax.experimental.pallas import tpu as pltpu
from jax.sharding import PartitionSpec as P

HEADS = 8
BF = jnp.bfloat16
F32 = jnp.float32
I32 = jnp.int32
LOG2E = 1.4426950408889634
GELU_A = math.sqrt(2.0 / math.pi)
GELU_B = GELU_A * 0.044715
ROW_TILE = 128
MLP_ROWS = 256
MLP_COLS = 512
VMEM = pl.BlockSpec(memory_space=pltpu.VMEM)
SMEM = pl.BlockSpec(memory_space=pltpu.SMEM)
ANY = pl.BlockSpec(memory_space=pl.ANY)


def dot(a, b):
    return jnp.dot(a, b, preferred_element_type=F32)


def dot_t(a, b):
    return lax.dot_general(a, b, (((1,), (1,)), ((), ())), preferred_element_type=F32)


def select_kernel(count_ref, index_ref, cands_ref, wq_ref, pre_wqt_ref, q_ref, pre_q_ref, place_ref, start_ref):
    requests, slots = index_ref.shape
    cands = cands_ref.shape[1]
    row_c = lax.broadcasted_iota(I32, (cands, slots), 0)
    lane = lax.broadcasted_iota(I32, (1, slots), 1)
    before = (
        lax.broadcasted_iota(I32, (cands, cands), 0) < lax.broadcasted_iota(I32, (cands, cands), 1)
    ).astype(BF)
    place_c = lax.broadcasted_iota(I32, (slots, cands), 0).astype(F32)
    ones = jnp.ones((8, slots), BF)
    start = jnp.int32(0)
    for r in range(requests):
        valid = lane < count_ref[r, 0]
        picked = jnp.where(valid, index_ref[r : r + 1, :], -1)
        match = (row_c == picked).astype(F32).astype(BF)
        used = jnp.where(dot_t(ones, match) > 0.5, 1.0, 0.0)
        position = dot(used.astype(BF), before)
        number = jnp.sum(used[0:1, :]).astype(I32)
        slot_place = dot(position.astype(BF), match)[0:1, :].astype(I32)
        place_ref[r : r + 1, :] = jnp.where(valid, slot_place, -1)
        chosen = jnp.where((used[0:1, :] > 0.5) & (position[0:1, :] == place_c), 1.0, 0.0).astype(BF)
        mine = cands_ref[r]
        rows = dot(chosen, mine).astype(BF)
        q_ref[pl.ds(pl.multiple_of(start, 16), slots), :] = dot(rows, wq_ref[...]).astype(BF)
        start_ref[r] = start
        start_ref[8 + r] = number
        start = start + (((number + 15) >> 4) << 4)
        pre_q_ref[r] = dot_t(pre_wqt_ref[...], mine).astype(BF)
    start_ref[requests] = start


def rank_kernel(
    start_ref,
    own_ref,
    left_ref,
    right_ref,
    far_ref,
    q_hbm,
    pre_q_ref,
    place_ref,
    pre_wk_ref,
    pre_wvt_ref,
    wkv_ref,
    gain_ref,
    up_hbm,
    score_w_ref,
    pre_out,
    rank_out,
    up_ref,
    q_ref,
    keys_ref,
    values_ref,
    normed_ref,
    ranked_ref,
    sems,
):
    requests = pre_q_ref.shape[0]
    events = keys_ref.shape[0]
    width = keys_ref.shape[1]
    head = width // HEADS
    up_copy = pltpu.make_async_copy(up_hbm, up_ref, sems.at[0])
    q_copy = pltpu.make_async_copy(q_hbm, q_ref, sems.at[1])
    q_copy.start()
    up_copy.start()
    for h in range(HEADS):
        values_ref[:, (2 * h + 1) * head : (2 * h + 2) * head] = jnp.ones((events, head), BF)
    q_copy.wait()

    def request(r, carry):
        parts = [
            ref[:, pl.ds(r, 1)].reshape(events // 4, ref.shape[-1])
            for ref in (own_ref, left_ref, right_ref, far_ref)
        ]
        history = jnp.concatenate(parts, axis=0)
        pre_q = pre_q_ref[pl.ds(r, 1)][0]
        pre_keys = dot(history, pre_wk_ref[...]).astype(BF)
        pre_values = dot_t(pre_wvt_ref[...], history).astype(BF)
        logits = dot(pre_keys, pre_q)
        top = jnp.max(logits, axis=0, keepdims=True)
        weights = jnp.exp2((logits - top) * (LOG2E / math.sqrt(pre_q.shape[0])))
        weights = (weights * (1.0 / jnp.sum(weights, axis=0, keepdims=True))).astype(BF)
        pooled = dot(pre_values, weights)
        query = pre_q.astype(F32)
        length = jnp.sqrt(jnp.sum(query * query, axis=0, keepdims=True))
        pre_out[pl.ds(r, 1), :] = jnp.sum(pooled * query, axis=0, keepdims=True) / (1.0 + length)
        for c in range(2):
            cols = slice(c * width // 2, (c + 1) * width // 2)
            keys_ref[:, cols] = dot(history, wkv_ref[:, cols]).astype(BF)
        for c in range(2):
            part = dot(history, wkv_ref[:, width + c * width // 2 : width + (c + 1) * width // 2]).astype(BF)
            for k in range(HEADS // 2):
                h = c * HEADS // 2 + k
                values_ref[:, 2 * h * head : (2 * h + 1) * head] = part[:, k * head : (k + 1) * head]
        start = start_ref[r]
        scale = LOG2E / math.sqrt(head)

        def tile(t, carry):
            at = pl.ds(pl.multiple_of(start + t * ROW_TILE, 16), ROW_TILE)
            mixed = []
            total = jnp.zeros((ROW_TILE, 1), F32)
            for h in range(HEADS):
                cols = slice(h * head, (h + 1) * head)
                query = q_ref[at, cols]
                logits = dot_t(query, keys_ref[:, cols])
                top = jnp.max(logits, axis=1, keepdims=True)
                weights = jnp.exp2((logits - top) * scale).astype(BF)
                both = dot(weights, values_ref[:, 2 * h * head : (2 * h + 2) * head])
                one = query.astype(F32) + both[:, :head] / both[:, head:]
                mixed.append(one)
            acc = mixed[0]
            for one in mixed[1:]:
                acc = acc + one
            center = jnp.sum(acc, axis=1, keepdims=True) * (1.0 / width)
            acc = jnp.zeros((ROW_TILE, head), F32)
            for one in mixed:
                acc = acc + (one - center) * (one - center)
            spread = jnp.sum(acc, axis=1, keepdims=True) * (1.0 / width)
            inverse = lax.rsqrt(spread + 1e-05)
            for h in range(HEADS):
                cols = slice(h * head, (h + 1) * head)
                normed_ref[at, cols] = ((mixed[h] - center) * inverse * gain_ref[:, cols]).astype(BF)
            return carry

        lax.fori_loop(0, (start_ref[8 + r] + ROW_TILE - 1) // ROW_TILE, tile, 0)
        return carry

    lax.fori_loop(0, requests, request, 0)
    up_copy.wait()
    total = start_ref[requests]
    hidden_size = up_ref.shape[1]

    def mlp(t, carry):
        at = pl.ds(pl.multiple_of(t * MLP_ROWS, MLP_ROWS), MLP_ROWS)
        rows = normed_ref[at, :]
        acc = jnp.zeros((MLP_ROWS, 128), F32)
        for j in range(hidden_size // MLP_COLS):
            cols = slice(j * MLP_COLS, (j + 1) * MLP_COLS)
            x = dot(rows, up_ref[:, cols])
            half = 0.5 * x
            x = half + half * jnp.tanh(x * (GELU_A + GELU_B * (x * x)))
            x = x.astype(BF).astype(F32) * score_w_ref[:, cols]
            for k in range(MLP_COLS // 128):
                acc = acc + x[:, k * 128 : (k + 1) * 128]
        ranked_ref[at, :] = jnp.broadcast_to(jnp.sum(acc, axis=1, keepdims=True), acc.shape)
        return carry

    lax.fori_loop(0, (total + MLP_ROWS - 1) // MLP_ROWS, mlp, 0)
    slots = place_ref.shape[1]
    row = lax.broadcasted_iota(I32, (slots, slots), 0)
    for r in range(requests):
        ranked = ranked_ref[pl.ds(pl.multiple_of(start_ref[r], 16), slots), :]
        ranked = jnp.concatenate([ranked] * (slots // 128), axis=1)
        hit = row == place_ref[r : r + 1, :]
        rank_out[r : r + 1, :] = jnp.sum(jnp.where(hit, ranked, 0.0), axis=0, keepdims=True)


def body(history, cands, surv_count, surv_index, pre_wq, pre_wkv, rank_wq, rank_wkv, norm_gain, mlp_up, score_w):
    requests, here, features = history.shape
    slots = surv_index.shape[1]
    width = rank_wq.shape[1]
    hidden = mlp_up.shape[1]
    shards = lax.axis_size("cand")
    nx = 4
    nz = shards // nx
    events = here * shards
    columns = [[z * nx + x for z in range(nz)] for x in range(nx)]

    def shift(x, by):
        pairs = [(z * nx + a, z * nx + (a + by) % nx) for z in range(nz) for a in range(nx)]
        return lax.ppermute(x, "cand", pairs)

    copies = jnp.broadcast_to(history[None], (nz,) + history.shape)
    own = lax.all_to_all(copies, "cand", split_axis=0, concat_axis=0, tiled=True, axis_index_groups=columns)
    left, right, far = shift(own, 1), shift(own, 3), shift(own, 2)

    q, pre_q, place, start = pl.pallas_call(
        select_kernel,
        name="select",
        out_shape=(
            jax.ShapeDtypeStruct((requests * slots, width), BF),
            jax.ShapeDtypeStruct((requests, features, slots), BF),
            jax.ShapeDtypeStruct((requests, slots), I32),
            jax.ShapeDtypeStruct((16,), I32),
        ),
        in_specs=[SMEM, VMEM, VMEM, VMEM, VMEM],
        out_specs=(VMEM, VMEM, VMEM, SMEM),
        compiler_params=pltpu.CompilerParams(vmem_limit_bytes=24 * 2**20),
        cost_estimate=pl.CostEstimate(flops=2 * 10**9, bytes_accessed=4 * 2**20, transcendentals=0),
    )(surv_count, surv_index, cands, rank_wq, pre_wq.T)

    pre_score, rank_score = pl.pallas_call(
        rank_kernel,
        name="rank",
        out_shape=(
            jax.ShapeDtypeStruct((requests, slots), F32),
            jax.ShapeDtypeStruct((requests, slots), F32),
        ),
        in_specs=[SMEM, VMEM, VMEM, VMEM, VMEM, ANY, VMEM, VMEM, VMEM, VMEM, VMEM, VMEM, ANY, VMEM],
        out_specs=(VMEM, VMEM),
        scratch_shapes=[
            pltpu.VMEM(mlp_up.shape, BF),
            pltpu.VMEM((requests * slots, width), BF),
            pltpu.VMEM((events, width), BF),
            pltpu.VMEM((events, 2 * width), BF),
            pltpu.VMEM((requests * slots, width), BF),
            pltpu.VMEM((requests * slots, 128), F32),
            pltpu.SemaphoreType.DMA((2,)),
        ],
        compiler_params=pltpu.CompilerParams(vmem_limit_bytes=52 * 2**20),
        cost_estimate=pl.CostEstimate(flops=10**10, bytes_accessed=16 * 2**20, transcendentals=4 * 10**6),
    )(
        start,
        own,
        left,
        right,
        far,
        q,
        pre_q,
        place,
        pre_wkv[:, :features],
        pre_wkv[:, features:].T,
        rank_wkv,
        norm_gain.reshape(1, -1),
        mlp_up,
        score_w.astype(F32).reshape(1, -1),
    )
    return pre_score, rank_score


def solution(mesh):
    in_specs = (
        P("grp", "cand", None),
        P("grp", "cand", None),
        P("grp", "cand"),
        P("grp", "cand"),
        P(),
        P(),
        P(),
        P(),
        P(),
        P(),
        P(),
    )
    out_specs = (P("grp", "cand"), P("grp", "cand"))
    return jax.shard_map(body, mesh=mesh, in_specs=in_specs, out_specs=out_specs, check_vma=False)
```

```python
import functools
import math

import jax
import jax.numpy as jnp
from jax import lax
from jax.experimental import pallas as pl
from jax.experimental.pallas import tpu as pltpu
from jax.sharding import PartitionSpec as P

HEADS = 8
BF = jnp.bfloat16
F32 = jnp.float32
I32 = jnp.int32
LOG2E = 1.4426950408889634
GELU_A = math.sqrt(2.0 / math.pi)
GELU_B = GELU_A * 0.044715
ROW_TILES = (128, 192, 256)
MLP_ROWS = 128
MLP_COLS = 512
PRE_Q = 1024
PRE_WKV = 1280
PACK = 1536
SELECT_LIMIT = 12 * 2**20
FIRST_LIMIT = 50 * 2**20
LAST_LIMIT = 50 * 2**20
VMEM = pl.BlockSpec(memory_space=pltpu.VMEM)
SMEM = pl.BlockSpec(memory_space=pltpu.SMEM)
HBM = pl.BlockSpec(memory_space=pltpu.HBM)


def dot(a, b):
    return jnp.dot(a, b, preferred_element_type=F32)


def dot_t(a, b):
    return lax.dot_general(a, b, (((1,), (1,)), ((), ())), preferred_element_type=F32)


def select_kernel(
    count_ref,
    index_ref,
    cands_hbm,
    wq_hbm,
    pre_wq_hbm,
    pre_wkv_hbm,
    gain_ref,
    pack_ref,
    place_ref,
    start_ref,
    gain_out,
    cands_ref,
    wq_ref,
    pre_wq_ref,
    sems,
):
    pairs = (
        (cands_hbm, cands_ref),
        (wq_hbm, wq_ref),
        (pre_wq_hbm, pre_wq_ref),
        (pre_wkv_hbm, pack_ref.at[pl.ds(PRE_WKV, pre_wkv_hbm.shape[0]), pl.ds(0, pre_wkv_hbm.shape[1])]),
    )
    copies = [pltpu.make_async_copy(a, b, sems.at[i]) for i, (a, b) in enumerate(pairs)]
    for copy in copies:
        copy.start()
    gain_out[...] = gain_ref[...]
    requests, slots = index_ref.shape
    _, cands, features = cands_ref.shape
    row_c = lax.broadcasted_iota(I32, (cands, slots), 0)
    lane = lax.broadcasted_iota(I32, (1, slots), 1)
    before = (
        lax.broadcasted_iota(I32, (cands, cands), 0) < lax.broadcasted_iota(I32, (cands, cands), 1)
    ).astype(BF)
    place_c = lax.broadcasted_iota(I32, (slots, cands), 0).astype(F32)
    ones = jnp.ones((8, slots), BF)
    for copy in copies:
        copy.wait()
    start = jnp.int32(0)
    for r in range(requests):
        valid = lane < count_ref[r]
        picked = jnp.where(valid, index_ref[r : r + 1, :], -1)
        match = (row_c == picked).astype(F32).astype(BF)
        used = jnp.where(dot_t(ones, match) > 0.5, 1.0, 0.0)
        position = dot(used.astype(BF), before)
        number = jnp.sum(used[0:1, :]).astype(I32)
        slot_place = dot(position.astype(BF), match)[0:1, :].astype(I32)
        place_ref[r : r + 1, :] = jnp.where(valid, slot_place, -1)
        chosen = jnp.where((used[0:1, :] > 0.5) & (position[0:1, :] == place_c), 1.0, 0.0).astype(BF)
        mine = cands_ref[r]
        rows = dot(chosen, mine).astype(BF)
        pack_ref[pl.ds(pl.multiple_of(start, 16), slots), :] = dot(rows, wq_ref[...]).astype(BF)
        start_ref[r] = start
        start_ref[8 + r] = number
        start = start + (((number + 15) >> 4) << 4)
        pack_ref[PRE_Q : PRE_Q + features, r * slots : (r + 1) * slots] = lax.dot_general(
            pre_wq_ref[...], mine, (((0,), (1,)), ((), ())), preferred_element_type=F32
        ).astype(BF)
    start_ref[requests] = start
    start_ref[15] = 0


def attend(
    first,
    count,
    start_ref,
    own_ref,
    chunk_refs,
    pack_hbm,
    wkv_ref,
    gain_ref,
    pre_out,
    pack_ref,
    sems,
    keys_ref,
    values_ref,
    normed_ref,
):
    slots = pre_out.shape[1]
    rows = [(PRE_Q, PACK - PRE_Q), (0, (first + count) * slots)]
    copies = [
        pltpu.make_async_copy(pack_hbm.at[pl.ds(*at)], pack_ref.at[pl.ds(*at)], sems.at[i]) for i, at in enumerate(rows)
    ]
    for copy in copies:
        copy.start()
    events, width = keys_ref.shape
    head = width // HEADS
    features = wkv_ref.shape[0]
    pre_wk = (pl.ds(PRE_WKV, features), pl.ds(0, features))
    pre_wv = (pl.ds(PRE_WKV, features), pl.ds(features, features))
    scale = LOG2E / math.sqrt(head)
    for h in range(HEADS):
        values_ref[:, (2 * h + 1) * head : (2 * h + 2) * head] = jnp.ones((events, head), BF)
    for copy in copies:
        copy.wait()

    def request(i, carry):
        r = first + i
        parts = [own_ref[:, pl.ds(r, 1)].reshape(events // 4, features)]
        parts += [ref[:, pl.ds(i, 1)].reshape(events // 4, features) for ref in chunk_refs]
        history = jnp.concatenate(parts, axis=0)
        pre_q = pack_ref[PRE_Q : PRE_Q + features, pl.ds(pl.multiple_of(r * slots, slots), slots)]
        pre_keys = dot(history, pack_ref[pre_wk]).astype(BF)
        pre_values = lax.dot_general(
            pack_ref[pre_wv], history, (((0,), (1,)), ((), ())), preferred_element_type=F32
        ).astype(BF)
        logits = dot(pre_keys, pre_q)
        top = jnp.max(logits, axis=0, keepdims=True)
        weights = jnp.exp2((logits - top) * (LOG2E / math.sqrt(features)))
        weights = (weights * (1.0 / jnp.sum(weights, axis=0, keepdims=True))).astype(BF)
        pooled = dot(pre_values, weights)
        query = pre_q.astype(F32)
        length = jnp.sqrt(jnp.sum(query * query, axis=0, keepdims=True))
        pre_out[pl.ds(r, 1), :] = jnp.sum(pooled * query, axis=0, keepdims=True) / (1.0 + length)
        for c in range(2):
            cols = slice(c * width // 2, (c + 1) * width // 2)
            keys_ref[:, cols] = dot(history, wkv_ref[:, cols]).astype(BF)
        for c in range(2):
            part = dot(history, wkv_ref[:, width + c * width // 2 : width + (c + 1) * width // 2]).astype(BF)
            for k in range(HEADS // 2):
                h = c * HEADS // 2 + k
                values_ref[:, 2 * h * head : (2 * h + 1) * head] = part[:, k * head : (k + 1) * head]

        def tile(rows):
            at = pl.ds(pl.multiple_of(start_ref[r], 16), rows)
            mixed = []
            for h in range(HEADS):
                cols = slice(h * head, (h + 1) * head)
                query = pack_ref[at, cols]
                logits = dot_t(query, keys_ref[:, cols])
                top = jnp.max(logits, axis=1, keepdims=True)
                weights = jnp.exp2((logits - top) * scale).astype(BF)
                both = dot(weights, values_ref[:, 2 * h * head : (2 * h + 2) * head])
                mixed.append(query.astype(F32) + both[:, :head] / both[:, head:])
            acc = mixed[0]
            for one in mixed[1:]:
                acc = acc + one
            center = jnp.sum(acc, axis=1, keepdims=True) * (1.0 / width)
            acc = jnp.zeros((rows, head), F32)
            for one in mixed:
                acc = acc + (one - center) * (one - center)
            spread = jnp.sum(acc, axis=1, keepdims=True) * (1.0 / width)
            inverse = lax.rsqrt(spread + 1e-05)
            for h in range(HEADS):
                cols = slice(h * head, (h + 1) * head)
                normed_ref[at, cols] = ((mixed[h] - center) * inverse * gain_ref[:, cols]).astype(BF)

        number = start_ref[8 + r]
        low = 0
        for rows in ROW_TILES:
            pl.when((number > low) & (number <= rows))(functools.partial(tile, rows))
            low = rows
        return carry

    lax.fori_loop(0, count, request, 0)


def first_kernel(
    start_ref, own_ref, a_ref, b_ref, c_ref, pack_hbm, wkv_ref, gain_ref,
    pre_out, normed_ref,
    keys_ref, values_ref, pack_ref, sems,
):
    attend(
        0, a_ref.shape[1], start_ref, own_ref, (a_ref, b_ref, c_ref), pack_hbm, wkv_ref, gain_ref,
        pre_out, pack_ref, sems, keys_ref, values_ref, normed_ref,
    )


def last_kernel(
    start_ref, own_ref, a_ref, b_ref, c_ref, pack_hbm, wkv_ref, gain_ref,
    pre_before, normed_before, place_ref, up_hbm, score_w_ref,
    pre_out, rank_out,
    keys_ref, values_ref, pack_ref, sems, normed_ref, ranked_ref, up_ref, sem,
):
    up_copy = pltpu.make_async_copy(up_hbm, up_ref, sem)
    up_copy.start()
    requests, slots = place_ref.shape
    half = requests - a_ref.shape[1]
    pre_out[:half, :] = pre_before[...]
    normed_ref[: half * slots, :] = normed_before[...]
    attend(
        half, requests - half, start_ref, own_ref, (a_ref, b_ref, c_ref), pack_hbm, wkv_ref,
        gain_ref, pre_out, pack_ref, sems, keys_ref, values_ref, normed_ref,
    )
    up_copy.wait()
    total = start_ref[requests]
    hidden_size = up_ref.shape[1]

    def mlp(t, carry):
        at = pl.ds(pl.multiple_of(t * MLP_ROWS, MLP_ROWS), MLP_ROWS)
        rows = normed_ref[at, :]
        acc = jnp.zeros((MLP_ROWS, 128), F32)
        for j in range(hidden_size // MLP_COLS):
            cols = slice(j * MLP_COLS, (j + 1) * MLP_COLS)
            x = dot(rows, up_ref[:, cols])
            half = 0.5 * x
            x = half + half * jnp.tanh(x * (GELU_A + GELU_B * (x * x)))
            x = x.astype(BF).astype(F32)
            for k in range(MLP_COLS // 128):
                at_w = j * (MLP_COLS // 128) + k
                acc = acc + x[:, k * 128 : (k + 1) * 128] * score_w_ref[at_w : at_w + 1, :].astype(F32)
        ranked_ref[at, :] = jnp.broadcast_to(jnp.sum(acc, axis=1, keepdims=True), acc.shape)
        return carry

    lax.fori_loop(0, (total + MLP_ROWS - 1) // MLP_ROWS, mlp, 0)
    row = lax.broadcasted_iota(I32, (slots, slots), 0)
    for r in range(requests):
        ranked = ranked_ref[pl.ds(pl.multiple_of(start_ref[r], 16), slots), :]
        ranked = jnp.concatenate([ranked] * (slots // 128), axis=1)
        hit = row == place_ref[r : r + 1, :]
        rank_out[r : r + 1, :] = jnp.sum(jnp.where(hit, ranked, 0.0), axis=0, keepdims=True)


def select_call(surv_count, surv_index, cands, rank_wq, pre_wq, pre_wkv, norm_gain):
    requests, slots = surv_index.shape
    width = rank_wq.shape[1]
    return pl.pallas_call(
        select_kernel,
        name="select",
        out_shape=(
            jax.ShapeDtypeStruct((PACK, width), BF),
            jax.ShapeDtypeStruct((requests, slots), I32),
            jax.ShapeDtypeStruct((16,), I32),
            jax.ShapeDtypeStruct((1, width), F32),
        ),
        in_specs=[SMEM, VMEM, HBM, HBM, HBM, HBM, VMEM],
        out_specs=(VMEM, VMEM, SMEM, VMEM),
        scratch_shapes=[
            pltpu.VMEM(cands.shape, BF),
            pltpu.VMEM(rank_wq.shape, BF),
            pltpu.VMEM(pre_wq.shape, BF),
            pltpu.SemaphoreType.DMA((4,)),
        ],
        compiler_params=pltpu.CompilerParams(vmem_limit_bytes=SELECT_LIMIT),
        cost_estimate=pl.CostEstimate(flops=2 * 10**9, bytes_accessed=12 * 2**20, transcendentals=0),
    )(surv_count.reshape(requests), surv_index, cands, rank_wq, pre_wq, pre_wkv, norm_gain.reshape(1, -1))


def rank_call(start, own, chunks, pack, place, rank_wkv, gain, mlp_up, score_w):
    requests, slots = place.shape
    width = pack.shape[1]
    events = 4 * own.shape[0] * own.shape[2]
    half = requests // 2
    attention = [
        pltpu.VMEM((events, width), BF),
        pltpu.VMEM((events, 2 * width), BF),
        pltpu.VMEM(pack.shape, BF),
        pltpu.SemaphoreType.DMA((2,)),
    ]
    pre_before, normed_before = pl.pallas_call(
        first_kernel,
        name="rank_first",
        out_shape=(
            jax.ShapeDtypeStruct((half, slots), F32),
            jax.ShapeDtypeStruct((half * slots, width), BF),
        ),
        in_specs=[SMEM] + [VMEM] * 4 + [HBM] + [VMEM] * 2,
        out_specs=(VMEM, VMEM),
        scratch_shapes=attention,
        compiler_params=pltpu.CompilerParams(vmem_limit_bytes=FIRST_LIMIT),
        cost_estimate=pl.CostEstimate(flops=5 * 10**9, bytes_accessed=4 * 2**20, transcendentals=4 * 10**6),
    )(start, own, *chunks[0], pack, rank_wkv, gain)
    return pl.pallas_call(
        last_kernel,
        name="rank_last",
        out_shape=(
            jax.ShapeDtypeStruct((requests, slots), F32),
            jax.ShapeDtypeStruct((requests, slots), F32),
        ),
        in_specs=[SMEM] + [VMEM] * 4 + [HBM] + [VMEM] * 5 + [HBM, VMEM],
        out_specs=(VMEM, VMEM),
        scratch_shapes=attention
        + [
            pltpu.VMEM((requests * slots, width), BF),
            pltpu.VMEM((requests * slots, 128), F32),
            pltpu.VMEM(mlp_up.shape, BF),
            pltpu.SemaphoreType.DMA,
        ],
        compiler_params=pltpu.CompilerParams(vmem_limit_bytes=LAST_LIMIT),
        cost_estimate=pl.CostEstimate(flops=12 * 10**9, bytes_accessed=16 * 2**20, transcendentals=8 * 10**6),
    )(
        start, own, *chunks[1], pack, rank_wkv, gain,
        pre_before, normed_before, place, mlp_up, score_w.reshape(-1, 128),
    )


def body(history, cands, surv_count, surv_index, pre_wq, pre_wkv, rank_wq, rank_wkv, norm_gain, mlp_up, score_w):
    requests = history.shape[0]
    half = requests // 2
    nx = 4
    nz = lax.axis_size("cand") // nx
    columns = [[z * nx + x for z in range(nz)] for x in range(nx)]

    def shift(x, by):
        pairs = [(z * nx + a, z * nx + (a + by) % nx) for z in range(nz) for a in range(nx)]
        return lax.ppermute(x, "cand", pairs)

    copies = jnp.broadcast_to(history[None], (nz,) + history.shape)
    own = lax.all_to_all(copies, "cand", split_axis=0, concat_axis=0, tiled=True, axis_index_groups=columns)
    pack, place, start, gain = select_call(surv_count, surv_index, cands, rank_wq, pre_wq, pre_wkv, norm_gain)
    after = start[15].astype(BF)
    chunks = []
    for part in (own[:, :half] + after, own[:, half:] + after):
        chunks.append([shift(part, by) for by in (2, 1, 3)])
    return rank_call(start, own, chunks, pack, place, rank_wkv, gain, mlp_up, score_w)


def solution(mesh):
    in_specs = (
        P("grp", "cand", None),
        P("grp", "cand", None),
        P("grp", "cand"),
        P("grp", "cand"),
        P(),
        P(),
        P(),
        P(),
        P(),
        P(),
        P(),
    )
    out_specs = (P("grp", "cand"), P("grp", "cand"))
    return jax.shard_map(body, mesh=mesh, in_specs=in_specs, out_specs=out_specs, check_vma=False)
```

```python
import functools
import math

import jax
import jax.numpy as jnp
from jax import lax
from jax.experimental import pallas as pl
from jax.experimental.pallas import tpu as pltpu
from jax.sharding import PartitionSpec as P

HEADS = 8
BF = jnp.bfloat16
F32 = jnp.float32
I32 = jnp.int32
LOG2E = 1.4426950408889634
GELU_A = math.sqrt(2.0 / math.pi)
GELU_B = GELU_A * 0.044715
ROW_TILES = (128, 192, 256)
MLP_ROWS = 128
MLP_COLS = 512
PRE_Q = 1024
PRE_WKV = 1280
RANK_WK = 1536
RANK_WV = 1792
PACK = 2048
SELECT_LIMIT = 57 * 2**20
RANK_LIMIT = 50 * 2**20
VMEM = pl.BlockSpec(memory_space=pltpu.VMEM)
SMEM = pl.BlockSpec(memory_space=pltpu.SMEM)
HBM = pl.BlockSpec(memory_space=pltpu.HBM)


def dot(a, b):
    return jnp.dot(a, b, preferred_element_type=F32)


def dot_t(a, b):
    return lax.dot_general(a, b, (((1,), (1,)), ((), ())), preferred_element_type=F32)


def select_kernel(
    count_ref,
    index_ref,
    cands_hbm,
    wq_hbm,
    pre_wq_hbm,
    pre_wkv_hbm,
    wkv_hbm,
    gain_ref,
    score_w_ref,
    pack_ref,
    place_ref,
    start_ref,
    small_ref,
    cands_ref,
    wq_ref,
    pre_wq_ref,
    sems,
):
    width = pack_ref.shape[1]
    pairs = (
        (cands_hbm, cands_ref),
        (wq_hbm, wq_ref),
        (pre_wq_hbm, pre_wq_ref),
        (pre_wkv_hbm, pack_ref.at[pl.ds(PRE_WKV, pre_wkv_hbm.shape[0]), pl.ds(0, pre_wkv_hbm.shape[1])]),
        (wkv_hbm.at[:, pl.ds(0, width)], pack_ref.at[pl.ds(RANK_WK, RANK_WV - RANK_WK)]),
        (wkv_hbm.at[:, pl.ds(width, width)], pack_ref.at[pl.ds(RANK_WV, PACK - RANK_WV)]),
    )
    copies = [pltpu.make_async_copy(a, b, sems.at[i]) for i, (a, b) in enumerate(pairs)]
    for copy in copies:
        copy.start()
    small_ref[:HEADS, :] = gain_ref[...]
    small_ref[HEADS:, :] = score_w_ref[...].astype(F32)
    requests, slots = index_ref.shape
    _, cands, features = cands_ref.shape
    row_c = lax.broadcasted_iota(I32, (cands, slots), 0)
    lane = lax.broadcasted_iota(I32, (1, slots), 1)
    before = (
        lax.broadcasted_iota(I32, (cands, cands), 0) < lax.broadcasted_iota(I32, (cands, cands), 1)
    ).astype(BF)
    place_c = lax.broadcasted_iota(I32, (slots, cands), 0).astype(F32)
    ones = jnp.ones((8, slots), BF)
    for copy in copies[:3]:
        copy.wait()
    start = jnp.int32(0)
    for r in range(requests):
        valid = lane < count_ref[r]
        picked = jnp.where(valid, index_ref[r : r + 1, :], -1)
        match = (row_c == picked).astype(F32).astype(BF)
        used = jnp.where(dot_t(ones, match) > 0.5, 1.0, 0.0)
        position = dot(used.astype(BF), before)
        number = jnp.sum(used[0:1, :]).astype(I32)
        slot_place = dot(position.astype(BF), match)[0:1, :].astype(I32)
        place_ref[r : r + 1, :] = jnp.where(valid, slot_place, -1)
        chosen = jnp.where((used[0:1, :] > 0.5) & (position[0:1, :] == place_c), 1.0, 0.0).astype(BF)
        mine = cands_ref[r]
        rows = dot(chosen, mine).astype(BF)
        pack_ref[pl.ds(pl.multiple_of(start, 16), slots), :] = dot(rows, wq_ref[...]).astype(BF)
        start_ref[r] = start
        start_ref[8 + r] = number
        start = start + (((number + 15) >> 4) << 4)
        pack_ref[PRE_Q : PRE_Q + features, r * slots : (r + 1) * slots] = lax.dot_general(
            pre_wq_ref[...], mine, (((0,), (1,)), ((), ())), preferred_element_type=F32
        ).astype(BF)
    start_ref[requests] = start
    for copy in copies[3:]:
        copy.wait()


def attend(
    up_copy,
    start_ref,
    chunk_refs,
    pack_hbm,
    small_ref,
    pre_out,
    pack_ref,
    sems,
    keys_ref,
    values_ref,
    normed_ref,
):
    requests, slots = pre_out.shape
    rows = [(PRE_Q, PACK - PRE_Q), (0, requests * slots)]
    copies = [
        pltpu.make_async_copy(pack_hbm.at[pl.ds(*at)], pack_ref.at[pl.ds(*at)], sems.at[i]) for i, at in enumerate(rows)
    ]
    for copy in copies:
        copy.start()
    up_copy.start()
    events, width = keys_ref.shape
    head = width // HEADS
    features = chunk_refs[0].shape[-1]
    pre_wk = (pl.ds(PRE_WKV, features), pl.ds(0, features))
    pre_wv = (pl.ds(PRE_WKV, features), pl.ds(features, features))
    scale = LOG2E / math.sqrt(head)
    for h in range(HEADS):
        values_ref[:, (2 * h + 1) * head : (2 * h + 2) * head] = jnp.ones((events, head), BF)
    copies[0].wait()

    def request(r, carry):
        parts = [ref[:, pl.ds(r, 1)].reshape(events // 4, features) for ref in chunk_refs]
        history = jnp.concatenate(parts, axis=0)
        pre_q = pack_ref[PRE_Q : PRE_Q + features, pl.ds(pl.multiple_of(r * slots, slots), slots)]
        pre_keys = dot(history, pack_ref[pre_wk]).astype(BF)
        pre_values = lax.dot_general(
            pack_ref[pre_wv], history, (((0,), (1,)), ((), ())), preferred_element_type=F32
        ).astype(BF)
        logits = dot(pre_keys, pre_q)
        top = jnp.max(logits, axis=0, keepdims=True)
        weights = jnp.exp2((logits - top) * (LOG2E / math.sqrt(features)))
        weights = (weights * (1.0 / jnp.sum(weights, axis=0, keepdims=True))).astype(BF)
        pooled = dot(pre_values, weights)
        query = pre_q.astype(F32)
        length = jnp.sqrt(jnp.sum(query * query, axis=0, keepdims=True))
        pre_out[pl.ds(r, 1), :] = jnp.sum(pooled * query, axis=0, keepdims=True) / (1.0 + length)
        for c in range(2):
            cols = slice(c * width // 2, (c + 1) * width // 2)
            keys_ref[:, cols] = dot(history, pack_ref[RANK_WK:RANK_WV, cols]).astype(BF)
        for c in range(2):
            cols = slice(c * width // 2, (c + 1) * width // 2)
            part = dot(history, pack_ref[RANK_WV:PACK, cols]).astype(BF)
            for k in range(HEADS // 2):
                h = c * HEADS // 2 + k
                values_ref[:, 2 * h * head : (2 * h + 1) * head] = part[:, k * head : (k + 1) * head]

        pl.when(r == 0)(copies[1].wait)

        def tile(rows):
            at = pl.ds(pl.multiple_of(start_ref[r], 16), rows)
            mixed = []
            for h in range(HEADS):
                cols = slice(h * head, (h + 1) * head)
                query = pack_ref[at, cols]
                logits = dot_t(query, keys_ref[:, cols])
                top = jnp.max(logits, axis=1, keepdims=True)
                weights = jnp.exp2((logits - top) * scale).astype(BF)
                both = dot(weights, values_ref[:, 2 * h * head : (2 * h + 2) * head])
                mixed.append(query.astype(F32) + both[:, :head] / both[:, head:])
            acc = mixed[0]
            for one in mixed[1:]:
                acc = acc + one
            center = jnp.sum(acc, axis=1, keepdims=True) * (1.0 / width)
            acc = jnp.zeros((rows, head), F32)
            for one in mixed:
                acc = acc + (one - center) * (one - center)
            spread = jnp.sum(acc, axis=1, keepdims=True) * (1.0 / width)
            inverse = lax.rsqrt(spread + 1e-05)
            for h in range(HEADS):
                cols = slice(h * head, (h + 1) * head)
                normed_ref[at, cols] = ((mixed[h] - center) * inverse * small_ref[h : h + 1, :]).astype(BF)

        number = start_ref[8 + r]
        low = 0
        for rows in ROW_TILES:
            pl.when((number > low) & (number <= rows))(functools.partial(tile, rows))
            low = rows
        return carry

    lax.fori_loop(0, requests, request, 0)


def rank_kernel(
    start_ref, own_ref, a_ref, b_ref, c_ref, pack_hbm, place_ref, small_ref, up_hbm,
    pre_out, rank_out,
    keys_ref, values_ref, pack_ref, sems, normed_ref, ranked_ref, up_ref, sem,
):
    up_copy = pltpu.make_async_copy(up_hbm, up_ref, sem)
    requests, slots = place_ref.shape
    attend(
        up_copy, start_ref, (own_ref, a_ref, b_ref, c_ref), pack_hbm, small_ref,
        pre_out, pack_ref, sems, keys_ref, values_ref, normed_ref,
    )
    up_copy.wait()
    total = start_ref[requests]
    hidden_size = up_ref.shape[1]

    def mlp(t, carry):
        at = pl.ds(pl.multiple_of(t * MLP_ROWS, MLP_ROWS), MLP_ROWS)
        rows = normed_ref[at, :]
        acc = jnp.zeros((MLP_ROWS, 128), F32)
        for j in range(hidden_size // MLP_COLS):
            cols = slice(j * MLP_COLS, (j + 1) * MLP_COLS)
            x = dot(rows, up_ref[:, cols])
            half = 0.5 * x
            x = half + half * jnp.tanh(x * (GELU_A + GELU_B * (x * x)))
            x = x.astype(BF).astype(F32)
            for k in range(MLP_COLS // 128):
                at_w = HEADS + j * (MLP_COLS // 128) + k
                acc = acc + x[:, k * 128 : (k + 1) * 128] * small_ref[at_w : at_w + 1, :]
        ranked_ref[at, :] = jnp.broadcast_to(jnp.sum(acc, axis=1, keepdims=True), acc.shape)
        return carry

    lax.fori_loop(0, (total + MLP_ROWS - 1) // MLP_ROWS, mlp, 0)
    row = lax.broadcasted_iota(I32, (slots, slots), 0)
    for r in range(requests):
        ranked = ranked_ref[pl.ds(pl.multiple_of(start_ref[r], 16), slots), :]
        ranked = jnp.concatenate([ranked] * (slots // 128), axis=1)
        hit = row == place_ref[r : r + 1, :]
        rank_out[r : r + 1, :] = jnp.sum(jnp.where(hit, ranked, 0.0), axis=0, keepdims=True)


def select_call(surv_count, surv_index, cands, rank_wq, pre_wq, pre_wkv, rank_wkv, norm_gain, score_w):
    requests, slots = surv_index.shape
    width = rank_wq.shape[1]
    return pl.pallas_call(
        select_kernel,
        name="select",
        out_shape=(
            jax.ShapeDtypeStruct((PACK, width), BF),
            jax.ShapeDtypeStruct((requests, slots), I32),
            jax.ShapeDtypeStruct((16,), I32),
            jax.ShapeDtypeStruct((HEADS + score_w.shape[0] // 128, 128), F32),
        ),
        in_specs=[SMEM, VMEM, HBM, HBM, HBM, HBM, HBM, VMEM, VMEM],
        out_specs=(VMEM, VMEM, SMEM, VMEM),
        scratch_shapes=[
            pltpu.VMEM(cands.shape, BF),
            pltpu.VMEM(rank_wq.shape, BF),
            pltpu.VMEM(pre_wq.shape, BF),
            pltpu.SemaphoreType.DMA((6,)),
        ],
        compiler_params=pltpu.CompilerParams(vmem_limit_bytes=SELECT_LIMIT),
        cost_estimate=pl.CostEstimate(flops=2 * 10**9, bytes_accessed=12 * 2**20, transcendentals=0),
    )(
        surv_count.reshape(requests), surv_index, cands, rank_wq, pre_wq, pre_wkv, rank_wkv,
        norm_gain.reshape(HEADS, 128), score_w.reshape(-1, 128),
    )


def rank_call(start, chunks, pack, place, small, mlp_up):
    requests, slots = place.shape
    width = pack.shape[1]
    events = 4 * chunks[0].shape[0] * chunks[0].shape[2]
    return pl.pallas_call(
        rank_kernel,
        name="rank",
        out_shape=(
            jax.ShapeDtypeStruct((requests, slots), F32),
            jax.ShapeDtypeStruct((requests, slots), F32),
        ),
        in_specs=[SMEM] + [VMEM] * 4 + [HBM, VMEM, VMEM, HBM],
        out_specs=(VMEM, VMEM),
        scratch_shapes=[
            pltpu.VMEM((events, width), BF),
            pltpu.VMEM((events, 2 * width), BF),
            pltpu.VMEM(pack.shape, BF),
            pltpu.SemaphoreType.DMA((2,)),
            pltpu.VMEM((requests * slots, width), BF),
            pltpu.VMEM((requests * slots, 128), F32),
            pltpu.VMEM(mlp_up.shape, BF),
            pltpu.SemaphoreType.DMA,
        ],
        compiler_params=pltpu.CompilerParams(vmem_limit_bytes=RANK_LIMIT),
        cost_estimate=pl.CostEstimate(flops=16 * 10**9, bytes_accessed=16 * 2**20, transcendentals=8 * 10**6),
    )(start, *chunks, pack, place, small, mlp_up)


def body(history, cands, surv_count, surv_index, pre_wq, pre_wkv, rank_wq, rank_wkv, norm_gain, mlp_up, score_w):
    nx = 4
    nz = lax.axis_size("cand") // nx
    columns = [[z * nx + x for z in range(nz)] for x in range(nx)]

    def shift(x, by):
        pairs = [(z * nx + a, z * nx + (a + by) % nx) for z in range(nz) for a in range(nx)]
        return lax.ppermute(x, "cand", pairs)

    copies = jnp.broadcast_to(history[None], (nz,) + history.shape)
    own = lax.all_to_all(copies, "cand", split_axis=0, concat_axis=0, tiled=True, axis_index_groups=columns)
    pack, place, start, small = select_call(
        surv_count, surv_index, cands, rank_wq, pre_wq, pre_wkv, rank_wkv, norm_gain, score_w
    )
    chunks = [own] + [shift(own, by) for by in (1, 3, 2)]
    return rank_call(start, chunks, pack, place, small, mlp_up)


def solution(mesh):
    in_specs = (
        P("grp", "cand", None),
        P("grp", "cand", None),
        P("grp", "cand"),
        P("grp", "cand"),
        P(),
        P(),
        P(),
        P(),
        P(),
        P(),
        P(),
    )
    out_specs = (P("grp", "cand"), P("grp", "cand"))
    return jax.shard_map(body, mesh=mesh, in_specs=in_specs, out_specs=out_specs, check_vma=False)
```

```python
import functools
import math

import jax
import jax.numpy as jnp
from jax import lax
from jax.experimental import pallas as pl
from jax.experimental.pallas import tpu as pltpu
from jax.sharding import PartitionSpec as P

HEADS = 8
BF = jnp.bfloat16
F32 = jnp.float32
I32 = jnp.int32
LOG2E = 1.4426950408889634
GELU_A = math.sqrt(2.0 / math.pi)
GELU_B = GELU_A * 0.044715
ROW_TILES = (128, 176, 256)
MLP_ROWS = 160
MLP_COLS = 512
PRE_Q = 1024
PRE_WKV = 1280
RANK_WK = 1536
RANK_WV = 1792
SMALL = 2048
PACK = 2064
SELECT_LIMIT = 57 * 2**20
RANK_LIMIT = 50 * 2**20
VMEM = pl.BlockSpec(memory_space=pltpu.VMEM)
SMEM = pl.BlockSpec(memory_space=pltpu.SMEM)
HBM = pl.BlockSpec(memory_space=pltpu.HBM)


def dot(a, b):
    return jnp.dot(a, b, preferred_element_type=F32)


def dot_t(a, b):
    return lax.dot_general(a, b, (((1,), (1,)), ((), ())), preferred_element_type=F32)


def select_kernel(
    count_ref,
    index_ref,
    cands_hbm,
    wq_hbm,
    pre_wq_hbm,
    pre_wkv_hbm,
    wkv_hbm,
    gain_ref,
    score_w_ref,
    pack_ref,
    cands_ref,
    wq_ref,
    pre_wq_ref,
    sems,
):
    width = pack_ref.shape[1]
    pairs = (
        (cands_hbm, cands_ref),
        (wq_hbm, wq_ref),
        (pre_wq_hbm, pre_wq_ref),
        (pre_wkv_hbm, pack_ref.at[pl.ds(PRE_WKV, pre_wkv_hbm.shape[0]), pl.ds(0, pre_wkv_hbm.shape[1])]),
        (wkv_hbm.at[:, pl.ds(0, width)], pack_ref.at[pl.ds(RANK_WK, RANK_WV - RANK_WK)]),
        (wkv_hbm.at[:, pl.ds(width, width)], pack_ref.at[pl.ds(RANK_WV, SMALL - RANK_WV)]),
    )
    copies = [pltpu.make_async_copy(a, b, sems.at[i]) for i, (a, b) in enumerate(pairs)]
    for copy in copies:
        copy.start()
    requests, slots = index_ref.shape
    _, cands, features = cands_ref.shape
    row_c = lax.broadcasted_iota(I32, (cands, slots), 0)
    lane = lax.broadcasted_iota(I32, (1, slots), 1)
    before = (
        lax.broadcasted_iota(I32, (cands, cands), 0) < lax.broadcasted_iota(I32, (cands, cands), 1)
    ).astype(BF)
    place_c = lax.broadcasted_iota(I32, (slots, cands), 0).astype(F32)
    ones = jnp.ones((8, slots), BF)
    for copy in copies[:3]:
        copy.wait()
    start = jnp.int32(0)
    places = []
    for r in range(requests):
        valid = lane < count_ref[r]
        picked = jnp.where(valid, index_ref[r : r + 1, :], -1)
        match = (row_c == picked).astype(F32).astype(BF)
        used = jnp.where(dot_t(ones, match) > 0.5, 1.0, 0.0)
        position = dot(used.astype(BF), before)
        number = jnp.sum(used[0:1, :]).astype(I32)
        places.append(jnp.where(valid, dot(position.astype(BF), match)[0:1, :], -1.0))
        chosen = jnp.where((used[0:1, :] > 0.5) & (position[0:1, :] == place_c), 1.0, 0.0).astype(BF)
        mine = cands_ref[r]
        rows = dot(chosen, mine).astype(BF)
        pack_ref[pl.ds(pl.multiple_of(start, 16), slots), :] = dot(rows, wq_ref[...]).astype(BF)
        start = start + (((number + 15) >> 4) << 4)
        pack_ref[PRE_Q : PRE_Q + features, r * slots : (r + 1) * slots] = lax.dot_general(
            pre_wq_ref[...], mine, (((0,), (1,)), ((), ())), preferred_element_type=F32
        ).astype(BF)
    gain = gain_ref[...]
    high = gain.astype(BF).astype(F32)
    middle = (gain - high).astype(BF).astype(F32)
    per_row = width // 128
    small = [jnp.concatenate(places, axis=1), high, middle, gain - high - middle]
    for k in range(score_w_ref.shape[0] // per_row):
        lanes = [score_w_ref[i : i + 1, :].astype(F32) for i in range(k * per_row, (k + 1) * per_row)]
        small.append(jnp.concatenate(lanes, axis=1))
    small.append(jnp.zeros((PACK - SMALL - len(small), width), F32))
    pack_ref[SMALL:PACK, :] = jnp.concatenate(small, axis=0).astype(BF)
    for copy in copies[3:]:
        copy.wait()


def attend(
    chunk_refs,
    pack_hbm,
    pack_ref,
    pack_sems,
    keys_ref,
    values_ref,
    normed_ref,
    state_ref,
    state_hbm,
    state_sems,
    pre_out,
    extra=None,
):
    last = normed_ref is not None
    requests, _, _ = state_ref.shape
    events, width = keys_ref.shape
    head = width // HEADS
    features = chunk_refs[0].shape[-1]
    slots = width // requests
    rows = [(PRE_Q, PACK - PRE_Q), (0, PRE_Q)]
    copies = [
        pltpu.make_async_copy(pack_hbm.at[pl.ds(*at)], pack_ref.at[pl.ds(*at)], pack_sems.at[i])
        for i, at in enumerate(rows)
    ]
    for copy in copies:
        copy.start()
    if last:
        for r in range(requests):
            pltpu.make_async_copy(state_hbm.at[r], state_ref.at[r], state_sems.at[r]).start()
        extra.start()
    for h in range(HEADS):
        values_ref[:, (2 * h + 1) * head : (2 * h + 2) * head] = jnp.ones((events, head), BF)
    scale = LOG2E / math.sqrt(head)
    pre_scale = LOG2E / math.sqrt(features)
    copies[0].wait()
    small = pack_ref[SMALL:PACK, :].astype(F32)
    gain = small[1:2, :] + small[2:3, :] + small[3:4, :]
    numbers = [jnp.max(small[0:1, r * slots : (r + 1) * slots]).astype(I32) + 1 for r in range(requests)]
    starts = [jnp.int32(0)]
    for number in numbers:
        starts.append(starts[-1] + (((number + 15) >> 4) << 4))

    def request(r, carry):
        number, start = numbers[0], starts[0]
        for k in range(1, requests):
            number, start = jnp.where(r == k, numbers[k], number), jnp.where(r == k, starts[k], start)
        parts = [ref[:, pl.ds(r, 1)].reshape(events // len(chunk_refs), features) for ref in chunk_refs]
        history = jnp.concatenate(parts, axis=0)
        pre_q = pack_ref[PRE_Q : PRE_Q + features, pl.ds(pl.multiple_of(r * slots, slots), slots)]
        pre_keys = dot(history, pack_ref[PRE_WKV : PRE_WKV + features, :features]).astype(BF)
        pre_values = lax.dot_general(
            pack_ref[PRE_WKV : PRE_WKV + features, features : 2 * features],
            history,
            (((0,), (1,)), ((), ())),
            preferred_element_type=F32,
        ).astype(BF)
        logits = dot(pre_keys, pre_q)
        top = jnp.max(logits, axis=0, keepdims=True)
        weights = jnp.exp2((logits - top) * pre_scale).astype(BF)
        mass = jnp.sum(weights.astype(F32), axis=0, keepdims=True)
        query = pre_q.astype(F32)
        score = jnp.sum(dot(pre_values, weights) * query, axis=0, keepdims=True)
        for c in range(2):
            cols = slice(c * width // 2, (c + 1) * width // 2)
            keys_ref[:, cols] = dot(history, pack_ref[RANK_WK:RANK_WV, cols]).astype(BF)
        for c in range(2):
            cols = slice(c * width // 2, (c + 1) * width // 2)
            part = dot(history, pack_ref[RANK_WV:SMALL, cols]).astype(BF)
            for k in range(HEADS // 2):
                h = c * HEADS // 2 + k
                values_ref[:, 2 * h * head : (2 * h + 1) * head] = part[:, k * head : (k + 1) * head]
        pl.when(r == 0)(copies[1].wait)
        if last:
            pltpu.make_async_copy(state_hbm.at[r], state_ref.at[r], state_sems.at[r]).wait()
            other_top = state_ref[r, slots : slots + 1, :slots]
            peak = jnp.maximum(top, other_top)
            mine, other = jnp.exp2((top - peak) * pre_scale), jnp.exp2((other_top - peak) * pre_scale)
            score = score * mine + state_ref[r, slots + 2 : slots + 3, :slots] * other
            mass = mass * mine + state_ref[r, slots + 1 : slots + 2, :slots] * other
            length = jnp.sqrt(jnp.sum(query * query, axis=0, keepdims=True))
            pre_out[pl.ds(r, 1), :] = score / mass / (1.0 + length)
        else:
            state_ref[r, slots : slots + 1, :slots] = top
            state_ref[r, slots + 1 : slots + 2, :slots] = mass
            state_ref[r, slots + 2 : slots + 3, :slots] = score

        def tile(rows):
            at = pl.ds(pl.multiple_of(start, 16), rows)
            mixed = []
            stat = jnp.zeros((rows, 128), F32)
            lane = lax.broadcasted_iota(I32, (rows, 128), 1)
            for h in range(HEADS):
                cols = slice(h * head, (h + 1) * head)
                query = pack_ref[at, cols]
                logits = dot_t(query, keys_ref[:, cols])
                top = jnp.max(logits, axis=1, keepdims=True)
                weights = jnp.exp2((logits - top) * scale).astype(BF)
                both = dot(weights, values_ref[:, 2 * h * head : (2 * h + 2) * head])
                mass = both[:, head:]
                out = both[:, :head] / mass
                mass = top * scale + jnp.log2(mass)
                if last:
                    share = 1.0 / (1.0 + jnp.exp2(state_ref[r, :rows, width + h : width + h + 1] - mass))
                    other = state_ref[r, :rows, cols]
                    mixed.append(query.astype(F32) + other + share * (out - other))
                else:
                    state_ref[r, :rows, cols] = out
                    stat = jnp.where(lane == h, mass, stat)
            if not last:
                state_ref[r, :rows, width : width + 128] = stat
                return
            acc = mixed[0]
            for one in mixed[1:]:
                acc = acc + one
            center = jnp.sum(acc, axis=1, keepdims=True) * (1.0 / width)
            acc = jnp.zeros((rows, head), F32)
            for one in mixed:
                acc = acc + (one - center) * (one - center)
            spread = jnp.sum(acc, axis=1, keepdims=True) * (1.0 / width)
            inverse = lax.rsqrt(spread + 1e-05)
            for h in range(HEADS):
                cols = slice(h * head, (h + 1) * head)
                normed_ref[at, cols] = ((mixed[h] - center) * inverse * gain[:, cols]).astype(BF)

        low = 0
        for rows in ROW_TILES:
            pl.when((number > low) & (number <= rows))(functools.partial(tile, rows))
            low = rows
        if not last:
            pltpu.make_async_copy(state_ref.at[r], state_hbm.at[r], state_sems.at[r]).start()
        return carry

    lax.fori_loop(0, requests, request, 0)
    if not last:
        for r in range(requests):
            pltpu.make_async_copy(state_ref.at[r], state_hbm.at[r], state_sems.at[r]).wait()
    return starts, small


def first_kernel(
    own_ref, near_ref, pack_hbm,
    state_hbm,
    keys_ref, values_ref, pack_ref, pack_sems, state_ref, state_sems,
):
    attend(
        (own_ref, near_ref), pack_hbm, pack_ref, pack_sems, keys_ref, values_ref, None, state_ref, state_hbm, state_sems, None
    )


def last_kernel(
    a_ref, b_ref, pack_hbm, state_hbm, up_hbm,
    pre_out, rank_out,
    keys_ref, values_ref, pack_ref, pack_sems, state_ref, state_sems, normed_ref, ranked_ref, up_ref, sem,
):
    up_copy = pltpu.make_async_copy(up_hbm, up_ref, sem)
    requests, slots = rank_out.shape
    starts, small = attend(
        (a_ref, b_ref), pack_hbm, pack_ref, pack_sems, keys_ref, values_ref, normed_ref, state_ref, state_hbm, state_sems,
        pre_out, up_copy,
    )
    up_copy.wait()
    width, hidden_size = up_ref.shape

    def mlp(t, carry):
        at = pl.ds(pl.multiple_of(t * MLP_ROWS, 16), MLP_ROWS)
        rows = normed_ref[at, :]
        acc = jnp.zeros((MLP_ROWS, 128), F32)
        for j in range(hidden_size // MLP_COLS):
            cols = slice(j * MLP_COLS, (j + 1) * MLP_COLS)
            x = dot(rows, up_ref[:, cols])
            x = x + x * jnp.tanh(x * (GELU_A + GELU_B * (x * x)))
            for k in range(MLP_COLS // 128):
                row, lane = divmod(j * MLP_COLS + k * 128, width)
                weight = 0.5 * small[4 + row : 5 + row, lane : lane + 128]
                acc = acc + x[:, k * 128 : (k + 1) * 128] * weight
        ranked_ref[at, :] = jnp.broadcast_to(jnp.sum(acc, axis=1, keepdims=True), acc.shape)
        return carry

    lax.fori_loop(0, (starts[requests] + MLP_ROWS - 1) // MLP_ROWS, mlp, 0)
    row = lax.broadcasted_iota(I32, (slots, slots), 0).astype(F32)
    for r in range(requests):
        ranked = ranked_ref[pl.ds(pl.multiple_of(starts[r], 16), slots), :]
        ranked = jnp.concatenate([ranked] * (slots // 128), axis=1)
        hit = row == small[0:1, r * slots : (r + 1) * slots]
        rank_out[r : r + 1, :] = jnp.sum(jnp.where(hit, ranked, 0.0), axis=0, keepdims=True)


def select_call(surv_count, surv_index, cands, rank_wq, pre_wq, pre_wkv, rank_wkv, norm_gain, score_w):
    requests, slots = surv_index.shape
    width = rank_wq.shape[1]
    return pl.pallas_call(
        select_kernel,
        name="select",
        out_shape=jax.ShapeDtypeStruct((PACK, width), BF),
        in_specs=[SMEM, VMEM, HBM, HBM, HBM, HBM, HBM, VMEM, VMEM],
        out_specs=VMEM,
        scratch_shapes=[
            pltpu.VMEM(cands.shape, BF),
            pltpu.VMEM(rank_wq.shape, BF),
            pltpu.VMEM(pre_wq.shape, BF),
            pltpu.SemaphoreType.DMA((6,)),
        ],
        compiler_params=pltpu.CompilerParams(vmem_limit_bytes=SELECT_LIMIT),
        cost_estimate=pl.CostEstimate(flops=2 * 10**9, bytes_accessed=12 * 2**20, transcendentals=0),
    )(
        surv_count.reshape(requests), surv_index, cands, rank_wq, pre_wq, pre_wkv, rank_wkv,
        norm_gain.reshape(1, -1), score_w.reshape(-1, 128),
    )


def rank_call(chunks, pack, mlp_up):
    nz, requests, here, _ = chunks[0].shape
    width = pack.shape[1]
    slots = width // requests
    events = 2 * nz * here
    padded = -(-requests * slots // MLP_ROWS) * MLP_ROWS
    state = jax.ShapeDtypeStruct((requests, slots + 8, width + 128), F32)
    attention = [
        pltpu.VMEM((events, width), BF),
        pltpu.VMEM((events, 2 * width), BF),
        pltpu.VMEM(pack.shape, BF),
        pltpu.SemaphoreType.DMA((2,)),
        pltpu.VMEM(state.shape, F32),
        pltpu.SemaphoreType.DMA((requests,)),
    ]
    state = pl.pallas_call(
        first_kernel,
        name="rank_first",
        out_shape=state,
        in_specs=[VMEM, VMEM, HBM],
        out_specs=HBM,
        scratch_shapes=attention,
        compiler_params=pltpu.CompilerParams(vmem_limit_bytes=RANK_LIMIT),
        cost_estimate=pl.CostEstimate(flops=6 * 10**9, bytes_accessed=10 * 2**20, transcendentals=2 * 10**6),
    )(*chunks[:2], pack)
    score = jax.ShapeDtypeStruct((requests, slots), F32)
    return pl.pallas_call(
        last_kernel,
        name="rank_last",
        out_shape=(score, score),
        in_specs=[VMEM, VMEM, HBM, HBM, HBM],
        out_specs=(VMEM, VMEM),
        scratch_shapes=attention
        + [
            pltpu.VMEM((padded, width), BF),
            pltpu.VMEM((padded, 128), F32),
            pltpu.VMEM(mlp_up.shape, BF),
            pltpu.SemaphoreType.DMA,
        ],
        compiler_params=pltpu.CompilerParams(vmem_limit_bytes=RANK_LIMIT),
        cost_estimate=pl.CostEstimate(flops=16 * 10**9, bytes_accessed=20 * 2**20, transcendentals=4 * 10**6),
    )(*chunks[2:], pack, state, mlp_up)


def body(history, cands, surv_count, surv_index, pre_wq, pre_wkv, rank_wq, rank_wkv, norm_gain, mlp_up, score_w):
    nx = 4
    nz = lax.axis_size("cand") // nx
    columns = [[z * nx + x for z in range(nz)] for x in range(nx)]

    def shift(x, by):
        pairs = [(z * nx + a, z * nx + (a + by) % nx) for z in range(nz) for a in range(nx)]
        return lax.ppermute(x, "cand", pairs)

    copies = jnp.broadcast_to(history[None], (nz,) + history.shape)
    own = lax.all_to_all(copies, "cand", split_axis=0, concat_axis=0, tiled=True, axis_index_groups=columns)
    pack = select_call(
        surv_count, surv_index, cands, rank_wq, pre_wq, pre_wkv, rank_wkv, norm_gain, score_w
    )
    chunks = [own] + [shift(own, by) for by in (1, 3, 2)]
    return rank_call(chunks, pack, mlp_up)


def solution(mesh):
    in_specs = (
        P("grp", "cand", None),
        P("grp", "cand", None),
        P("grp", "cand"),
        P("grp", "cand"),
        P(),
        P(),
        P(),
        P(),
        P(),
        P(),
        P(),
    )
    out_specs = (P("grp", "cand"), P("grp", "cand"))
    return jax.shard_map(body, mesh=mesh, in_specs=in_specs, out_specs=out_specs, check_vma=False)
```

```python
import functools
import math

import jax
import jax.numpy as jnp
from jax import lax
from jax.experimental import pallas as pl
from jax.experimental.pallas import tpu as pltpu
from jax.sharding import PartitionSpec as P

HEADS = 8
BF = jnp.bfloat16
F32 = jnp.float32
I32 = jnp.int32
LOG2E = 1.4426950408889634
GELU_A = math.sqrt(2.0 / math.pi)
GELU_B = GELU_A * 0.044715
ROW_TILES = (128, 176, 256)
MLP_ROWS = 160
MLP_COLS = 512
PRE_Q = 1024
PRE_WKV = 1280
RANK_WK = 1536
RANK_WV = 1792
SMALL = 2048
PACK = 2064
SELECT_LIMIT = 57 * 2**20
RANK_LIMIT = 50 * 2**20
VMEM = pl.BlockSpec(memory_space=pltpu.VMEM)
SMEM = pl.BlockSpec(memory_space=pltpu.SMEM)
HBM = pl.BlockSpec(memory_space=pltpu.HBM)
ANY = pl.BlockSpec(memory_space=pl.ANY)


def dot(a, b):
    return jnp.dot(a, b, preferred_element_type=F32)


def dot_t(a, b):
    return lax.dot_general(a, b, (((1,), (1,)), ((), ())), preferred_element_type=F32)


def select_kernel(
    count_ref,
    index_ref,
    cands_hbm,
    wq_hbm,
    pre_wq_hbm,
    pre_wkv_hbm,
    wkv_hbm,
    gain_ref,
    score_w_ref,
    pack_hbm,
    pack_ref,
    cands_ref,
    wq_ref,
    pre_wq_ref,
    sems,
    out_sems,
):
    width = pack_hbm.shape[1]
    pairs = (
        (cands_hbm, cands_ref),
        (wq_hbm, wq_ref),
        (pre_wq_hbm, pre_wq_ref),
        (pre_wkv_hbm, pack_hbm.at[pl.ds(PRE_WKV, pre_wkv_hbm.shape[0]), pl.ds(0, pre_wkv_hbm.shape[1])]),
        (wkv_hbm.at[:, pl.ds(0, width)], pack_hbm.at[pl.ds(RANK_WK, RANK_WV - RANK_WK)]),
        (wkv_hbm.at[:, pl.ds(width, width)], pack_hbm.at[pl.ds(RANK_WV, SMALL - RANK_WV)]),
    )
    copies = [pltpu.make_async_copy(a, b, sems.at[i]) for i, (a, b) in enumerate(pairs)]
    for copy in copies:
        copy.start()
    requests, slots = index_ref.shape
    _, cands, features = cands_ref.shape
    row_c = lax.broadcasted_iota(I32, (cands, slots), 0)
    lane = lax.broadcasted_iota(I32, (1, slots), 1)
    before = (
        lax.broadcasted_iota(I32, (cands, cands), 0) < lax.broadcasted_iota(I32, (cands, cands), 1)
    ).astype(BF)
    place_c = lax.broadcasted_iota(I32, (slots, cands), 0).astype(F32)
    ones = jnp.ones((8, slots), BF)
    for copy in copies[:3]:
        copy.wait()
    start = jnp.int32(0)
    places = []
    for r in range(requests):
        valid = lane < count_ref[r]
        picked = jnp.where(valid, index_ref[r : r + 1, :], -1)
        match = (row_c == picked).astype(F32).astype(BF)
        used = jnp.where(dot_t(ones, match) > 0.5, 1.0, 0.0)
        position = dot(used.astype(BF), before)
        number = jnp.sum(used[0:1, :]).astype(I32)
        places.append(jnp.where(valid, dot(position.astype(BF), match)[0:1, :], -1.0))
        chosen = jnp.where((used[0:1, :] > 0.5) & (position[0:1, :] == place_c), 1.0, 0.0).astype(BF)
        mine = cands_ref[r]
        rows = dot(chosen, mine).astype(BF)
        pack_ref[pl.ds(pl.multiple_of(start, 16), slots), :] = dot(rows, wq_ref[...]).astype(BF)
        start = start + (((number + 15) >> 4) << 4)
        pack_ref[PRE_Q : PRE_Q + features, r * slots : (r + 1) * slots] = lax.dot_general(
            pre_wq_ref[...], mine, (((0,), (1,)), ((), ())), preferred_element_type=F32
        ).astype(BF)
    gain = gain_ref[...]
    high = gain.astype(BF).astype(F32)
    middle = (gain - high).astype(BF).astype(F32)
    per_row = width // 128
    small = [jnp.concatenate(places, axis=1), high, middle, gain - high - middle]
    for k in range(score_w_ref.shape[0] // per_row):
        lanes = [score_w_ref[i : i + 1, :].astype(F32) for i in range(k * per_row, (k + 1) * per_row)]
        small.append(jnp.concatenate(lanes, axis=1))
    small.append(jnp.zeros((PACK - SMALL - len(small), width), F32))
    pack_ref[SMALL:PACK, :] = jnp.concatenate(small, axis=0).astype(BF)
    writes = [(PRE_Q, features), (SMALL, PACK - SMALL), (0, PRE_Q)]
    for i, at in enumerate(writes):
        copies.append(pltpu.make_async_copy(pack_ref.at[pl.ds(*at)], pack_hbm.at[pl.ds(*at)], out_sems.at[i]))
        copies[-1].start()
    for copy in copies[3:]:
        copy.wait()


def attend(
    chunk_refs,
    pack_hbm,
    pack_ref,
    pack_sems,
    keys_ref,
    values_ref,
    normed_ref,
    state_ref,
    state_hbm,
    state_sems,
    pre_out,
    extra=None,
):
    last = normed_ref is not None
    requests, _, _ = state_ref.shape
    events, width = keys_ref.shape
    head = width // HEADS
    features = chunk_refs[0].shape[-1]
    slots = width // requests
    rows = [(PRE_Q, PACK - PRE_Q), (0, PRE_Q)]
    copies = [
        pltpu.make_async_copy(pack_hbm.at[pl.ds(*at)], pack_ref.at[pl.ds(*at)], pack_sems.at[i])
        for i, at in enumerate(rows)
    ]
    for copy in copies:
        copy.start()
    if last:
        for r in range(requests):
            pltpu.make_async_copy(state_hbm.at[r], state_ref.at[r], state_sems.at[r]).start()
        extra.start()
    for h in range(HEADS):
        values_ref[:, (2 * h + 1) * head : (2 * h + 2) * head] = jnp.ones((events, head), BF)
    scale = LOG2E / math.sqrt(head)
    pre_scale = LOG2E / math.sqrt(features)
    copies[0].wait()
    small = pack_ref[SMALL:PACK, :].astype(F32)
    gain = small[1:2, :] + small[2:3, :] + small[3:4, :]
    numbers = [jnp.max(small[0:1, r * slots : (r + 1) * slots]).astype(I32) + 1 for r in range(requests)]
    starts = [jnp.int32(0)]
    for number in numbers:
        starts.append(starts[-1] + (((number + 15) >> 4) << 4))

    def request(r, carry):
        number, start = numbers[0], starts[0]
        for k in range(1, requests):
            number, start = jnp.where(r == k, numbers[k], number), jnp.where(r == k, starts[k], start)
        parts = [ref[:, pl.ds(r, 1)].reshape(events // len(chunk_refs), features) for ref in chunk_refs]
        history = jnp.concatenate(parts, axis=0)
        pre_q = pack_ref[PRE_Q : PRE_Q + features, pl.ds(pl.multiple_of(r * slots, slots), slots)]
        pre_keys = dot(history, pack_ref[PRE_WKV : PRE_WKV + features, :features]).astype(BF)
        pre_values = lax.dot_general(
            pack_ref[PRE_WKV : PRE_WKV + features, features : 2 * features],
            history,
            (((0,), (1,)), ((), ())),
            preferred_element_type=F32,
        ).astype(BF)
        logits = dot(pre_keys, pre_q)
        top = jnp.max(logits, axis=0, keepdims=True)
        weights = jnp.exp2((logits - top) * pre_scale).astype(BF)
        mass = jnp.sum(weights.astype(F32), axis=0, keepdims=True)
        query = pre_q.astype(F32)
        score = jnp.sum(dot(pre_values, weights) * query, axis=0, keepdims=True)
        for c in range(2):
            cols = slice(c * width // 2, (c + 1) * width // 2)
            keys_ref[:, cols] = dot(history, pack_ref[RANK_WK:RANK_WV, cols]).astype(BF)
        for c in range(2):
            cols = slice(c * width // 2, (c + 1) * width // 2)
            part = dot(history, pack_ref[RANK_WV:SMALL, cols]).astype(BF)
            for k in range(HEADS // 2):
                h = c * HEADS // 2 + k
                values_ref[:, 2 * h * head : (2 * h + 1) * head] = part[:, k * head : (k + 1) * head]
        pl.when(r == 0)(copies[1].wait)
        if last:
            pltpu.make_async_copy(state_hbm.at[r], state_ref.at[r], state_sems.at[r]).wait()
            other_top = state_ref[r, slots : slots + 1, :slots]
            peak = jnp.maximum(top, other_top)
            mine, other = jnp.exp2((top - peak) * pre_scale), jnp.exp2((other_top - peak) * pre_scale)
            score = score * mine + state_ref[r, slots + 2 : slots + 3, :slots] * other
            mass = mass * mine + state_ref[r, slots + 1 : slots + 2, :slots] * other
            length = jnp.sqrt(jnp.sum(query * query, axis=0, keepdims=True))
            pre_out[pl.ds(r, 1), :] = score / mass / (1.0 + length)
        else:
            state_ref[r, slots : slots + 1, :slots] = top
            state_ref[r, slots + 1 : slots + 2, :slots] = mass
            state_ref[r, slots + 2 : slots + 3, :slots] = score

        def tile(rows):
            at = pl.ds(pl.multiple_of(start, 16), rows)
            mixed = []
            stat = jnp.zeros((rows, 128), F32)
            lane = lax.broadcasted_iota(I32, (rows, 128), 1)
            for h in range(HEADS):
                cols = slice(h * head, (h + 1) * head)
                query = pack_ref[at, cols]
                logits = dot_t(query, keys_ref[:, cols])
                top = jnp.max(logits, axis=1, keepdims=True)
                weights = jnp.exp2((logits - top) * scale).astype(BF)
                both = dot(weights, values_ref[:, 2 * h * head : (2 * h + 2) * head])
                mass = both[:, head:]
                out = both[:, :head] / mass
                mass = top * scale + jnp.log2(mass)
                if last:
                    share = 1.0 / (1.0 + jnp.exp2(state_ref[r, :rows, width + h : width + h + 1] - mass))
                    other = state_ref[r, :rows, cols]
                    mixed.append(query.astype(F32) + other + share * (out - other))
                else:
                    state_ref[r, :rows, cols] = out
                    stat = jnp.where(lane == h, mass, stat)
            if not last:
                state_ref[r, :rows, width : width + 128] = stat
                return
            acc = mixed[0]
            for one in mixed[1:]:
                acc = acc + one
            center = jnp.sum(acc, axis=1, keepdims=True) * (1.0 / width)
            acc = jnp.zeros((rows, head), F32)
            for one in mixed:
                acc = acc + (one - center) * (one - center)
            spread = jnp.sum(acc, axis=1, keepdims=True) * (1.0 / width)
            inverse = lax.rsqrt(spread + 1e-05)
            for h in range(HEADS):
                cols = slice(h * head, (h + 1) * head)
                normed_ref[at, cols] = ((mixed[h] - center) * inverse * gain[:, cols]).astype(BF)

        low = 0
        for rows in ROW_TILES:
            pl.when((number > low) & (number <= rows))(functools.partial(tile, rows))
            low = rows
        if not last:
            pltpu.make_async_copy(state_ref.at[r], state_hbm.at[r], state_sems.at[r]).start()
        return carry

    lax.fori_loop(0, requests, request, 0)
    if not last:
        for r in range(requests):
            pltpu.make_async_copy(state_ref.at[r], state_hbm.at[r], state_sems.at[r]).wait()
    return starts, small


def first_kernel(
    own_ref, near_ref, pack_hbm,
    state_hbm,
    keys_ref, values_ref, pack_ref, pack_sems, state_ref, state_sems,
):
    attend(
        (own_ref, near_ref), pack_hbm, pack_ref, pack_sems, keys_ref, values_ref, None, state_ref, state_hbm, state_sems, None
    )


def last_kernel(
    a_ref, b_ref, pack_hbm, state_hbm, up_hbm,
    pre_out, rank_out,
    keys_ref, values_ref, pack_ref, pack_sems, state_ref, state_sems, normed_ref, ranked_ref, up_ref, sem,
):
    up_copy = pltpu.make_async_copy(up_hbm, up_ref, sem)
    requests, slots = rank_out.shape
    starts, small = attend(
        (a_ref, b_ref), pack_hbm, pack_ref, pack_sems, keys_ref, values_ref, normed_ref, state_ref, state_hbm, state_sems,
        pre_out, up_copy,
    )
    up_copy.wait()
    width, hidden_size = up_ref.shape

    def mlp(t, carry):
        at = pl.ds(pl.multiple_of(t * MLP_ROWS, 16), MLP_ROWS)
        rows = normed_ref[at, :]
        acc = jnp.zeros((MLP_ROWS, 128), F32)
        for j in range(hidden_size // MLP_COLS):
            cols = slice(j * MLP_COLS, (j + 1) * MLP_COLS)
            x = dot(rows, up_ref[:, cols])
            x = x + x * jnp.tanh(x * (GELU_A + GELU_B * (x * x)))
            for k in range(MLP_COLS // 128):
                row, lane = divmod(j * MLP_COLS + k * 128, width)
                weight = 0.5 * small[4 + row : 5 + row, lane : lane + 128]
                acc = acc + x[:, k * 128 : (k + 1) * 128] * weight
        ranked_ref[at, :] = jnp.broadcast_to(jnp.sum(acc, axis=1, keepdims=True), acc.shape)
        return carry

    lax.fori_loop(0, (starts[requests] + MLP_ROWS - 1) // MLP_ROWS, mlp, 0)
    row = lax.broadcasted_iota(I32, (slots, slots), 0).astype(F32)
    for r in range(requests):
        ranked = ranked_ref[pl.ds(pl.multiple_of(starts[r], 16), slots), :]
        ranked = jnp.concatenate([ranked] * (slots // 128), axis=1)
        hit = row == small[0:1, r * slots : (r + 1) * slots]
        rank_out[r : r + 1, :] = jnp.sum(jnp.where(hit, ranked, 0.0), axis=0, keepdims=True)


def select_call(surv_count, surv_index, cands, rank_wq, pre_wq, pre_wkv, rank_wkv, norm_gain, score_w):
    requests, slots = surv_index.shape
    width = rank_wq.shape[1]
    return pl.pallas_call(
        select_kernel,
        name="select",
        out_shape=jax.ShapeDtypeStruct((PACK, width), BF),
        in_specs=[SMEM, VMEM, HBM, HBM, HBM, HBM, HBM, VMEM, VMEM],
        out_specs=HBM,
        scratch_shapes=[
            pltpu.VMEM((PACK, width), BF),
            pltpu.VMEM(cands.shape, BF),
            pltpu.VMEM(rank_wq.shape, BF),
            pltpu.VMEM(pre_wq.shape, BF),
            pltpu.SemaphoreType.DMA((6,)),
            pltpu.SemaphoreType.DMA((3,)),
        ],
        compiler_params=pltpu.CompilerParams(vmem_limit_bytes=SELECT_LIMIT),
        cost_estimate=pl.CostEstimate(flops=2 * 10**9, bytes_accessed=12 * 2**20, transcendentals=0),
    )(
        surv_count.reshape(requests), surv_index, cands, rank_wq, pre_wq, pre_wkv, rank_wkv,
        norm_gain.reshape(1, -1), score_w.reshape(-1, 128),
    )


def after_kernel(x_ref, first_ref, out_ref):
    pass


def after(x, first):
    return pl.pallas_call(
        after_kernel,
        name="after",
        out_shape=jax.ShapeDtypeStruct(x.shape, x.dtype),
        in_specs=[ANY, ANY],
        out_specs=ANY,
        input_output_aliases={0: 0},
        compiler_params=pltpu.CompilerParams(vmem_limit_bytes=53 * 2**20),
    )(x, first)


def rank_call(chunks, pack, mlp_up):
    nz, requests, here, _ = chunks[0].shape
    width = pack.shape[1]
    slots = width // requests
    events = 2 * nz * here
    padded = -(-requests * slots // MLP_ROWS) * MLP_ROWS
    state = jax.ShapeDtypeStruct((requests, slots + 8, width + 128), F32)
    attention = [
        pltpu.VMEM((events, width), BF),
        pltpu.VMEM((events, 2 * width), BF),
        pltpu.VMEM(pack.shape, BF),
        pltpu.SemaphoreType.DMA((2,)),
        pltpu.VMEM(state.shape, F32),
        pltpu.SemaphoreType.DMA((requests,)),
    ]
    state = pl.pallas_call(
        first_kernel,
        name="rank_first",
        out_shape=state,
        in_specs=[VMEM, VMEM, HBM],
        out_specs=HBM,
        scratch_shapes=attention,
        compiler_params=pltpu.CompilerParams(vmem_limit_bytes=RANK_LIMIT),
        cost_estimate=pl.CostEstimate(flops=6 * 10**9, bytes_accessed=10 * 2**20, transcendentals=2 * 10**6),
    )(*chunks[:2], pack)
    score = jax.ShapeDtypeStruct((requests, slots), F32)
    return pl.pallas_call(
        last_kernel,
        name="rank_last",
        out_shape=(score, score),
        in_specs=[VMEM, VMEM, HBM, HBM, HBM],
        out_specs=(VMEM, VMEM),
        scratch_shapes=attention
        + [
            pltpu.VMEM((padded, width), BF),
            pltpu.VMEM((padded, 128), F32),
            pltpu.VMEM(mlp_up.shape, BF),
            pltpu.SemaphoreType.DMA,
        ],
        compiler_params=pltpu.CompilerParams(vmem_limit_bytes=RANK_LIMIT),
        cost_estimate=pl.CostEstimate(flops=16 * 10**9, bytes_accessed=20 * 2**20, transcendentals=4 * 10**6),
    )(*chunks[2:], pack, state, mlp_up)


def body(history, cands, surv_count, surv_index, pre_wq, pre_wkv, rank_wq, rank_wkv, norm_gain, mlp_up, score_w):
    nx = 4
    nz = lax.axis_size("cand") // nx
    columns = [[z * nx + x for z in range(nz)] for x in range(nx)]

    def shift(x, by):
        pairs = [(z * nx + a, z * nx + (a + by) % nx) for z in range(nz) for a in range(nx)]
        return lax.ppermute(x, "cand", pairs)

    copies = jnp.broadcast_to(history[None], (nz,) + history.shape)
    own = lax.all_to_all(copies, "cand", split_axis=0, concat_axis=0, tiled=True, axis_index_groups=columns)
    pack = select_call(
        surv_count, surv_index, cands, rank_wq, pre_wq, pre_wkv, rank_wkv, norm_gain, score_w
    )
    own = after(own, pack)
    chunks = [own] + [shift(own, by) for by in (1, 3, 2)]
    return rank_call(chunks, pack, mlp_up)


def solution(mesh):
    in_specs = (
        P("grp", "cand", None),
        P("grp", "cand", None),
        P("grp", "cand"),
        P("grp", "cand"),
        P(),
        P(),
        P(),
        P(),
        P(),
        P(),
        P(),
    )
    out_specs = (P("grp", "cand"), P("grp", "cand"))
    return jax.shard_map(body, mesh=mesh, in_specs=in_specs, out_specs=out_specs, check_vma=False)
```

```python
import functools
import math

import jax
import jax.numpy as jnp
from jax import lax
from jax.experimental import pallas as pl
from jax.experimental.pallas import tpu as pltpu
from jax.sharding import PartitionSpec as P

HEADS = 8
BF = jnp.bfloat16
F32 = jnp.float32
I32 = jnp.int32
LOG2E = 1.4426950408889634
GELU_A = math.sqrt(2.0 / math.pi)
GELU_B = GELU_A * 0.044715
ROW_TILES = (128, 176, 256)
MLP_ROWS = 160
MLP_COLS = 512
PRE_Q = 1024
PRE_WKV = 1280
RANK_WK = 1536
RANK_WV = 1792
SMALL = 2048
PACK = 2064
SELECT_LIMIT = 57 * 2**20
RANK_LIMIT = 50 * 2**20
VMEM = pl.BlockSpec(memory_space=pltpu.VMEM)
SMEM = pl.BlockSpec(memory_space=pltpu.SMEM)
HBM = pl.BlockSpec(memory_space=pltpu.HBM)
ANY = pl.BlockSpec(memory_space=pl.ANY)


def dot(a, b):
    return jnp.dot(a, b, preferred_element_type=F32)


def dot_t(a, b):
    return lax.dot_general(a, b, (((1,), (1,)), ((), ())), preferred_element_type=F32)


def select_kernel(
    count_ref,
    index_ref,
    cands_hbm,
    wq_hbm,
    pre_wq_hbm,
    pre_wkv_hbm,
    wkv_hbm,
    gain_ref,
    score_w_ref,
    pack_hbm,
    pack_ref,
    cands_ref,
    wq_ref,
    pre_wq_ref,
    sems,
    out_sem,
):
    width = pack_hbm.shape[1]
    pairs = (
        (cands_hbm, cands_ref),
        (wq_hbm, wq_ref),
        (pre_wq_hbm, pre_wq_ref),
        (pre_wkv_hbm, pack_ref.at[pl.ds(PRE_WKV, pre_wkv_hbm.shape[0]), pl.ds(0, pre_wkv_hbm.shape[1])]),
        (wkv_hbm.at[:, pl.ds(0, width)], pack_ref.at[pl.ds(RANK_WK, RANK_WV - RANK_WK)]),
        (wkv_hbm.at[:, pl.ds(width, width)], pack_ref.at[pl.ds(RANK_WV, SMALL - RANK_WV)]),
    )
    copies = [pltpu.make_async_copy(a, b, sems.at[i]) for i, (a, b) in enumerate(pairs)]
    for copy in copies:
        copy.start()
    requests, slots = index_ref.shape
    _, cands, features = cands_ref.shape
    row_c = lax.broadcasted_iota(I32, (cands, slots), 0)
    lane = lax.broadcasted_iota(I32, (1, slots), 1)
    before = (
        lax.broadcasted_iota(I32, (cands, cands), 0) < lax.broadcasted_iota(I32, (cands, cands), 1)
    ).astype(BF)
    place_c = lax.broadcasted_iota(I32, (slots, cands), 0).astype(F32)
    ones = jnp.ones((8, slots), BF)
    for copy in copies[:3]:
        copy.wait()
    start = jnp.int32(0)
    places = []
    for r in range(requests):
        valid = lane < count_ref[r]
        picked = jnp.where(valid, index_ref[r : r + 1, :], -1)
        match = (row_c == picked).astype(F32).astype(BF)
        used = jnp.where(dot_t(ones, match) > 0.5, 1.0, 0.0)
        position = dot(used.astype(BF), before)
        number = jnp.sum(used[0:1, :]).astype(I32)
        places.append(jnp.where(valid, dot(position.astype(BF), match)[0:1, :], -1.0))
        chosen = jnp.where((used[0:1, :] > 0.5) & (position[0:1, :] == place_c), 1.0, 0.0).astype(BF)
        mine = cands_ref[r]
        rows = dot(chosen, mine).astype(BF)
        pack_ref[pl.ds(pl.multiple_of(start, 16), slots), :] = dot(rows, wq_ref[...]).astype(BF)
        start = start + (((number + 15) >> 4) << 4)
        pack_ref[PRE_Q : PRE_Q + features, r * slots : (r + 1) * slots] = lax.dot_general(
            pre_wq_ref[...], mine, (((0,), (1,)), ((), ())), preferred_element_type=F32
        ).astype(BF)
    gain = gain_ref[...]
    high = gain.astype(BF).astype(F32)
    middle = (gain - high).astype(BF).astype(F32)
    per_row = width // 128
    small = [jnp.concatenate(places, axis=1), high, middle, gain - high - middle]
    for k in range(score_w_ref.shape[0] // per_row):
        lanes = [score_w_ref[i : i + 1, :].astype(F32) for i in range(k * per_row, (k + 1) * per_row)]
        small.append(jnp.concatenate(lanes, axis=1))
    small.append(jnp.zeros((PACK - SMALL - len(small), width), F32))
    pack_ref[SMALL:PACK, :] = jnp.concatenate(small, axis=0).astype(BF)
    for copy in copies[3:]:
        copy.wait()
    write = pltpu.make_async_copy(pack_ref, pack_hbm, out_sem)
    write.start()
    write.wait()


def attend(
    chunk_refs,
    pack_hbm,
    pack_ref,
    pack_sems,
    keys_ref,
    values_ref,
    normed_ref,
    state_ref,
    state_hbm,
    state_sems,
    pre_out,
    extra=None,
):
    last = normed_ref is not None
    requests, _, _ = state_ref.shape
    events, width = keys_ref.shape
    head = width // HEADS
    features = chunk_refs[0].shape[-1]
    slots = width // requests
    rows = [(PRE_Q, PACK - PRE_Q), (0, PRE_Q)]
    copies = [
        pltpu.make_async_copy(pack_hbm.at[pl.ds(*at)], pack_ref.at[pl.ds(*at)], pack_sems.at[i])
        for i, at in enumerate(rows)
    ]
    copies[0].start()
    if last:
        pltpu.make_async_copy(state_hbm.at[0], state_ref.at[0], state_sems.at[0]).start()
    copies[1].start()
    if last:
        for r in range(1, requests):
            pltpu.make_async_copy(state_hbm.at[r], state_ref.at[r], state_sems.at[r]).start()
        extra.start()
    for h in range(HEADS):
        values_ref[:, (2 * h + 1) * head : (2 * h + 2) * head] = jnp.ones((events, head), BF)
    scale = LOG2E / math.sqrt(head)
    pre_scale = LOG2E / math.sqrt(features)
    copies[0].wait()
    small = pack_ref[SMALL:PACK, :].astype(F32)
    gain = small[1:2, :] + small[2:3, :] + small[3:4, :]
    numbers = [jnp.max(small[0:1, r * slots : (r + 1) * slots]).astype(I32) + 1 for r in range(requests)]
    starts = [jnp.int32(0)]
    for number in numbers:
        starts.append(starts[-1] + (((number + 15) >> 4) << 4))

    def request(r, carry):
        number, start = numbers[0], starts[0]
        for k in range(1, requests):
            number, start = jnp.where(r == k, numbers[k], number), jnp.where(r == k, starts[k], start)
        parts = [ref[:, pl.ds(r, 1)].reshape(events // len(chunk_refs), features) for ref in chunk_refs]
        history = jnp.concatenate(parts, axis=0)
        pre_q = pack_ref[PRE_Q : PRE_Q + features, pl.ds(pl.multiple_of(r * slots, slots), slots)]
        pre_keys = dot(history, pack_ref[PRE_WKV : PRE_WKV + features, :features]).astype(BF)
        pre_values = lax.dot_general(
            pack_ref[PRE_WKV : PRE_WKV + features, features : 2 * features],
            history,
            (((0,), (1,)), ((), ())),
            preferred_element_type=F32,
        ).astype(BF)
        logits = dot(pre_keys, pre_q)
        top = jnp.max(logits, axis=0, keepdims=True)
        weights = jnp.exp2((logits - top) * pre_scale).astype(BF)
        mass = jnp.sum(weights.astype(F32), axis=0, keepdims=True)
        query = pre_q.astype(F32)
        score = jnp.sum(dot(pre_values, weights) * query, axis=0, keepdims=True)
        for c in range(2):
            cols = slice(c * width // 2, (c + 1) * width // 2)
            keys_ref[:, cols] = dot(history, pack_ref[RANK_WK:RANK_WV, cols]).astype(BF)
        for c in range(2):
            cols = slice(c * width // 2, (c + 1) * width // 2)
            part = dot(history, pack_ref[RANK_WV:SMALL, cols]).astype(BF)
            for k in range(HEADS // 2):
                h = c * HEADS // 2 + k
                values_ref[:, 2 * h * head : (2 * h + 1) * head] = part[:, k * head : (k + 1) * head]
        pl.when(r == 0)(copies[1].wait)
        if last:
            pltpu.make_async_copy(state_hbm.at[r], state_ref.at[r], state_sems.at[r]).wait()
            other_top = state_ref[r, slots : slots + 1, :slots]
            peak = jnp.maximum(top, other_top)
            mine, other = jnp.exp2((top - peak) * pre_scale), jnp.exp2((other_top - peak) * pre_scale)
            score = score * mine + state_ref[r, slots + 2 : slots + 3, :slots] * other
            mass = mass * mine + state_ref[r, slots + 1 : slots + 2, :slots] * other
            length = jnp.sqrt(jnp.sum(query * query, axis=0, keepdims=True))
            pre_out[pl.ds(r, 1), :] = score / mass / (1.0 + length)
        else:
            state_ref[r, slots : slots + 1, :slots] = top
            state_ref[r, slots + 1 : slots + 2, :slots] = mass
            state_ref[r, slots + 2 : slots + 3, :slots] = score

        def tile(rows):
            at = pl.ds(pl.multiple_of(start, 16), rows)
            mixed = []
            stat = jnp.zeros((rows, 128), F32)
            lane = lax.broadcasted_iota(I32, (rows, 128), 1)
            for h in range(HEADS):
                cols = slice(h * head, (h + 1) * head)
                query = pack_ref[at, cols]
                logits = dot_t(query, keys_ref[:, cols])
                top = jnp.max(logits, axis=1, keepdims=True)
                weights = jnp.exp2((logits - top) * scale).astype(BF)
                both = dot(weights, values_ref[:, 2 * h * head : (2 * h + 2) * head])
                mass = both[:, head:]
                out = both[:, :head] / mass
                mass = top * scale + jnp.log2(mass)
                if last:
                    share = 1.0 / (1.0 + jnp.exp2(state_ref[r, :rows, width + h : width + h + 1] - mass))
                    other = state_ref[r, :rows, cols]
                    mixed.append(query.astype(F32) + other + share * (out - other))
                else:
                    state_ref[r, :rows, cols] = out
                    stat = jnp.where(lane == h, mass, stat)
            if not last:
                state_ref[r, :rows, width : width + 128] = stat
                return
            acc = mixed[0]
            for one in mixed[1:]:
                acc = acc + one
            center = jnp.sum(acc, axis=1, keepdims=True) * (1.0 / width)
            acc = jnp.zeros((rows, head), F32)
            for one in mixed:
                acc = acc + (one - center) * (one - center)
            spread = jnp.sum(acc, axis=1, keepdims=True) * (1.0 / width)
            inverse = lax.rsqrt(spread + 1e-05)
            for h in range(HEADS):
                cols = slice(h * head, (h + 1) * head)
                normed_ref[at, cols] = ((mixed[h] - center) * inverse * gain[:, cols]).astype(BF)

        low = 0
        for rows in ROW_TILES:
            pl.when((number > low) & (number <= rows))(functools.partial(tile, rows))
            low = rows
        if not last:
            pltpu.make_async_copy(state_ref.at[r], state_hbm.at[r], state_sems.at[r]).start()
        return carry

    lax.fori_loop(0, requests, request, 0)
    if not last:
        for r in range(requests):
            pltpu.make_async_copy(state_ref.at[r], state_hbm.at[r], state_sems.at[r]).wait()
    return starts, small


def first_kernel(
    own_ref, pack_hbm,
    state_hbm,
    keys_ref, values_ref, pack_ref, pack_sems, state_ref, state_sems,
):
    attend(
        (own_ref,), pack_hbm, pack_ref, pack_sems, keys_ref, values_ref, None, state_ref, state_hbm, state_sems, None
    )


def last_kernel(
    a_ref, b_ref, c_ref, pack_hbm, state_hbm, up_hbm,
    pre_out, rank_out,
    keys_ref, values_ref, pack_ref, pack_sems, state_ref, state_sems, normed_ref, ranked_ref, up_ref, sem,
):
    up_copy = pltpu.make_async_copy(up_hbm, up_ref, sem)
    requests, slots = rank_out.shape
    starts, small = attend(
        (a_ref, b_ref, c_ref), pack_hbm, pack_ref, pack_sems, keys_ref, values_ref, normed_ref, state_ref, state_hbm, state_sems,
        pre_out, up_copy,
    )
    up_copy.wait()
    width, hidden_size = up_ref.shape

    def mlp(t, carry):
        at = pl.ds(pl.multiple_of(t * MLP_ROWS, 16), MLP_ROWS)
        rows = normed_ref[at, :]
        acc = jnp.zeros((MLP_ROWS, 128), F32)
        for j in range(hidden_size // MLP_COLS):
            cols = slice(j * MLP_COLS, (j + 1) * MLP_COLS)
            x = dot(rows, up_ref[:, cols])
            x = x + x * jnp.tanh(x * (GELU_A + GELU_B * (x * x)))
            for k in range(MLP_COLS // 128):
                row, lane = divmod(j * MLP_COLS + k * 128, width)
                weight = 0.5 * small[4 + row : 5 + row, lane : lane + 128]
                acc = acc + x[:, k * 128 : (k + 1) * 128] * weight
        ranked_ref[at, :] = jnp.broadcast_to(jnp.sum(acc, axis=1, keepdims=True), acc.shape)
        return carry

    lax.fori_loop(0, (starts[requests] + MLP_ROWS - 1) // MLP_ROWS, mlp, 0)
    row = lax.broadcasted_iota(I32, (slots, slots), 0).astype(F32)
    for r in range(requests):
        ranked = ranked_ref[pl.ds(pl.multiple_of(starts[r], 16), slots), :]
        ranked = jnp.concatenate([ranked] * (slots // 128), axis=1)
        hit = row == small[0:1, r * slots : (r + 1) * slots]
        rank_out[r : r + 1, :] = jnp.sum(jnp.where(hit, ranked, 0.0), axis=0, keepdims=True)


def select_call(surv_count, surv_index, cands, rank_wq, pre_wq, pre_wkv, rank_wkv, norm_gain, score_w):
    requests, slots = surv_index.shape
    width = rank_wq.shape[1]
    return pl.pallas_call(
        select_kernel,
        name="select",
        out_shape=jax.ShapeDtypeStruct((PACK, width), BF),
        in_specs=[SMEM, VMEM, HBM, HBM, HBM, HBM, HBM, VMEM, VMEM],
        out_specs=HBM,
        scratch_shapes=[
            pltpu.VMEM((PACK, width), BF),
            pltpu.VMEM(cands.shape, BF),
            pltpu.VMEM(rank_wq.shape, BF),
            pltpu.VMEM(pre_wq.shape, BF),
            pltpu.SemaphoreType.DMA((6,)),
            pltpu.SemaphoreType.DMA,
        ],
        compiler_params=pltpu.CompilerParams(vmem_limit_bytes=SELECT_LIMIT),
        cost_estimate=pl.CostEstimate(flops=2 * 10**9, bytes_accessed=12 * 2**20, transcendentals=0),
    )(
        surv_count.reshape(requests), surv_index, cands, rank_wq, pre_wq, pre_wkv, rank_wkv,
        norm_gain.reshape(1, -1), score_w.reshape(-1, 128),
    )


def after_kernel(x_ref, first_ref, out_ref):
    pass


def after(x, first):
    return pl.pallas_call(
        after_kernel,
        name="after",
        out_shape=jax.ShapeDtypeStruct(x.shape, x.dtype),
        in_specs=[ANY, ANY],
        out_specs=ANY,
        input_output_aliases={0: 0},
        compiler_params=pltpu.CompilerParams(vmem_limit_bytes=53 * 2**20),
    )(x, first)


def rank_call(chunks, pack, mlp_up):
    nz, requests, here, _ = chunks[0].shape
    width = pack.shape[1]
    slots = width // requests
    padded = -(-requests * slots // MLP_ROWS) * MLP_ROWS
    state = jax.ShapeDtypeStruct((requests, slots + 8, width + 128), F32)

    def attention(events):
        return [
            pltpu.VMEM((events, width), BF),
            pltpu.VMEM((events, 2 * width), BF),
            pltpu.VMEM(pack.shape, BF),
            pltpu.SemaphoreType.DMA((2,)),
            pltpu.VMEM((requests, slots + 8, width + 128), F32),
            pltpu.SemaphoreType.DMA((requests,)),
        ]

    state = pl.pallas_call(
        first_kernel,
        name="rank_first",
        out_shape=state,
        in_specs=[VMEM, HBM],
        out_specs=HBM,
        scratch_shapes=attention(nz * here),
        compiler_params=pltpu.CompilerParams(vmem_limit_bytes=RANK_LIMIT),
        cost_estimate=pl.CostEstimate(flops=6 * 10**9, bytes_accessed=10 * 2**20, transcendentals=2 * 10**6),
    )(chunks[0], pack)
    score = jax.ShapeDtypeStruct((requests, slots), F32)
    return pl.pallas_call(
        last_kernel,
        name="rank_last",
        out_shape=(score, score),
        in_specs=[VMEM, VMEM, VMEM, HBM, HBM, HBM],
        out_specs=(VMEM, VMEM),
        scratch_shapes=attention(3 * nz * here)
        + [
            pltpu.VMEM((padded, width), BF),
            pltpu.VMEM((padded, 128), F32),
            pltpu.VMEM(mlp_up.shape, BF),
            pltpu.SemaphoreType.DMA,
        ],
        compiler_params=pltpu.CompilerParams(vmem_limit_bytes=RANK_LIMIT),
        cost_estimate=pl.CostEstimate(flops=16 * 10**9, bytes_accessed=20 * 2**20, transcendentals=4 * 10**6),
    )(*chunks[1:], pack, state, mlp_up)


def body(history, cands, surv_count, surv_index, pre_wq, pre_wkv, rank_wq, rank_wkv, norm_gain, mlp_up, score_w):
    nx = 4
    nz = lax.axis_size("cand") // nx
    columns = [[z * nx + x for z in range(nz)] for x in range(nx)]

    def shift(x, by):
        pairs = [(z * nx + a, z * nx + (a + by) % nx) for z in range(nz) for a in range(nx)]
        return lax.ppermute(x, "cand", pairs)

    copies = jnp.broadcast_to(history[None], (nz,) + history.shape)
    own = lax.all_to_all(copies, "cand", split_axis=0, concat_axis=0, tiled=True, axis_index_groups=columns)
    pack = select_call(
        surv_count, surv_index, cands, rank_wq, pre_wq, pre_wkv, rank_wkv, norm_gain, score_w
    )
    own = after(own, pack)
    chunks = [own] + [shift(own, by) for by in (1, 3, 2)]
    return rank_call(chunks, pack, mlp_up)


def solution(mesh):
    in_specs = (
        P("grp", "cand", None),
        P("grp", "cand", None),
        P("grp", "cand"),
        P("grp", "cand"),
        P(),
        P(),
        P(),
        P(),
        P(),
        P(),
        P(),
    )
    out_specs = (P("grp", "cand"), P("grp", "cand"))
    return jax.shard_map(body, mesh=mesh, in_specs=in_specs, out_specs=out_specs, check_vma=False)
```

```python
import functools
import math

import jax
import jax.numpy as jnp
from jax import lax
from jax.experimental import pallas as pl
from jax.experimental.pallas import tpu as pltpu
from jax.sharding import PartitionSpec as P

HEADS = 8
BF = jnp.bfloat16
F32 = jnp.float32
I32 = jnp.int32
LOG2E = 1.4426950408889634
GELU_A = math.sqrt(2.0 / math.pi)
GELU_B = GELU_A * 0.044715
ROW_TILES = (128, 176, 256)
MLP_ROWS = 352
MLP_COLS = 512
PRE_Q = 1024
PRE_WKV = 1280
RANK_WK = 1536
RANK_WV = 1792
SMALL = 2048
PACK = 2064
SELECT_LIMIT = 57 * 2**20
RANK_LIMIT = 50 * 2**20
VMEM = pl.BlockSpec(memory_space=pltpu.VMEM)
SMEM = pl.BlockSpec(memory_space=pltpu.SMEM)
HBM = pl.BlockSpec(memory_space=pltpu.HBM)


def dot(a, b):
    return jnp.dot(a, b, preferred_element_type=F32)


def dot_t(a, b):
    return lax.dot_general(a, b, (((1,), (1,)), ((), ())), preferred_element_type=F32)


def select_kernel(
    count_ref,
    index_ref,
    cands_hbm,
    wq_hbm,
    pre_wq_hbm,
    pre_wkv_hbm,
    wkv_hbm,
    gain_ref,
    score_w_ref,
    pack_hbm,
    pack_ref,
    cands_ref,
    wq_ref,
    pre_wq_ref,
    sems,
    out_sem,
):
    width = pack_hbm.shape[1]
    pairs = (
        (cands_hbm, cands_ref),
        (wq_hbm, wq_ref),
        (pre_wq_hbm, pre_wq_ref),
        (pre_wkv_hbm, pack_ref.at[pl.ds(PRE_WKV, pre_wkv_hbm.shape[0]), pl.ds(0, pre_wkv_hbm.shape[1])]),
        (wkv_hbm.at[:, pl.ds(0, width)], pack_ref.at[pl.ds(RANK_WK, RANK_WV - RANK_WK)]),
        (wkv_hbm.at[:, pl.ds(width, width)], pack_ref.at[pl.ds(RANK_WV, SMALL - RANK_WV)]),
    )
    copies = [pltpu.make_async_copy(a, b, sems.at[i]) for i, (a, b) in enumerate(pairs)]
    for copy in copies:
        copy.start()
    requests, slots = index_ref.shape
    _, cands, features = cands_ref.shape
    row_c = lax.broadcasted_iota(I32, (cands, slots), 0)
    lane = lax.broadcasted_iota(I32, (1, slots), 1)
    before = (
        lax.broadcasted_iota(I32, (cands, cands), 0) < lax.broadcasted_iota(I32, (cands, cands), 1)
    ).astype(BF)
    place_c = lax.broadcasted_iota(I32, (slots, cands), 0).astype(F32)
    ones = jnp.ones((8, slots), BF)
    for copy in copies[:3]:
        copy.wait()
    start = jnp.int32(0)
    places = []
    for r in range(requests):
        valid = lane < count_ref[r]
        picked = jnp.where(valid, index_ref[r : r + 1, :], -1)
        match = (row_c == picked).astype(F32).astype(BF)
        used = jnp.where(dot_t(ones, match) > 0.5, 1.0, 0.0)
        position = dot(used.astype(BF), before)
        number = jnp.sum(used[0:1, :]).astype(I32)
        places.append(jnp.where(valid, dot(position.astype(BF), match)[0:1, :], -1.0))
        chosen = jnp.where((used[0:1, :] > 0.5) & (position[0:1, :] == place_c), 1.0, 0.0).astype(BF)
        mine = cands_ref[r]
        rows = dot(chosen, mine).astype(BF)
        pack_ref[pl.ds(pl.multiple_of(start, 16), slots), :] = dot(rows, wq_ref[...]).astype(BF)
        start = start + (((number + 15) >> 4) << 4)
        pack_ref[PRE_Q : PRE_Q + features, r * slots : (r + 1) * slots] = lax.dot_general(
            pre_wq_ref[...], mine, (((0,), (1,)), ((), ())), preferred_element_type=F32
        ).astype(BF)
    gain = gain_ref[...]
    high = gain.astype(BF).astype(F32)
    middle = (gain - high).astype(BF).astype(F32)
    per_row = width // 128
    small = [jnp.concatenate(places, axis=1), high, middle, gain - high - middle]
    for k in range(score_w_ref.shape[0] // per_row):
        lanes = [score_w_ref[i : i + 1, :].astype(F32) for i in range(k * per_row, (k + 1) * per_row)]
        small.append(jnp.concatenate(lanes, axis=1))
    small.append(jnp.zeros((PACK - SMALL - len(small), width), F32))
    pack_ref[SMALL:PACK, :] = jnp.concatenate(small, axis=0).astype(BF)
    for copy in copies[3:]:
        copy.wait()
    write = pltpu.make_async_copy(pack_ref, pack_hbm, out_sem)
    write.start()
    write.wait()


def attend(
    chunk_refs,
    pack_hbm,
    pack_ref,
    pack_sems,
    keys_ref,
    values_ref,
    normed_ref,
    pre_out,
    up_copy,
):
    requests, slots = pre_out.shape
    events, width = keys_ref.shape
    half = width // 2
    head = width // HEADS
    features = chunk_refs[0].shape[-1]
    rows = [(PRE_Q, PACK - PRE_Q), (0, PRE_Q)]
    copies = [
        pltpu.make_async_copy(pack_hbm.at[pl.ds(*at)], pack_ref.at[pl.ds(*at)], pack_sems.at[i])
        for i, at in enumerate(rows)
    ]
    for copy in copies:
        copy.start()
    up_copy.start()
    for h in range(HEADS):
        values_ref[:, (2 * h + 1) * head : (2 * h + 2) * head] = jnp.ones((events, head), BF)
    scale = LOG2E / math.sqrt(head)
    pre_scale = LOG2E / math.sqrt(features)
    copies[0].wait()
    small = pack_ref[SMALL:PACK, :].astype(F32)
    gain = small[1:2, :] + small[2:3, :] + small[3:4, :]
    numbers = [jnp.max(small[0:1, r * slots : (r + 1) * slots]).astype(I32) + 1 for r in range(requests)]
    starts = [jnp.int32(0)]
    for number in numbers:
        starts.append(starts[-1] + (((number + 15) >> 4) << 4))

    def request(r, carry):
        number, start = numbers[0], starts[0]
        for k in range(1, requests):
            number, start = jnp.where(r == k, numbers[k], number), jnp.where(r == k, starts[k], start)
        parts = [ref[:, pl.ds(r, 1)].reshape(events // len(chunk_refs), features) for ref in chunk_refs]
        history = jnp.concatenate(parts, axis=0)

        def put_keys(c):
            cols = slice(c * half, (c + 1) * half)
            keys_ref[:, cols] = dot(history, pack_ref[RANK_WK:RANK_WV, cols]).astype(BF)

        def put_values(c):
            part = dot(history, pack_ref[RANK_WV:SMALL, c * half : (c + 1) * half]).astype(BF)
            for k in range(HEADS // 2):
                h = c * HEADS // 2 + k
                values_ref[:, 2 * h * head : (2 * h + 1) * head] = part[:, k * head : (k + 1) * head]

        pre_q = pack_ref[PRE_Q : PRE_Q + features, pl.ds(pl.multiple_of(r * slots, slots), slots)]
        pre_keys = dot(history, pack_ref[PRE_WKV : PRE_WKV + features, :features]).astype(BF)
        pre_values = lax.dot_general(
            pack_ref[PRE_WKV : PRE_WKV + features, features : 2 * features],
            history,
            (((0,), (1,)), ((), ())),
            preferred_element_type=F32,
        ).astype(BF)
        put_keys(0)
        logits = dot(pre_keys, pre_q)
        put_keys(1)
        top = jnp.max(logits, axis=0, keepdims=True)
        weights = jnp.exp2((logits - top) * pre_scale)
        weights = (weights * (1.0 / jnp.sum(weights, axis=0, keepdims=True))).astype(BF)
        put_values(0)
        pooled = dot(pre_values, weights)
        put_values(1)
        query = pre_q.astype(F32)
        length = jnp.sqrt(jnp.sum(query * query, axis=0, keepdims=True))
        pre_out[pl.ds(r, 1), :] = jnp.sum(pooled * query, axis=0, keepdims=True) / (1.0 + length)
        pl.when(r == 0)(copies[1].wait)

        def tile(rows):
            at = pl.ds(pl.multiple_of(start, 16), rows)
            mixed = []
            for h in range(HEADS):
                cols = slice(h * head, (h + 1) * head)
                query = pack_ref[at, cols]
                logits = dot_t(query, keys_ref[:, cols])
                top = jnp.max(logits, axis=1, keepdims=True)
                weights = jnp.exp2((logits - top) * scale).astype(BF)
                both = dot(weights, values_ref[:, 2 * h * head : (2 * h + 2) * head])
                mixed.append(query.astype(F32) + both[:, :head] / both[:, head:])
            acc = mixed[0]
            for one in mixed[1:]:
                acc = acc + one
            center = jnp.sum(acc, axis=1, keepdims=True) * (1.0 / width)
            acc = jnp.zeros((rows, head), F32)
            for one in mixed:
                acc = acc + (one - center) * (one - center)
            spread = jnp.sum(acc, axis=1, keepdims=True) * (1.0 / width)
            inverse = lax.rsqrt(spread + 1e-05)
            for h in range(HEADS):
                cols = slice(h * head, (h + 1) * head)
                normed_ref[at, cols] = ((mixed[h] - center) * inverse * gain[:, cols]).astype(BF)

        low = 0
        for rows in ROW_TILES:
            pl.when((number > low) & (number <= rows))(functools.partial(tile, rows))
            low = rows
        return carry

    lax.fori_loop(0, requests, request, 0)
    return starts, small


def rank_kernel(
    own_ref, a_ref, b_ref, c_ref, pack_hbm, up_hbm,
    pre_out, rank_out,
    keys_ref, values_ref, pack_ref, pack_sems, normed_ref, ranked_ref, up_ref, sem,
):
    up_copy = pltpu.make_async_copy(up_hbm, up_ref, sem)
    requests, slots = rank_out.shape
    starts, small = attend(
        (own_ref, a_ref, b_ref, c_ref), pack_hbm, pack_ref, pack_sems, keys_ref, values_ref, normed_ref, pre_out, up_copy
    )
    up_copy.wait()
    width, hidden_size = up_ref.shape

    def mlp(t, carry):
        at = pl.ds(pl.multiple_of(t * MLP_ROWS, 16), MLP_ROWS)
        rows = normed_ref[at, :]
        acc = jnp.zeros((MLP_ROWS, 128), F32)
        for j in range(hidden_size // MLP_COLS):
            cols = slice(j * MLP_COLS, (j + 1) * MLP_COLS)
            x = dot(rows, up_ref[:, cols])
            x = x + x * jnp.tanh(x * (GELU_A + GELU_B * (x * x)))
            for k in range(MLP_COLS // 128):
                row, lane = divmod(j * MLP_COLS + k * 128, width)
                weight = 0.5 * small[4 + row : 5 + row, lane : lane + 128]
                acc = acc + x[:, k * 128 : (k + 1) * 128] * weight
        ranked_ref[at, :] = jnp.broadcast_to(jnp.sum(acc, axis=1, keepdims=True), acc.shape)
        return carry

    lax.fori_loop(0, (starts[requests] + MLP_ROWS - 1) // MLP_ROWS, mlp, 0)
    row = lax.broadcasted_iota(I32, (slots, slots), 0).astype(F32)
    for r in range(requests):
        ranked = ranked_ref[pl.ds(pl.multiple_of(starts[r], 16), slots), :]
        ranked = jnp.concatenate([ranked] * (slots // 128), axis=1)
        hit = row == small[0:1, r * slots : (r + 1) * slots]
        rank_out[r : r + 1, :] = jnp.sum(jnp.where(hit, ranked, 0.0), axis=0, keepdims=True)


def select_call(surv_count, surv_index, cands, rank_wq, pre_wq, pre_wkv, rank_wkv, norm_gain, score_w):
    requests, slots = surv_index.shape
    width = rank_wq.shape[1]
    return pl.pallas_call(
        select_kernel,
        name="select",
        out_shape=jax.ShapeDtypeStruct((PACK, width), BF),
        in_specs=[SMEM, VMEM, HBM, HBM, HBM, HBM, HBM, VMEM, VMEM],
        out_specs=HBM,
        scratch_shapes=[
            pltpu.VMEM((PACK, width), BF),
            pltpu.VMEM(cands.shape, BF),
            pltpu.VMEM(rank_wq.shape, BF),
            pltpu.VMEM(pre_wq.shape, BF),
            pltpu.SemaphoreType.DMA((6,)),
            pltpu.SemaphoreType.DMA,
        ],
        compiler_params=pltpu.CompilerParams(vmem_limit_bytes=SELECT_LIMIT),
        cost_estimate=pl.CostEstimate(flops=2 * 10**9, bytes_accessed=12 * 2**20, transcendentals=0),
    )(
        surv_count.reshape(requests), surv_index, cands, rank_wq, pre_wq, pre_wkv, rank_wkv,
        norm_gain.reshape(1, -1), score_w.reshape(-1, 128),
    )


def rank_call(chunks, pack, mlp_up):
    nz, requests, here, _ = chunks[0].shape
    width = pack.shape[1]
    slots = width // requests
    events = len(chunks) * nz * here
    padded = -(-requests * slots // MLP_ROWS) * MLP_ROWS
    score = jax.ShapeDtypeStruct((requests, slots), F32)
    return pl.pallas_call(
        rank_kernel,
        name="rank",
        out_shape=(score, score),
        in_specs=[VMEM] * 4 + [HBM, HBM],
        out_specs=(VMEM, VMEM),
        scratch_shapes=[
            pltpu.VMEM((events, width), BF),
            pltpu.VMEM((events, 2 * width), BF),
            pltpu.VMEM(pack.shape, BF),
            pltpu.SemaphoreType.DMA((2,)),
            pltpu.VMEM((padded, width), BF),
            pltpu.VMEM((padded, 128), F32),
            pltpu.VMEM(mlp_up.shape, BF),
            pltpu.SemaphoreType.DMA,
        ],
        compiler_params=pltpu.CompilerParams(vmem_limit_bytes=RANK_LIMIT),
        cost_estimate=pl.CostEstimate(flops=16 * 10**9, bytes_accessed=20 * 2**20, transcendentals=4 * 10**6),
    )(*chunks, pack, mlp_up)


def body(history, cands, surv_count, surv_index, pre_wq, pre_wkv, rank_wq, rank_wkv, norm_gain, mlp_up, score_w):
    nx = 4
    nz = lax.axis_size("cand") // nx
    columns = [[z * nx + x for z in range(nz)] for x in range(nx)]

    def shift(x, by):
        pairs = [(z * nx + a, z * nx + (a + by) % nx) for z in range(nz) for a in range(nx)]
        return lax.ppermute(x, "cand", pairs)

    copies = jnp.broadcast_to(history[None], (nz,) + history.shape)
    own = lax.all_to_all(copies, "cand", split_axis=0, concat_axis=0, tiled=True, axis_index_groups=columns)
    pack = select_call(
        surv_count, surv_index, cands, rank_wq, pre_wq, pre_wkv, rank_wkv, norm_gain, score_w
    )
    chunks = [own] + [shift(own, by) for by in (1, 3, 2)]
    return rank_call(chunks, pack, mlp_up)


def solution(mesh):
    in_specs = (
        P("grp", "cand", None),
        P("grp", "cand", None),
        P("grp", "cand"),
        P("grp", "cand"),
        P(),
        P(),
        P(),
        P(),
        P(),
        P(),
        P(),
    )
    out_specs = (P("grp", "cand"), P("grp", "cand"))
    return jax.shard_map(body, mesh=mesh, in_specs=in_specs, out_specs=out_specs, check_vma=False)
```

```python
import functools
import math

import jax
import jax.numpy as jnp
from jax import lax
from jax.experimental import pallas as pl
from jax.experimental.pallas import tpu as pltpu
from jax.sharding import PartitionSpec as P

HEADS = 8
BF = jnp.bfloat16
F32 = jnp.float32
I32 = jnp.int32
LOG2E = 1.4426950408889634
GELU_A = math.sqrt(2.0 / math.pi)
GELU_B = GELU_A * 0.044715
ROW_TILES = (128, 176, 256)
MLP_ROWS = 352
MLP_COLS = 512
PRE_Q = 1024
PRE_WKV = 1280
RANK_WK = 1536
RANK_WV = 1792
SMALL = 2048
PACK = 2064
FIXED = PRE_Q
SELECT_LIMIT = 57 * 2**20
RANK_LIMIT = 50 * 2**20
STAGE_LIMIT = 50 * 2**20
VMEM = pl.BlockSpec(memory_space=pltpu.VMEM)
SMEM = pl.BlockSpec(memory_space=pltpu.SMEM)
HBM = pl.BlockSpec(memory_space=pltpu.HBM)


def dot(a, b):
    return jnp.dot(a, b, preferred_element_type=F32)


def dot_t(a, b):
    return lax.dot_general(a, b, (((1,), (1,)), ((), ())), preferred_element_type=F32)


def select_kernel(
    count_ref,
    index_ref,
    cands_hbm,
    wq_hbm,
    pre_wq_hbm,
    pre_wkv_hbm,
    wkv_hbm,
    gain_ref,
    score_w_ref,
    pack_hbm,
    pack_ref,
    cands_ref,
    wq_ref,
    pre_wq_ref,
    sems,
    out_sem,
):
    width = pack_hbm.shape[1]
    pairs = (
        (cands_hbm, cands_ref),
        (wq_hbm, wq_ref),
        (pre_wq_hbm, pre_wq_ref),
        (pre_wkv_hbm, pack_ref.at[pl.ds(PRE_WKV, pre_wkv_hbm.shape[0]), pl.ds(0, pre_wkv_hbm.shape[1])]),
        (wkv_hbm.at[:, pl.ds(0, width)], pack_ref.at[pl.ds(RANK_WK, RANK_WV - RANK_WK)]),
        (wkv_hbm.at[:, pl.ds(width, width)], pack_ref.at[pl.ds(RANK_WV, SMALL - RANK_WV)]),
    )
    copies = [pltpu.make_async_copy(a, b, sems.at[i]) for i, (a, b) in enumerate(pairs)]
    for copy in copies:
        copy.start()
    requests, slots = index_ref.shape
    _, cands, features = cands_ref.shape
    row_c = lax.broadcasted_iota(I32, (cands, slots), 0)
    lane = lax.broadcasted_iota(I32, (1, slots), 1)
    before = (
        lax.broadcasted_iota(I32, (cands, cands), 0) < lax.broadcasted_iota(I32, (cands, cands), 1)
    ).astype(BF)
    place_c = lax.broadcasted_iota(I32, (slots, cands), 0).astype(F32)
    ones = jnp.ones((8, slots), BF)
    for copy in copies[:3]:
        copy.wait()
    start = jnp.int32(0)
    places = []
    for r in range(requests):
        valid = lane < count_ref[r]
        picked = jnp.where(valid, index_ref[r : r + 1, :], -1)
        match = (row_c == picked).astype(F32).astype(BF)
        used = jnp.where(dot_t(ones, match) > 0.5, 1.0, 0.0)
        position = dot(used.astype(BF), before)
        number = jnp.sum(used[0:1, :]).astype(I32)
        places.append(jnp.where(valid, dot(position.astype(BF), match)[0:1, :], -1.0))
        chosen = jnp.where((used[0:1, :] > 0.5) & (position[0:1, :] == place_c), 1.0, 0.0).astype(BF)
        mine = cands_ref[r]
        rows = dot(chosen, mine).astype(BF)
        pack_ref[pl.ds(pl.multiple_of(start, 16), slots), :] = dot(rows, wq_ref[...]).astype(BF)
        start = start + (((number + 15) >> 4) << 4)
        pack_ref[PRE_Q : PRE_Q + features, r * slots : (r + 1) * slots] = lax.dot_general(
            pre_wq_ref[...], mine, (((0,), (1,)), ((), ())), preferred_element_type=F32
        ).astype(BF)
    gain = gain_ref[...]
    high = gain.astype(BF).astype(F32)
    middle = (gain - high).astype(BF).astype(F32)
    per_row = width // 128
    small = [jnp.concatenate(places, axis=1), high, middle, gain - high - middle]
    for k in range(score_w_ref.shape[0] // per_row):
        lanes = [score_w_ref[i : i + 1, :].astype(F32) for i in range(k * per_row, (k + 1) * per_row)]
        small.append(jnp.concatenate(lanes, axis=1))
    small.append(jnp.zeros((PACK - SMALL - len(small), width), F32))
    pack_ref[SMALL:PACK, :] = jnp.concatenate(small, axis=0).astype(BF)
    for copy in copies[3:]:
        copy.wait()
    write = pltpu.make_async_copy(pack_ref, pack_hbm, out_sem)
    write.start()
    write.wait()


def attend(
    chunk_refs,
    pack_hbm,
    fixed_ref,
    query_ref,
    query_sem,
    keys_ref,
    values_ref,
    normed_ref,
    pre_out,
    up_copy,
):
    requests, slots = pre_out.shape
    events, width = keys_ref.shape
    half = width // 2
    head = width // HEADS
    features = chunk_refs[0].shape[-1]
    query_copy = pltpu.make_async_copy(pack_hbm.at[pl.ds(0, PRE_Q)], query_ref, query_sem)
    query_copy.start()
    up_copy.start()
    for h in range(HEADS):
        values_ref[:, (2 * h + 1) * head : (2 * h + 2) * head] = jnp.ones((events, head), BF)
    scale = LOG2E / math.sqrt(head)
    pre_w = slice(PRE_WKV - FIXED, PRE_WKV - FIXED + features)
    pre_scale = LOG2E / math.sqrt(features)
    small = fixed_ref[SMALL - FIXED : PACK - FIXED, :].astype(F32)
    gain = small[1:2, :] + small[2:3, :] + small[3:4, :]
    numbers = [jnp.max(small[0:1, r * slots : (r + 1) * slots]).astype(I32) + 1 for r in range(requests)]
    starts = [jnp.int32(0)]
    for number in numbers:
        starts.append(starts[-1] + (((number + 15) >> 4) << 4))

    def request(r, carry):
        number, start = numbers[0], starts[0]
        for k in range(1, requests):
            number, start = jnp.where(r == k, numbers[k], number), jnp.where(r == k, starts[k], start)
        parts = [ref[:, pl.ds(r, 1)].reshape(events // len(chunk_refs), features) for ref in chunk_refs]
        history = jnp.concatenate(parts, axis=0)

        def put_keys(c):
            cols = slice(c * half, (c + 1) * half)
            keys_ref[:, cols] = dot(history, fixed_ref[RANK_WK - FIXED : RANK_WV - FIXED, cols]).astype(BF)

        def put_values(c):
            part = dot(history, fixed_ref[RANK_WV - FIXED : SMALL - FIXED, c * half : (c + 1) * half]).astype(BF)
            for k in range(HEADS // 2):
                h = c * HEADS // 2 + k
                values_ref[:, 2 * h * head : (2 * h + 1) * head] = part[:, k * head : (k + 1) * head]

        pre_q = fixed_ref[PRE_Q - FIXED : PRE_Q - FIXED + features, pl.ds(pl.multiple_of(r * slots, slots), slots)]
        pre_keys = dot(history, fixed_ref[pre_w, :features]).astype(BF)
        pre_values = lax.dot_general(
            fixed_ref[pre_w, features : 2 * features],
            history,
            (((0,), (1,)), ((), ())),
            preferred_element_type=F32,
        ).astype(BF)
        put_keys(0)
        logits = dot(pre_keys, pre_q)
        put_keys(1)
        top = jnp.max(logits, axis=0, keepdims=True)
        weights = jnp.exp2((logits - top) * pre_scale)
        weights = (weights * (1.0 / jnp.sum(weights, axis=0, keepdims=True))).astype(BF)
        put_values(0)
        pooled = dot(pre_values, weights)
        put_values(1)
        query = pre_q.astype(F32)
        length = jnp.sqrt(jnp.sum(query * query, axis=0, keepdims=True))
        pre_out[pl.ds(r, 1), :] = jnp.sum(pooled * query, axis=0, keepdims=True) / (1.0 + length)
        pl.when(r == 0)(query_copy.wait)

        def tile(rows):
            at = pl.ds(pl.multiple_of(start, 16), rows)
            mixed = []
            for h in range(HEADS):
                cols = slice(h * head, (h + 1) * head)
                query = query_ref[at, cols]
                logits = dot_t(query, keys_ref[:, cols])
                top = jnp.max(logits, axis=1, keepdims=True)
                weights = jnp.exp2((logits - top) * scale).astype(BF)
                both = dot(weights, values_ref[:, 2 * h * head : (2 * h + 2) * head])
                mixed.append(query.astype(F32) + both[:, :head] / both[:, head:])
            acc = mixed[0]
            for one in mixed[1:]:
                acc = acc + one
            center = jnp.sum(acc, axis=1, keepdims=True) * (1.0 / width)
            acc = jnp.zeros((rows, head), F32)
            for one in mixed:
                acc = acc + (one - center) * (one - center)
            spread = jnp.sum(acc, axis=1, keepdims=True) * (1.0 / width)
            inverse = lax.rsqrt(spread + 1e-05)
            for h in range(HEADS):
                cols = slice(h * head, (h + 1) * head)
                normed_ref[at, cols] = ((mixed[h] - center) * inverse * gain[:, cols]).astype(BF)

        low = 0
        for rows in ROW_TILES:
            pl.when((number > low) & (number <= rows))(functools.partial(tile, rows))
            low = rows
        return carry

    lax.fori_loop(0, requests, request, 0)
    return starts, small


def rank_kernel(
    own_ref, a_ref, b_ref, c_ref, pack_hbm, fixed_ref, up_hbm,
    pre_out, rank_out,
    keys_ref, values_ref, query_ref, query_sem, normed_ref, ranked_ref, up_ref, sem,
):
    up_copy = pltpu.make_async_copy(up_hbm, up_ref, sem)
    requests, slots = rank_out.shape
    starts, small = attend(
        (own_ref, a_ref, b_ref, c_ref), pack_hbm, fixed_ref, query_ref, query_sem, keys_ref, values_ref, normed_ref,
        pre_out, up_copy,
    )
    up_copy.wait()
    width, hidden_size = up_ref.shape

    def mlp(t, carry):
        at = pl.ds(pl.multiple_of(t * MLP_ROWS, 16), MLP_ROWS)
        rows = normed_ref[at, :]
        acc = jnp.zeros((MLP_ROWS, 128), F32)
        for j in range(hidden_size // MLP_COLS):
            cols = slice(j * MLP_COLS, (j + 1) * MLP_COLS)
            x = dot(rows, up_ref[:, cols])
            x = x + x * jnp.tanh(x * (GELU_A + GELU_B * (x * x)))
            for k in range(MLP_COLS // 128):
                row, lane = divmod(j * MLP_COLS + k * 128, width)
                weight = 0.5 * small[4 + row : 5 + row, lane : lane + 128]
                acc = acc + x[:, k * 128 : (k + 1) * 128] * weight
        ranked_ref[at, :] = jnp.broadcast_to(jnp.sum(acc, axis=1, keepdims=True), acc.shape)
        return carry

    lax.fori_loop(0, (starts[requests] + MLP_ROWS - 1) // MLP_ROWS, mlp, 0)
    row = lax.broadcasted_iota(I32, (slots, slots), 0).astype(F32)
    for r in range(requests):
        ranked = ranked_ref[pl.ds(pl.multiple_of(starts[r], 16), slots), :]
        ranked = jnp.concatenate([ranked] * (slots // 128), axis=1)
        hit = row == small[0:1, r * slots : (r + 1) * slots]
        rank_out[r : r + 1, :] = jnp.sum(jnp.where(hit, ranked, 0.0), axis=0, keepdims=True)


def select_call(surv_count, surv_index, cands, rank_wq, pre_wq, pre_wkv, rank_wkv, norm_gain, score_w):
    requests, slots = surv_index.shape
    width = rank_wq.shape[1]
    return pl.pallas_call(
        select_kernel,
        name="select",
        out_shape=jax.ShapeDtypeStruct((PACK, width), BF),
        in_specs=[SMEM, VMEM, HBM, HBM, HBM, HBM, HBM, VMEM, VMEM],
        out_specs=HBM,
        scratch_shapes=[
            pltpu.VMEM((PACK, width), BF),
            pltpu.VMEM(cands.shape, BF),
            pltpu.VMEM(rank_wq.shape, BF),
            pltpu.VMEM(pre_wq.shape, BF),
            pltpu.SemaphoreType.DMA((6,)),
            pltpu.SemaphoreType.DMA,
        ],
        compiler_params=pltpu.CompilerParams(vmem_limit_bytes=SELECT_LIMIT),
        cost_estimate=pl.CostEstimate(flops=2 * 10**9, bytes_accessed=12 * 2**20, transcendentals=0),
    )(
        surv_count.reshape(requests), surv_index, cands, rank_wq, pre_wq, pre_wkv, rank_wkv,
        norm_gain.reshape(1, -1), score_w.reshape(-1, 128),
    )


def stage_kernel(pack_hbm, fixed_ref, sem):
    copy = pltpu.make_async_copy(pack_hbm.at[pl.ds(FIXED, PACK - FIXED)], fixed_ref, sem)
    copy.start()
    copy.wait()


def stage_call(pack):
    return pl.pallas_call(
        stage_kernel,
        name="stage",
        out_shape=jax.ShapeDtypeStruct((PACK - FIXED, pack.shape[1]), BF),
        in_specs=[HBM],
        out_specs=VMEM,
        scratch_shapes=[pltpu.SemaphoreType.DMA],
        compiler_params=pltpu.CompilerParams(vmem_limit_bytes=STAGE_LIMIT),
        cost_estimate=pl.CostEstimate(flops=0, bytes_accessed=4 * 2**20, transcendentals=0),
    )(pack)


def rank_call(chunks, pack, fixed, mlp_up):
    nz, requests, here, _ = chunks[0].shape
    width = pack.shape[1]
    slots = width // requests
    events = len(chunks) * nz * here
    padded = -(-requests * slots // MLP_ROWS) * MLP_ROWS
    score = jax.ShapeDtypeStruct((requests, slots), F32)
    return pl.pallas_call(
        rank_kernel,
        name="rank",
        out_shape=(score, score),
        in_specs=[VMEM] * 4 + [HBM, VMEM, HBM],
        out_specs=(VMEM, VMEM),
        scratch_shapes=[
            pltpu.VMEM((events, width), BF),
            pltpu.VMEM((events, 2 * width), BF),
            pltpu.VMEM((PRE_Q, width), BF),
            pltpu.SemaphoreType.DMA,
            pltpu.VMEM((padded, width), BF),
            pltpu.VMEM((padded, 128), F32),
            pltpu.VMEM(mlp_up.shape, BF),
            pltpu.SemaphoreType.DMA,
        ],
        compiler_params=pltpu.CompilerParams(vmem_limit_bytes=RANK_LIMIT),
        cost_estimate=pl.CostEstimate(flops=16 * 10**9, bytes_accessed=20 * 2**20, transcendentals=4 * 10**6),
    )(*chunks, pack, fixed, mlp_up)


def body(history, cands, surv_count, surv_index, pre_wq, pre_wkv, rank_wq, rank_wkv, norm_gain, mlp_up, score_w):
    nx = 4
    nz = lax.axis_size("cand") // nx
    columns = [[z * nx + x for z in range(nz)] for x in range(nx)]

    def shift(x, by):
        pairs = [(z * nx + a, z * nx + (a + by) % nx) for z in range(nz) for a in range(nx)]
        return lax.ppermute(x, "cand", pairs)

    copies = jnp.broadcast_to(history[None], (nz,) + history.shape)
    own = lax.all_to_all(copies, "cand", split_axis=0, concat_axis=0, tiled=True, axis_index_groups=columns)
    pack = select_call(
        surv_count, surv_index, cands, rank_wq, pre_wq, pre_wkv, rank_wkv, norm_gain, score_w
    )
    chunks = [own] + [shift(own, by) for by in (1, 3, 2)]
    return rank_call(chunks, pack, stage_call(pack), mlp_up)


def solution(mesh):
    in_specs = (
        P("grp", "cand", None),
        P("grp", "cand", None),
        P("grp", "cand"),
        P("grp", "cand"),
        P(),
        P(),
        P(),
        P(),
        P(),
        P(),
        P(),
    )
    out_specs = (P("grp", "cand"), P("grp", "cand"))
    return jax.shard_map(body, mesh=mesh, in_specs=in_specs, out_specs=out_specs, check_vma=False)
```

```python
import functools
import math

import jax
import jax.numpy as jnp
from jax import lax
from jax.experimental import pallas as pl
from jax.experimental.pallas import tpu as pltpu
from jax.sharding import PartitionSpec as P

HEADS = 8
BF = jnp.bfloat16
F32 = jnp.float32
I32 = jnp.int32
LOG2E = 1.4426950408889634
GELU_A = math.sqrt(2.0 / math.pi)
GELU_B = GELU_A * 0.044715
ROW_TILES = (128, 176, 256)
MLP_ROWS = (128, 192, 256, 336)
MLP_COLS = 512
PRE_Q = 1024
PRE_WKV = 1280
RANK_WK = 1536
RANK_WV = 1792
SMALL = 2048
PACK = 2064
FIXED = PRE_Q
SELECT_LIMIT = 57 * 2**20
RANK_LIMIT = 50 * 2**20
STAGE_LIMIT = 50 * 2**20
VMEM = pl.BlockSpec(memory_space=pltpu.VMEM)
SMEM = pl.BlockSpec(memory_space=pltpu.SMEM)
HBM = pl.BlockSpec(memory_space=pltpu.HBM)


def dot(a, b):
    return jnp.dot(a, b, preferred_element_type=F32)


def dot_t(a, b):
    return lax.dot_general(a, b, (((1,), (1,)), ((), ())), preferred_element_type=F32)


def select_kernel(
    count_ref,
    index_ref,
    cands_hbm,
    wq_hbm,
    pre_wq_hbm,
    pre_wkv_hbm,
    wkv_hbm,
    gain_ref,
    score_w_ref,
    pack_hbm,
    pack_ref,
    cands_ref,
    wq_ref,
    pre_wq_ref,
    sems,
    out_sem,
):
    width = pack_hbm.shape[1]
    pairs = (
        (cands_hbm, cands_ref),
        (wq_hbm, wq_ref),
        (pre_wq_hbm, pre_wq_ref),
        (pre_wkv_hbm, pack_ref.at[pl.ds(PRE_WKV, pre_wkv_hbm.shape[0]), pl.ds(0, pre_wkv_hbm.shape[1])]),
        (wkv_hbm.at[:, pl.ds(0, width)], pack_ref.at[pl.ds(RANK_WK, RANK_WV - RANK_WK)]),
        (wkv_hbm.at[:, pl.ds(width, width)], pack_ref.at[pl.ds(RANK_WV, SMALL - RANK_WV)]),
    )
    copies = [pltpu.make_async_copy(a, b, sems.at[i]) for i, (a, b) in enumerate(pairs)]
    for copy in copies:
        copy.start()
    requests, slots = index_ref.shape
    _, cands, features = cands_ref.shape
    row_c = lax.broadcasted_iota(I32, (cands, slots), 0)
    lane = lax.broadcasted_iota(I32, (1, slots), 1)
    before = (
        lax.broadcasted_iota(I32, (cands, cands), 0) < lax.broadcasted_iota(I32, (cands, cands), 1)
    ).astype(BF)
    place_c = lax.broadcasted_iota(I32, (slots, cands), 0).astype(F32)
    ones = jnp.ones((8, slots), BF)
    for copy in copies[:3]:
        copy.wait()
    start = jnp.int32(0)
    places = []
    for r in range(requests):
        valid = lane < count_ref[r]
        picked = jnp.where(valid, index_ref[r : r + 1, :], -1)
        match = (row_c == picked).astype(F32).astype(BF)
        used = jnp.where(dot_t(ones, match) > 0.5, 1.0, 0.0)
        position = dot(used.astype(BF), before)
        number = jnp.sum(used[0:1, :]).astype(I32)
        places.append(jnp.where(valid, dot(position.astype(BF), match)[0:1, :], -1.0))
        chosen = jnp.where((used[0:1, :] > 0.5) & (position[0:1, :] == place_c), 1.0, 0.0).astype(BF)
        mine = cands_ref[r]
        rows = dot(chosen, mine).astype(BF)
        pack_ref[pl.ds(pl.multiple_of(start, 16), slots), :] = dot(rows, wq_ref[...]).astype(BF)
        start = start + (((number + 15) >> 4) << 4)
        pack_ref[PRE_Q : PRE_Q + features, r * slots : (r + 1) * slots] = lax.dot_general(
            pre_wq_ref[...], mine, (((0,), (1,)), ((), ())), preferred_element_type=F32
        ).astype(BF)
    gain = gain_ref[...]
    high = gain.astype(BF).astype(F32)
    middle = (gain - high).astype(BF).astype(F32)
    per_row = width // 128
    small = [jnp.concatenate(places, axis=1), high, middle, gain - high - middle]
    for k in range(score_w_ref.shape[0] // per_row):
        lanes = [score_w_ref[i : i + 1, :].astype(F32) for i in range(k * per_row, (k + 1) * per_row)]
        small.append(jnp.concatenate(lanes, axis=1))
    small.append(jnp.zeros((PACK - SMALL - len(small), width), F32))
    pack_ref[SMALL:PACK, :] = jnp.concatenate(small, axis=0).astype(BF)
    for copy in copies[3:]:
        copy.wait()
    write = pltpu.make_async_copy(pack_ref, pack_hbm, out_sem)
    write.start()
    write.wait()


def attend(
    chunk_refs,
    pack_hbm,
    fixed_ref,
    query_ref,
    query_sem,
    keys_ref,
    values_ref,
    normed_ref,
    pre_out,
    up_copy,
):
    requests, slots = pre_out.shape
    events, width = keys_ref.shape
    half = width // 2
    head = width // HEADS
    features = chunk_refs[0].shape[-1]
    query_copy = pltpu.make_async_copy(pack_hbm.at[pl.ds(0, PRE_Q)], query_ref, query_sem)
    query_copy.start()
    up_copy.start()
    for h in range(HEADS):
        values_ref[:, (2 * h + 1) * head : (2 * h + 2) * head] = jnp.ones((events, head), BF)
    scale = LOG2E / math.sqrt(head)
    pre_w = slice(PRE_WKV - FIXED, PRE_WKV - FIXED + features)
    pre_scale = LOG2E / math.sqrt(features)
    small = fixed_ref[SMALL - FIXED : PACK - FIXED, :].astype(F32)
    gain = small[1:2, :] + small[2:3, :] + small[3:4, :]
    numbers = [jnp.max(small[0:1, r * slots : (r + 1) * slots]).astype(I32) + 1 for r in range(requests)]
    starts = [jnp.int32(0)]
    for number in numbers:
        starts.append(starts[-1] + (((number + 15) >> 4) << 4))

    def request(r, carry):
        number, start = numbers[0], starts[0]
        for k in range(1, requests):
            number, start = jnp.where(r == k, numbers[k], number), jnp.where(r == k, starts[k], start)
        parts = [ref[:, pl.ds(r, 1)].reshape(events // len(chunk_refs), features) for ref in chunk_refs]
        history = jnp.concatenate(parts, axis=0)

        def put_keys(c):
            cols = slice(c * half, (c + 1) * half)
            keys_ref[:, cols] = dot(history, fixed_ref[RANK_WK - FIXED : RANK_WV - FIXED, cols]).astype(BF)

        def put_values(c):
            part = dot(history, fixed_ref[RANK_WV - FIXED : SMALL - FIXED, c * half : (c + 1) * half]).astype(BF)
            for k in range(HEADS // 2):
                h = c * HEADS // 2 + k
                values_ref[:, 2 * h * head : (2 * h + 1) * head] = part[:, k * head : (k + 1) * head]

        pre_q = fixed_ref[PRE_Q - FIXED : PRE_Q - FIXED + features, pl.ds(pl.multiple_of(r * slots, slots), slots)]
        pre_keys = dot(history, fixed_ref[pre_w, :features]).astype(BF)
        pre_values = lax.dot_general(
            fixed_ref[pre_w, features : 2 * features],
            history,
            (((0,), (1,)), ((), ())),
            preferred_element_type=F32,
        ).astype(BF)
        put_keys(0)
        logits = dot(pre_keys, pre_q)
        put_keys(1)
        top = jnp.max(logits, axis=0, keepdims=True)
        weights = jnp.exp2((logits - top) * pre_scale)
        weights = (weights * (1.0 / jnp.sum(weights, axis=0, keepdims=True))).astype(BF)
        put_values(0)
        pooled = dot(pre_values, weights)
        put_values(1)
        query = pre_q.astype(F32)
        length = jnp.sqrt(jnp.sum(query * query, axis=0, keepdims=True))
        pre_out[pl.ds(r, 1), :] = jnp.sum(pooled * query, axis=0, keepdims=True) / (1.0 + length)
        pl.when(r == 0)(query_copy.wait)

        def tile(rows):
            at = pl.ds(pl.multiple_of(start, 16), rows)
            mixed = []
            for h in range(HEADS):
                cols = slice(h * head, (h + 1) * head)
                query = query_ref[at, cols]
                logits = dot_t(query, keys_ref[:, cols])
                top = jnp.max(logits, axis=1, keepdims=True)
                weights = jnp.exp2((logits - top) * scale).astype(BF)
                both = dot(weights, values_ref[:, 2 * h * head : (2 * h + 2) * head])
                mixed.append(query.astype(F32) + both[:, :head] / both[:, head:])
            acc = mixed[0]
            for one in mixed[1:]:
                acc = acc + one
            center = jnp.sum(acc, axis=1, keepdims=True) * (1.0 / width)
            acc = jnp.zeros((rows, head), F32)
            for one in mixed:
                acc = acc + (one - center) * (one - center)
            spread = jnp.sum(acc, axis=1, keepdims=True) * (1.0 / width)
            inverse = lax.rsqrt(spread + 1e-05)
            for h in range(HEADS):
                cols = slice(h * head, (h + 1) * head)
                normed_ref[at, cols] = ((mixed[h] - center) * inverse * gain[:, cols]).astype(BF)

        low = 0
        for rows in ROW_TILES:
            pl.when((number > low) & (number <= rows))(functools.partial(tile, rows))
            low = rows
        return carry

    lax.fori_loop(0, requests, request, 0)
    return starts, small


def rank_kernel(
    own_ref, a_ref, b_ref, c_ref, pack_hbm, fixed_ref, up_hbm,
    pre_out, rank_out,
    keys_ref, values_ref, query_ref, query_sem, normed_ref, ranked_ref, up_ref, sem,
):
    up_copy = pltpu.make_async_copy(up_hbm, up_ref, sem)
    requests, slots = rank_out.shape
    starts, small = attend(
        (own_ref, a_ref, b_ref, c_ref), pack_hbm, fixed_ref, query_ref, query_sem, keys_ref, values_ref, normed_ref,
        pre_out, up_copy,
    )
    up_copy.wait()
    width, hidden_size = up_ref.shape

    def mlp(first, count):
        at = pl.ds(pl.multiple_of(first, 16), count)
        rows = normed_ref[at, :]
        acc = jnp.zeros((count, 128), F32)
        for j in range(hidden_size // MLP_COLS):
            cols = slice(j * MLP_COLS, (j + 1) * MLP_COLS)
            x = dot(rows, up_ref[:, cols])
            x = x + x * jnp.tanh(x * (GELU_A + GELU_B * (x * x)))
            for k in range(MLP_COLS // 128):
                row, lane = divmod(j * MLP_COLS + k * 128, width)
                weight = 0.5 * small[4 + row : 5 + row, lane : lane + 128]
                acc = acc + x[:, k * 128 : (k + 1) * 128] * weight
        ranked_ref[at, :] = jnp.broadcast_to(jnp.sum(acc, axis=1, keepdims=True), acc.shape)

    def step(t, carry):
        first = t * MLP_ROWS[-1]
        left = starts[requests] - first
        low = 0
        for count in MLP_ROWS:
            high = count if count < MLP_ROWS[-1] else requests * slots
            pl.when((left > low) & (left <= high))(functools.partial(mlp, first, count))
            low = count
        return carry

    lax.fori_loop(0, (starts[requests] + MLP_ROWS[-1] - 1) // MLP_ROWS[-1], step, 0)
    row = lax.broadcasted_iota(I32, (slots, slots), 0).astype(F32)
    for r in range(requests):
        ranked = ranked_ref[pl.ds(pl.multiple_of(starts[r], 16), slots), :]
        ranked = jnp.concatenate([ranked] * (slots // 128), axis=1)
        hit = row == small[0:1, r * slots : (r + 1) * slots]
        rank_out[r : r + 1, :] = jnp.sum(jnp.where(hit, ranked, 0.0), axis=0, keepdims=True)


def select_call(surv_count, surv_index, cands, rank_wq, pre_wq, pre_wkv, rank_wkv, norm_gain, score_w):
    requests, slots = surv_index.shape
    width = rank_wq.shape[1]
    return pl.pallas_call(
        select_kernel,
        name="select",
        out_shape=jax.ShapeDtypeStruct((PACK, width), BF),
        in_specs=[SMEM, VMEM, HBM, HBM, HBM, HBM, HBM, VMEM, VMEM],
        out_specs=HBM,
        scratch_shapes=[
            pltpu.VMEM((PACK, width), BF),
            pltpu.VMEM(cands.shape, BF),
            pltpu.VMEM(rank_wq.shape, BF),
            pltpu.VMEM(pre_wq.shape, BF),
            pltpu.SemaphoreType.DMA((6,)),
            pltpu.SemaphoreType.DMA,
        ],
        compiler_params=pltpu.CompilerParams(vmem_limit_bytes=SELECT_LIMIT),
        cost_estimate=pl.CostEstimate(flops=2 * 10**9, bytes_accessed=12 * 2**20, transcendentals=0),
    )(
        surv_count.reshape(requests), surv_index, cands, rank_wq, pre_wq, pre_wkv, rank_wkv,
        norm_gain.reshape(1, -1), score_w.reshape(-1, 128),
    )


def stage_kernel(pack_hbm, fixed_ref, sem):
    copy = pltpu.make_async_copy(pack_hbm.at[pl.ds(FIXED, PACK - FIXED)], fixed_ref, sem)
    copy.start()
    copy.wait()


def stage_call(pack):
    return pl.pallas_call(
        stage_kernel,
        name="stage",
        out_shape=jax.ShapeDtypeStruct((PACK - FIXED, pack.shape[1]), BF),
        in_specs=[HBM],
        out_specs=VMEM,
        scratch_shapes=[pltpu.SemaphoreType.DMA],
        compiler_params=pltpu.CompilerParams(vmem_limit_bytes=STAGE_LIMIT),
        cost_estimate=pl.CostEstimate(flops=0, bytes_accessed=4 * 2**20, transcendentals=0),
    )(pack)


def rank_call(chunks, pack, fixed, mlp_up):
    nz, requests, here, _ = chunks[0].shape
    width = pack.shape[1]
    slots = width // requests
    events = len(chunks) * nz * here
    padded = -(-requests * slots // MLP_ROWS[-1]) * MLP_ROWS[-1]
    score = jax.ShapeDtypeStruct((requests, slots), F32)
    return pl.pallas_call(
        rank_kernel,
        name="rank",
        out_shape=(score, score),
        in_specs=[VMEM] * 4 + [HBM, VMEM, HBM],
        out_specs=(VMEM, VMEM),
        scratch_shapes=[
            pltpu.VMEM((events, width), BF),
            pltpu.VMEM((events, 2 * width), BF),
            pltpu.VMEM((PRE_Q, width), BF),
            pltpu.SemaphoreType.DMA,
            pltpu.VMEM((padded, width), BF),
            pltpu.VMEM((padded, 128), F32),
            pltpu.VMEM(mlp_up.shape, BF),
            pltpu.SemaphoreType.DMA,
        ],
        compiler_params=pltpu.CompilerParams(vmem_limit_bytes=RANK_LIMIT),
        cost_estimate=pl.CostEstimate(flops=16 * 10**9, bytes_accessed=20 * 2**20, transcendentals=4 * 10**6),
    )(*chunks, pack, fixed, mlp_up)


def body(history, cands, surv_count, surv_index, pre_wq, pre_wkv, rank_wq, rank_wkv, norm_gain, mlp_up, score_w):
    nx = 4
    nz = lax.axis_size("cand") // nx
    columns = [[z * nx + x for z in range(nz)] for x in range(nx)]

    def shift(x, by):
        pairs = [(z * nx + a, z * nx + (a + by) % nx) for z in range(nz) for a in range(nx)]
        return lax.ppermute(x, "cand", pairs)

    copies = jnp.broadcast_to(history[None], (nz,) + history.shape)
    own = lax.all_to_all(copies, "cand", split_axis=0, concat_axis=0, tiled=True, axis_index_groups=columns)
    pack = select_call(
        surv_count, surv_index, cands, rank_wq, pre_wq, pre_wkv, rank_wkv, norm_gain, score_w
    )
    chunks = [own] + [shift(own, by) for by in (1, 3, 2)]
    return rank_call(chunks, pack, stage_call(pack), mlp_up)


def solution(mesh):
    in_specs = (
        P("grp", "cand", None),
        P("grp", "cand", None),
        P("grp", "cand"),
        P("grp", "cand"),
        P(),
        P(),
        P(),
        P(),
        P(),
        P(),
        P(),
    )
    out_specs = (P("grp", "cand"), P("grp", "cand"))
    return jax.shard_map(body, mesh=mesh, in_specs=in_specs, out_specs=out_specs, check_vma=False)
```

```python
import functools
import math

import jax
import jax.numpy as jnp
from jax import lax
from jax.experimental import pallas as pl
from jax.experimental.pallas import tpu as pltpu
from jax.sharding import PartitionSpec as P

HEADS = 8
BF = jnp.bfloat16
F32 = jnp.float32
I32 = jnp.int32
LOG2E = 1.4426950408889634
GELU_A = math.sqrt(2.0 / math.pi)
GELU_B = GELU_A * 0.044715
ROW_TILES = (128, 176, 256)
MLP_ROWS = (128, 192, 256, 336)
MLP_COLS = 512
PRE_Q = 1024
PRE_WKV = 1280
RANK_WK = 1536
RANK_WV = 1792
SMALL = 2048
PACK = 2064
FIXED = PRE_Q
SELECT_LIMIT = 57 * 2**20
RANK_LIMIT = 50 * 2**20
STAGE_LIMIT = 50 * 2**20
VMEM = pl.BlockSpec(memory_space=pltpu.VMEM)
SMEM = pl.BlockSpec(memory_space=pltpu.SMEM)
HBM = pl.BlockSpec(memory_space=pltpu.HBM)
ANY = pl.BlockSpec(memory_space=pl.ANY)


def dot(a, b):
    return jnp.dot(a, b, preferred_element_type=F32)


def dot_t(a, b):
    return lax.dot_general(a, b, (((1,), (1,)), ((), ())), preferred_element_type=F32)


def select_kernel(
    count_ref,
    index_ref,
    cands_hbm,
    wq_hbm,
    pre_wq_hbm,
    pre_wkv_hbm,
    wkv_hbm,
    gain_ref,
    score_w_ref,
    pack_hbm,
    pack_ref,
    cands_ref,
    wq_ref,
    pre_wq_ref,
    sems,
    out_sem,
):
    width = pack_hbm.shape[1]
    pairs = (
        (cands_hbm, cands_ref),
        (wq_hbm, wq_ref),
        (pre_wq_hbm, pre_wq_ref),
        (pre_wkv_hbm, pack_ref.at[pl.ds(PRE_WKV, pre_wkv_hbm.shape[0]), pl.ds(0, pre_wkv_hbm.shape[1])]),
        (wkv_hbm.at[:, pl.ds(0, width)], pack_ref.at[pl.ds(RANK_WK, RANK_WV - RANK_WK)]),
        (wkv_hbm.at[:, pl.ds(width, width)], pack_ref.at[pl.ds(RANK_WV, SMALL - RANK_WV)]),
    )
    copies = [pltpu.make_async_copy(a, b, sems.at[i]) for i, (a, b) in enumerate(pairs)]
    for copy in copies:
        copy.start()
    requests, slots = index_ref.shape
    _, cands, features = cands_ref.shape
    row_c = lax.broadcasted_iota(I32, (cands, slots), 0)
    lane = lax.broadcasted_iota(I32, (1, slots), 1)
    before = (
        lax.broadcasted_iota(I32, (cands, cands), 0) < lax.broadcasted_iota(I32, (cands, cands), 1)
    ).astype(BF)
    place_c = lax.broadcasted_iota(I32, (slots, cands), 0).astype(F32)
    ones = jnp.ones((8, slots), BF)
    for copy in copies[:3]:
        copy.wait()
    start = jnp.int32(0)
    places = []
    for r in range(requests):
        valid = lane < count_ref[r]
        picked = jnp.where(valid, index_ref[r : r + 1, :], -1)
        match = (row_c == picked).astype(F32).astype(BF)
        used = jnp.where(dot_t(ones, match) > 0.5, 1.0, 0.0)
        position = dot(used.astype(BF), before)
        number = jnp.sum(used[0:1, :]).astype(I32)
        places.append(jnp.where(valid, dot(position.astype(BF), match)[0:1, :], -1.0))
        chosen = jnp.where((used[0:1, :] > 0.5) & (position[0:1, :] == place_c), 1.0, 0.0).astype(BF)
        mine = cands_ref[r]
        rows = dot(chosen, mine).astype(BF)
        pack_ref[pl.ds(pl.multiple_of(start, 16), slots), :] = dot(rows, wq_ref[...]).astype(BF)
        start = start + (((number + 15) >> 4) << 4)
        pack_ref[PRE_Q : PRE_Q + features, r * slots : (r + 1) * slots] = lax.dot_general(
            pre_wq_ref[...], mine, (((0,), (1,)), ((), ())), preferred_element_type=F32
        ).astype(BF)
    gain = gain_ref[...]
    high = gain.astype(BF).astype(F32)
    middle = (gain - high).astype(BF).astype(F32)
    per_row = width // 128
    small = [jnp.concatenate(places, axis=1), high, middle, gain - high - middle]
    for k in range(score_w_ref.shape[0] // per_row):
        lanes = [score_w_ref[i : i + 1, :].astype(F32) for i in range(k * per_row, (k + 1) * per_row)]
        small.append(jnp.concatenate(lanes, axis=1))
    small.append(jnp.zeros((PACK - SMALL - len(small), width), F32))
    pack_ref[SMALL:PACK, :] = jnp.concatenate(small, axis=0).astype(BF)
    for copy in copies[3:]:
        copy.wait()
    write = pltpu.make_async_copy(pack_ref, pack_hbm, out_sem)
    write.start()
    write.wait()


def attend(
    chunk_refs,
    pack_hbm,
    fixed_ref,
    query_ref,
    query_sem,
    keys_ref,
    values_ref,
    normed_ref,
    pre_out,
    up_copy,
):
    requests, slots = pre_out.shape
    events, width = keys_ref.shape
    half = width // 2
    head = width // HEADS
    features = chunk_refs[0].shape[-1]
    query_copy = pltpu.make_async_copy(pack_hbm.at[pl.ds(0, PRE_Q)], query_ref, query_sem)
    query_copy.start()
    up_copy.start()
    for h in range(HEADS):
        values_ref[:, (2 * h + 1) * head : (2 * h + 2) * head] = jnp.ones((events, head), BF)
    scale = LOG2E / math.sqrt(head)
    pre_w = slice(PRE_WKV - FIXED, PRE_WKV - FIXED + features)
    pre_scale = LOG2E / math.sqrt(features)
    small = fixed_ref[SMALL - FIXED : PACK - FIXED, :].astype(F32)
    gain = small[1:2, :] + small[2:3, :] + small[3:4, :]
    numbers = [jnp.max(small[0:1, r * slots : (r + 1) * slots]).astype(I32) + 1 for r in range(requests)]
    starts = [jnp.int32(0)]
    for number in numbers:
        starts.append(starts[-1] + (((number + 15) >> 4) << 4))

    def request(r, carry):
        number, start = numbers[0], starts[0]
        for k in range(1, requests):
            number, start = jnp.where(r == k, numbers[k], number), jnp.where(r == k, starts[k], start)
        parts = [ref[:, pl.ds(r, 1)].reshape(events // len(chunk_refs), features) for ref in chunk_refs]
        history = jnp.concatenate(parts, axis=0)

        def put_keys(c):
            cols = slice(c * half, (c + 1) * half)
            keys_ref[:, cols] = dot(history, fixed_ref[RANK_WK - FIXED : RANK_WV - FIXED, cols]).astype(BF)

        def put_values(c):
            part = dot(history, fixed_ref[RANK_WV - FIXED : SMALL - FIXED, c * half : (c + 1) * half]).astype(BF)
            for k in range(HEADS // 2):
                h = c * HEADS // 2 + k
                values_ref[:, 2 * h * head : (2 * h + 1) * head] = part[:, k * head : (k + 1) * head]

        pre_q = fixed_ref[PRE_Q - FIXED : PRE_Q - FIXED + features, pl.ds(pl.multiple_of(r * slots, slots), slots)]
        pre_keys = dot(history, fixed_ref[pre_w, :features]).astype(BF)
        pre_values = lax.dot_general(
            fixed_ref[pre_w, features : 2 * features],
            history,
            (((0,), (1,)), ((), ())),
            preferred_element_type=F32,
        ).astype(BF)
        put_keys(0)
        logits = dot(pre_keys, pre_q)
        put_keys(1)
        top = jnp.max(logits, axis=0, keepdims=True)
        weights = jnp.exp2((logits - top) * pre_scale)
        weights = (weights * (1.0 / jnp.sum(weights, axis=0, keepdims=True))).astype(BF)
        put_values(0)
        pooled = dot(pre_values, weights)
        put_values(1)
        query = pre_q.astype(F32)
        length = jnp.sqrt(jnp.sum(query * query, axis=0, keepdims=True))
        pre_out[pl.ds(r, 1), :] = jnp.sum(pooled * query, axis=0, keepdims=True) / (1.0 + length)
        pl.when(r == 0)(query_copy.wait)

        def tile(rows):
            at = pl.ds(pl.multiple_of(start, 16), rows)
            mixed = []
            for h in range(HEADS):
                cols = slice(h * head, (h + 1) * head)
                query = query_ref[at, cols]
                logits = dot_t(query, keys_ref[:, cols])
                top = jnp.max(logits, axis=1, keepdims=True)
                weights = jnp.exp2((logits - top) * scale).astype(BF)
                both = dot(weights, values_ref[:, 2 * h * head : (2 * h + 2) * head])
                mixed.append(query.astype(F32) + both[:, :head] / both[:, head:])
            acc = mixed[0]
            for one in mixed[1:]:
                acc = acc + one
            center = jnp.sum(acc, axis=1, keepdims=True) * (1.0 / width)
            acc = jnp.zeros((rows, head), F32)
            for one in mixed:
                acc = acc + (one - center) * (one - center)
            spread = jnp.sum(acc, axis=1, keepdims=True) * (1.0 / width)
            inverse = lax.rsqrt(spread + 1e-05)
            for h in range(HEADS):
                cols = slice(h * head, (h + 1) * head)
                normed_ref[at, cols] = ((mixed[h] - center) * inverse * gain[:, cols]).astype(BF)

        low = 0
        for rows in ROW_TILES:
            pl.when((number > low) & (number <= rows))(functools.partial(tile, rows))
            low = rows
        return carry

    lax.fori_loop(0, requests, request, 0)
    return starts, small


def rank_kernel(
    own_ref, a_ref, b_ref, c_ref, pack_hbm, fixed_ref, up_hbm,
    pre_out, rank_out,
    keys_ref, values_ref, query_ref, query_sem, normed_ref, ranked_ref, up_ref, sem,
):
    up_copy = pltpu.make_async_copy(up_hbm, up_ref, sem)
    requests, slots = rank_out.shape
    starts, small = attend(
        (own_ref, a_ref, b_ref, c_ref), pack_hbm, fixed_ref, query_ref, query_sem, keys_ref, values_ref, normed_ref,
        pre_out, up_copy,
    )
    up_copy.wait()
    width, hidden_size = up_ref.shape

    def mlp(first, count):
        at = pl.ds(pl.multiple_of(first, 16), count)
        rows = normed_ref[at, :]
        acc = jnp.zeros((count, 128), F32)
        for j in range(hidden_size // MLP_COLS):
            cols = slice(j * MLP_COLS, (j + 1) * MLP_COLS)
            x = dot(rows, up_ref[:, cols])
            x = x + x * jnp.tanh(x * (GELU_A + GELU_B * (x * x)))
            for k in range(MLP_COLS // 128):
                row, lane = divmod(j * MLP_COLS + k * 128, width)
                weight = 0.5 * small[4 + row : 5 + row, lane : lane + 128]
                acc = acc + x[:, k * 128 : (k + 1) * 128] * weight
        ranked_ref[at, :] = jnp.broadcast_to(jnp.sum(acc, axis=1, keepdims=True), acc.shape)

    def step(t, carry):
        first = t * MLP_ROWS[-1]
        left = starts[requests] - first
        low = 0
        for count in MLP_ROWS:
            high = count if count < MLP_ROWS[-1] else requests * slots
            pl.when((left > low) & (left <= high))(functools.partial(mlp, first, count))
            low = count
        return carry

    lax.fori_loop(0, (starts[requests] + MLP_ROWS[-1] - 1) // MLP_ROWS[-1], step, 0)
    row = lax.broadcasted_iota(I32, (slots, slots), 0).astype(F32)
    for r in range(requests):
        ranked = ranked_ref[pl.ds(pl.multiple_of(starts[r], 16), slots), :]
        ranked = jnp.concatenate([ranked] * (slots // 128), axis=1)
        hit = row == small[0:1, r * slots : (r + 1) * slots]
        rank_out[r : r + 1, :] = jnp.sum(jnp.where(hit, ranked, 0.0), axis=0, keepdims=True)


def select_call(surv_count, surv_index, cands, rank_wq, pre_wq, pre_wkv, rank_wkv, norm_gain, score_w):
    requests, slots = surv_index.shape
    width = rank_wq.shape[1]
    return pl.pallas_call(
        select_kernel,
        name="select",
        out_shape=jax.ShapeDtypeStruct((PACK, width), BF),
        in_specs=[SMEM, VMEM, HBM, HBM, HBM, HBM, HBM, VMEM, VMEM],
        out_specs=HBM,
        scratch_shapes=[
            pltpu.VMEM((PACK, width), BF),
            pltpu.VMEM(cands.shape, BF),
            pltpu.VMEM(rank_wq.shape, BF),
            pltpu.VMEM(pre_wq.shape, BF),
            pltpu.SemaphoreType.DMA((6,)),
            pltpu.SemaphoreType.DMA,
        ],
        compiler_params=pltpu.CompilerParams(vmem_limit_bytes=SELECT_LIMIT),
        cost_estimate=pl.CostEstimate(flops=2 * 10**9, bytes_accessed=12 * 2**20, transcendentals=0),
    )(
        surv_count.reshape(requests), surv_index, cands, rank_wq, pre_wq, pre_wkv, rank_wkv,
        norm_gain.reshape(1, -1), score_w.reshape(-1, 128),
    )


def after_kernel(x_ref, first_ref, out_ref):
    pass


def after(x, first):
    return pl.pallas_call(
        after_kernel,
        name="after",
        out_shape=jax.ShapeDtypeStruct(x.shape, x.dtype),
        in_specs=[ANY, ANY],
        out_specs=ANY,
        input_output_aliases={0: 0},
        compiler_params=pltpu.CompilerParams(vmem_limit_bytes=53 * 2**20),
    )(x, first)


def stage_kernel(pack_hbm, fixed_ref, sem):
    copy = pltpu.make_async_copy(pack_hbm.at[pl.ds(FIXED, PACK - FIXED)], fixed_ref, sem)
    copy.start()
    copy.wait()


def stage_call(pack):
    return pl.pallas_call(
        stage_kernel,
        name="stage",
        out_shape=jax.ShapeDtypeStruct((PACK - FIXED, pack.shape[1]), BF),
        in_specs=[HBM],
        out_specs=VMEM,
        scratch_shapes=[pltpu.SemaphoreType.DMA],
        compiler_params=pltpu.CompilerParams(vmem_limit_bytes=STAGE_LIMIT),
        cost_estimate=pl.CostEstimate(flops=0, bytes_accessed=4 * 2**20, transcendentals=0),
    )(pack)


def rank_call(chunks, pack, fixed, mlp_up):
    nz, requests, here, _ = chunks[0].shape
    width = pack.shape[1]
    slots = width // requests
    events = len(chunks) * nz * here
    padded = -(-requests * slots // MLP_ROWS[-1]) * MLP_ROWS[-1]
    score = jax.ShapeDtypeStruct((requests, slots), F32)
    return pl.pallas_call(
        rank_kernel,
        name="rank",
        out_shape=(score, score),
        in_specs=[VMEM] * 4 + [HBM, VMEM, HBM],
        out_specs=(VMEM, VMEM),
        scratch_shapes=[
            pltpu.VMEM((events, width), BF),
            pltpu.VMEM((events, 2 * width), BF),
            pltpu.VMEM((PRE_Q, width), BF),
            pltpu.SemaphoreType.DMA,
            pltpu.VMEM((padded, width), BF),
            pltpu.VMEM((padded, 128), F32),
            pltpu.VMEM(mlp_up.shape, BF),
            pltpu.SemaphoreType.DMA,
        ],
        compiler_params=pltpu.CompilerParams(vmem_limit_bytes=RANK_LIMIT),
        cost_estimate=pl.CostEstimate(flops=16 * 10**9, bytes_accessed=20 * 2**20, transcendentals=4 * 10**6),
    )(*chunks, pack, fixed, mlp_up)


def body(history, cands, surv_count, surv_index, pre_wq, pre_wkv, rank_wq, rank_wkv, norm_gain, mlp_up, score_w):
    nx = 4
    nz = lax.axis_size("cand") // nx
    columns = [[z * nx + x for z in range(nz)] for x in range(nx)]

    def shift(x, by):
        pairs = [(z * nx + a, z * nx + (a + by) % nx) for z in range(nz) for a in range(nx)]
        return lax.ppermute(x, "cand", pairs)

    copies = jnp.broadcast_to(history[None], (nz,) + history.shape)
    own = lax.all_to_all(copies, "cand", split_axis=0, concat_axis=0, tiled=True, axis_index_groups=columns)
    pack = select_call(
        surv_count, surv_index, cands, rank_wq, pre_wq, pre_wkv, rank_wkv, norm_gain, score_w
    )
    own = after(own, pack)
    chunks = [own] + [shift(own, by) for by in (1, 3, 2)]
    return rank_call(chunks, pack, stage_call(pack), mlp_up)


def solution(mesh):
    in_specs = (
        P("grp", "cand", None),
        P("grp", "cand", None),
        P("grp", "cand"),
        P("grp", "cand"),
        P(),
        P(),
        P(),
        P(),
        P(),
        P(),
        P(),
    )
    out_specs = (P("grp", "cand"), P("grp", "cand"))
    return jax.shard_map(body, mesh=mesh, in_specs=in_specs, out_specs=out_specs, check_vma=False)
```

```python
import functools
import math

import jax
import jax.numpy as jnp
from jax import lax
from jax.experimental import pallas as pl
from jax.experimental.pallas import tpu as pltpu
from jax.sharding import PartitionSpec as P

HEADS = 8
BF = jnp.bfloat16
F32 = jnp.float32
I32 = jnp.int32
LOG2E = 1.4426950408889634
GELU_A = math.sqrt(2.0 / math.pi)
GELU_B = GELU_A * 0.044715
ROW_TILES = (128, 176, 256)
MLP_ROWS = (128, 192, 256, 352)
MLP_COLS = 512
PRE_Q = 1024
PRE_WKV = 1280
RANK_WK = 1536
RANK_WV = 1792
SMALL = 2048
PACK = 2064
FIXED = PRE_Q
SELECT_LIMIT = 57 * 2**20
RANK_LIMIT = 50 * 2**20
STAGE_LIMIT = 50 * 2**20
VMEM = pl.BlockSpec(memory_space=pltpu.VMEM)
SMEM = pl.BlockSpec(memory_space=pltpu.SMEM)
HBM = pl.BlockSpec(memory_space=pltpu.HBM)


def dot(a, b):
    return jnp.dot(a, b, preferred_element_type=F32)


def dot_t(a, b):
    return lax.dot_general(a, b, (((1,), (1,)), ((), ())), preferred_element_type=F32)


def select_kernel(
    count_ref,
    index_ref,
    cands_hbm,
    wq_hbm,
    pre_wq_hbm,
    pre_wkv_hbm,
    wkv_hbm,
    gain_ref,
    score_w_ref,
    pack_hbm,
    pack_ref,
    cands_ref,
    wq_ref,
    pre_wq_ref,
    sems,
    out_sem,
):
    width = pack_hbm.shape[1]
    pairs = (
        (cands_hbm, cands_ref),
        (wq_hbm, wq_ref),
        (pre_wq_hbm, pre_wq_ref),
        (pre_wkv_hbm, pack_ref.at[pl.ds(PRE_WKV, pre_wkv_hbm.shape[0]), pl.ds(0, pre_wkv_hbm.shape[1])]),
        (wkv_hbm.at[:, pl.ds(0, width)], pack_ref.at[pl.ds(RANK_WK, RANK_WV - RANK_WK)]),
        (wkv_hbm.at[:, pl.ds(width, width)], pack_ref.at[pl.ds(RANK_WV, SMALL - RANK_WV)]),
    )
    copies = [pltpu.make_async_copy(a, b, sems.at[i]) for i, (a, b) in enumerate(pairs)]
    for copy in copies:
        copy.start()
    requests, slots = index_ref.shape
    _, cands, features = cands_ref.shape
    row_c = lax.broadcasted_iota(I32, (cands, slots), 0)
    lane = lax.broadcasted_iota(I32, (1, slots), 1)
    before = (
        lax.broadcasted_iota(I32, (cands, cands), 0) < lax.broadcasted_iota(I32, (cands, cands), 1)
    ).astype(BF)
    place_c = lax.broadcasted_iota(I32, (slots, cands), 0).astype(F32)
    ones = jnp.ones((8, slots), BF)
    for copy in copies[:3]:
        copy.wait()
    start = jnp.int32(0)
    places = []
    for r in range(requests):
        valid = lane < count_ref[r]
        picked = jnp.where(valid, index_ref[r : r + 1, :], -1)
        match = (row_c == picked).astype(F32).astype(BF)
        used = jnp.where(dot_t(ones, match) > 0.5, 1.0, 0.0)
        position = dot(used.astype(BF), before)
        number = jnp.sum(used[0:1, :]).astype(I32)
        places.append(jnp.where(valid, dot(position.astype(BF), match)[0:1, :], -1.0))
        chosen = jnp.where((used[0:1, :] > 0.5) & (position[0:1, :] == place_c), 1.0, 0.0).astype(BF)
        mine = cands_ref[r]
        rows = dot(chosen, mine).astype(BF)
        pack_ref[pl.ds(pl.multiple_of(start, 16), slots), :] = dot(rows, wq_ref[...]).astype(BF)
        start = start + (((number + 15) >> 4) << 4)
        pack_ref[PRE_Q : PRE_Q + features, r * slots : (r + 1) * slots] = lax.dot_general(
            pre_wq_ref[...], mine, (((0,), (1,)), ((), ())), preferred_element_type=F32
        ).astype(BF)
    gain = gain_ref[...]
    high = gain.astype(BF).astype(F32)
    middle = (gain - high).astype(BF).astype(F32)
    per_row = width // 128
    small = [jnp.concatenate(places, axis=1), high, middle, gain - high - middle]
    for k in range(score_w_ref.shape[0] // per_row):
        lanes = [score_w_ref[i : i + 1, :].astype(F32) for i in range(k * per_row, (k + 1) * per_row)]
        small.append(jnp.concatenate(lanes, axis=1))
    small.append(jnp.zeros((PACK - SMALL - len(small), width), F32))
    pack_ref[SMALL:PACK, :] = jnp.concatenate(small, axis=0).astype(BF)
    for copy in copies[3:]:
        copy.wait()
    write = pltpu.make_async_copy(pack_ref, pack_hbm, out_sem)
    write.start()
    write.wait()


def attend(
    chunk_refs,
    pack_hbm,
    fixed_ref,
    query_ref,
    query_sem,
    keys_ref,
    values_ref,
    normed_ref,
    pre_out,
    up_copy,
):
    requests, slots = pre_out.shape
    events, width = keys_ref.shape
    half = width // 2
    head = width // HEADS
    features = chunk_refs[0].shape[-1]
    query_copy = pltpu.make_async_copy(pack_hbm.at[pl.ds(0, PRE_Q)], query_ref, query_sem)
    query_copy.start()
    up_copy.start()
    for h in range(HEADS):
        values_ref[:, (2 * h + 1) * head : (2 * h + 2) * head] = jnp.ones((events, head), BF)
    scale = LOG2E / math.sqrt(head)
    pre_w = slice(PRE_WKV - FIXED, PRE_WKV - FIXED + features)
    pre_scale = LOG2E / math.sqrt(features)
    small = fixed_ref[SMALL - FIXED : PACK - FIXED, :].astype(F32)
    gain = small[1:2, :] + small[2:3, :] + small[3:4, :]
    numbers = [jnp.max(small[0:1, r * slots : (r + 1) * slots]).astype(I32) + 1 for r in range(requests)]
    starts = [jnp.int32(0)]
    for number in numbers:
        starts.append(starts[-1] + (((number + 15) >> 4) << 4))

    def request(r, carry):
        number, start = numbers[0], starts[0]
        for k in range(1, requests):
            number, start = jnp.where(r == k, numbers[k], number), jnp.where(r == k, starts[k], start)
        parts = [ref[:, pl.ds(r, 1)].reshape(events // len(chunk_refs), features) for ref in chunk_refs]
        history = jnp.concatenate(parts, axis=0)

        def put_keys(c):
            cols = slice(c * half, (c + 1) * half)
            keys_ref[:, cols] = dot(history, fixed_ref[RANK_WK - FIXED : RANK_WV - FIXED, cols]).astype(BF)

        def put_values(c):
            part = dot(history, fixed_ref[RANK_WV - FIXED : SMALL - FIXED, c * half : (c + 1) * half]).astype(BF)
            for k in range(HEADS // 2):
                h = c * HEADS // 2 + k
                values_ref[:, 2 * h * head : (2 * h + 1) * head] = part[:, k * head : (k + 1) * head]

        pre_q = fixed_ref[PRE_Q - FIXED : PRE_Q - FIXED + features, pl.ds(pl.multiple_of(r * slots, slots), slots)]
        pre_keys = dot(history, fixed_ref[pre_w, :features]).astype(BF)
        pre_values = lax.dot_general(
            fixed_ref[pre_w, features : 2 * features],
            history,
            (((0,), (1,)), ((), ())),
            preferred_element_type=F32,
        ).astype(BF)
        put_keys(0)
        logits = dot(pre_keys, pre_q)
        put_keys(1)
        top = jnp.max(logits, axis=0, keepdims=True)
        weights = jnp.exp2((logits - top) * pre_scale)
        weights = (weights * (1.0 / jnp.sum(weights, axis=0, keepdims=True))).astype(BF)
        put_values(0)
        pooled = dot(pre_values, weights)
        put_values(1)
        query = pre_q.astype(F32)
        length = jnp.sqrt(jnp.sum(query * query, axis=0, keepdims=True))
        pre_out[pl.ds(r, 1), :] = jnp.sum(pooled * query, axis=0, keepdims=True) / (1.0 + length)
        pl.when(r == 0)(query_copy.wait)

        def tile(rows):
            at = pl.ds(pl.multiple_of(start, 16), rows)
            mixed = []
            for h in range(HEADS):
                cols = slice(h * head, (h + 1) * head)
                query = query_ref[at, cols]
                logits = dot_t(query, keys_ref[:, cols])
                top = jnp.max(logits, axis=1, keepdims=True)
                weights = jnp.exp2((logits - top) * scale).astype(BF)
                both = dot(weights, values_ref[:, 2 * h * head : (2 * h + 2) * head])
                mixed.append(query.astype(F32) + both[:, :head] / both[:, head:])
            acc = mixed[0]
            for one in mixed[1:]:
                acc = acc + one
            center = jnp.sum(acc, axis=1, keepdims=True) * (1.0 / width)
            acc = jnp.zeros((rows, head), F32)
            for one in mixed:
                acc = acc + (one - center) * (one - center)
            spread = jnp.sum(acc, axis=1, keepdims=True) * (1.0 / width)
            inverse = lax.rsqrt(spread + 1e-05)
            for h in range(HEADS):
                cols = slice(h * head, (h + 1) * head)
                normed_ref[at, cols] = ((mixed[h] - center) * inverse * gain[:, cols]).astype(BF)

        low = 0
        for rows in ROW_TILES:
            pl.when((number > low) & (number <= rows))(functools.partial(tile, rows))
            low = rows
        return carry

    lax.fori_loop(0, requests, request, 0)
    return starts, small


def rank_kernel(
    own_ref, a_ref, b_ref, c_ref, pack_hbm, fixed_ref, up_hbm,
    pre_out, rank_out,
    keys_ref, values_ref, query_ref, query_sem, normed_ref, ranked_ref, up_ref, sem,
):
    up_copy = pltpu.make_async_copy(up_hbm, up_ref, sem)
    requests, slots = rank_out.shape
    starts, small = attend(
        (own_ref, a_ref, b_ref, c_ref), pack_hbm, fixed_ref, query_ref, query_sem, keys_ref, values_ref, normed_ref,
        pre_out, up_copy,
    )
    up_copy.wait()
    width, hidden_size = up_ref.shape

    def mlp(first, count):
        at = pl.ds(pl.multiple_of(first, 16), count)
        rows = normed_ref[at, :]
        acc = jnp.zeros((count, 128), F32)
        for j in range(hidden_size // MLP_COLS):
            cols = slice(j * MLP_COLS, (j + 1) * MLP_COLS)
            x = dot(rows, up_ref[:, cols])
            x = x + x * jnp.tanh(x * (GELU_A + GELU_B * (x * x)))
            for k in range(MLP_COLS // 128):
                row, lane = divmod(j * MLP_COLS + k * 128, width)
                weight = 0.5 * small[4 + row : 5 + row, lane : lane + 128]
                acc = acc + x[:, k * 128 : (k + 1) * 128] * weight
        ranked_ref[at, :] = jnp.broadcast_to(jnp.sum(acc, axis=1, keepdims=True), acc.shape)

    def step(t, carry):
        first = t * MLP_ROWS[-1]
        left = starts[requests] - first
        low = 0
        for count in MLP_ROWS:
            high = count if count < MLP_ROWS[-1] else requests * slots
            pl.when((left > low) & (left <= high))(functools.partial(mlp, first, count))
            low = count
        return carry

    lax.fori_loop(0, (starts[requests] + MLP_ROWS[-1] - 1) // MLP_ROWS[-1], step, 0)
    row = lax.broadcasted_iota(I32, (slots, slots), 0).astype(F32)
    for r in range(requests):
        ranked = ranked_ref[pl.ds(pl.multiple_of(starts[r], 16), slots), :]
        ranked = jnp.concatenate([ranked] * (slots // 128), axis=1)
        hit = row == small[0:1, r * slots : (r + 1) * slots]
        rank_out[r : r + 1, :] = jnp.sum(jnp.where(hit, ranked, 0.0), axis=0, keepdims=True)


def select_call(surv_count, surv_index, cands, rank_wq, pre_wq, pre_wkv, rank_wkv, norm_gain, score_w):
    requests, slots = surv_index.shape
    width = rank_wq.shape[1]
    return pl.pallas_call(
        select_kernel,
        name="select",
        out_shape=jax.ShapeDtypeStruct((PACK, width), BF),
        in_specs=[SMEM, VMEM, HBM, HBM, HBM, HBM, HBM, VMEM, VMEM],
        out_specs=HBM,
        scratch_shapes=[
            pltpu.VMEM((PACK, width), BF),
            pltpu.VMEM(cands.shape, BF),
            pltpu.VMEM(rank_wq.shape, BF),
            pltpu.VMEM(pre_wq.shape, BF),
            pltpu.SemaphoreType.DMA((6,)),
            pltpu.SemaphoreType.DMA,
        ],
        compiler_params=pltpu.CompilerParams(vmem_limit_bytes=SELECT_LIMIT),
        cost_estimate=pl.CostEstimate(flops=2 * 10**9, bytes_accessed=12 * 2**20, transcendentals=0),
    )(
        surv_count.reshape(requests), surv_index, cands, rank_wq, pre_wq, pre_wkv, rank_wkv,
        norm_gain.reshape(1, -1), score_w.reshape(-1, 128),
    )


def stage_kernel(pack_hbm, fixed_ref, sem):
    copy = pltpu.make_async_copy(pack_hbm.at[pl.ds(FIXED, PACK - FIXED)], fixed_ref, sem)
    copy.start()
    copy.wait()


def stage_call(pack):
    return pl.pallas_call(
        stage_kernel,
        name="stage",
        out_shape=jax.ShapeDtypeStruct((PACK - FIXED, pack.shape[1]), BF),
        in_specs=[HBM],
        out_specs=VMEM,
        scratch_shapes=[pltpu.SemaphoreType.DMA],
        compiler_params=pltpu.CompilerParams(vmem_limit_bytes=STAGE_LIMIT),
        cost_estimate=pl.CostEstimate(flops=0, bytes_accessed=4 * 2**20, transcendentals=0),
    )(pack)


def rank_call(chunks, pack, fixed, mlp_up):
    nz, requests, here, _ = chunks[0].shape
    width = pack.shape[1]
    slots = width // requests
    events = len(chunks) * nz * here
    padded = -(-requests * slots // MLP_ROWS[-1]) * MLP_ROWS[-1]
    score = jax.ShapeDtypeStruct((requests, slots), F32)
    return pl.pallas_call(
        rank_kernel,
        name="rank",
        out_shape=(score, score),
        in_specs=[VMEM] * 4 + [HBM, VMEM, HBM],
        out_specs=(VMEM, VMEM),
        scratch_shapes=[
            pltpu.VMEM((events, width), BF),
            pltpu.VMEM((events, 2 * width), BF),
            pltpu.VMEM((PRE_Q, width), BF),
            pltpu.SemaphoreType.DMA,
            pltpu.VMEM((padded, width), BF),
            pltpu.VMEM((padded, 128), F32),
            pltpu.VMEM(mlp_up.shape, BF),
            pltpu.SemaphoreType.DMA,
        ],
        compiler_params=pltpu.CompilerParams(vmem_limit_bytes=RANK_LIMIT),
        cost_estimate=pl.CostEstimate(flops=16 * 10**9, bytes_accessed=20 * 2**20, transcendentals=4 * 10**6),
    )(*chunks, pack, fixed, mlp_up)


def body(history, cands, surv_count, surv_index, pre_wq, pre_wkv, rank_wq, rank_wkv, norm_gain, mlp_up, score_w):
    nx = 4
    nz = lax.axis_size("cand") // nx
    columns = [[z * nx + x for z in range(nz)] for x in range(nx)]

    def shift(x, by):
        pairs = [(z * nx + a, z * nx + (a + by) % nx) for z in range(nz) for a in range(nx)]
        return lax.ppermute(x, "cand", pairs)

    copies = jnp.broadcast_to(history[None], (nz,) + history.shape)
    own = lax.all_to_all(copies, "cand", split_axis=0, concat_axis=0, tiled=True, axis_index_groups=columns)
    pack = select_call(
        surv_count, surv_index, cands, rank_wq, pre_wq, pre_wkv, rank_wkv, norm_gain, score_w
    )
    chunks = [own] + [shift(own, by) for by in (1, 3, 2)]
    return rank_call(chunks, pack, stage_call(pack), mlp_up)


def solution(mesh):
    in_specs = (
        P("grp", "cand", None),
        P("grp", "cand", None),
        P("grp", "cand"),
        P("grp", "cand"),
        P(),
        P(),
        P(),
        P(),
        P(),
        P(),
        P(),
    )
    out_specs = (P("grp", "cand"), P("grp", "cand"))
    return jax.shard_map(body, mesh=mesh, in_specs=in_specs, out_specs=out_specs, check_vma=False)
```

```python
import functools
import math

import jax
import jax.numpy as jnp
from jax import lax
from jax.experimental import pallas as pl
from jax.experimental.pallas import tpu as pltpu
from jax.sharding import PartitionSpec as P

HEADS = 8
BF = jnp.bfloat16
F32 = jnp.float32
I32 = jnp.int32
LOG2E = 1.4426950408889634
GELU_A = math.sqrt(2.0 / math.pi)
GELU_B = GELU_A * 0.044715
ROW_TILES = (128, 160, 176, 256)
MLP_ROWS = (128, 192, 256, 352)
MLP_COLS = 512
PRE_Q = 1024
PRE_WKV = 1280
RANK_WK = 1536
RANK_WV = 1792
SMALL = 2048
PACK = 2064
FIXED = PRE_Q
SELECT_LIMIT = 57 * 2**20
RANK_LIMIT = 50 * 2**20
STAGE_LIMIT = 50 * 2**20
VMEM = pl.BlockSpec(memory_space=pltpu.VMEM)
SMEM = pl.BlockSpec(memory_space=pltpu.SMEM)
HBM = pl.BlockSpec(memory_space=pltpu.HBM)


def dot(a, b):
    return jnp.dot(a, b, preferred_element_type=F32)


def dot_t(a, b):
    return lax.dot_general(a, b, (((1,), (1,)), ((), ())), preferred_element_type=F32)


def select_kernel(
    count_ref,
    index_ref,
    cands_hbm,
    wq_hbm,
    pre_wq_hbm,
    pre_wkv_hbm,
    wkv_hbm,
    gain_ref,
    score_w_ref,
    pack_hbm,
    pack_ref,
    cands_ref,
    wq_ref,
    pre_wq_ref,
    sems,
    out_sem,
):
    width = pack_hbm.shape[1]
    pairs = (
        (cands_hbm, cands_ref),
        (wq_hbm, wq_ref),
        (pre_wq_hbm, pre_wq_ref),
        (pre_wkv_hbm, pack_ref.at[pl.ds(PRE_WKV, pre_wkv_hbm.shape[0]), pl.ds(0, pre_wkv_hbm.shape[1])]),
        (wkv_hbm.at[:, pl.ds(0, width)], pack_ref.at[pl.ds(RANK_WK, RANK_WV - RANK_WK)]),
        (wkv_hbm.at[:, pl.ds(width, width)], pack_ref.at[pl.ds(RANK_WV, SMALL - RANK_WV)]),
    )
    copies = [pltpu.make_async_copy(a, b, sems.at[i]) for i, (a, b) in enumerate(pairs)]
    for copy in copies:
        copy.start()
    requests, slots = index_ref.shape
    _, cands, features = cands_ref.shape
    row_c = lax.broadcasted_iota(I32, (cands, slots), 0)
    lane = lax.broadcasted_iota(I32, (1, slots), 1)
    before = (
        lax.broadcasted_iota(I32, (cands, cands), 0) < lax.broadcasted_iota(I32, (cands, cands), 1)
    ).astype(BF)
    place_c = lax.broadcasted_iota(I32, (slots, cands), 0).astype(F32)
    ones = jnp.ones((8, slots), BF)
    for copy in copies[:3]:
        copy.wait()
    start = jnp.int32(0)
    places = []
    for r in range(requests):
        valid = lane < count_ref[r]
        picked = jnp.where(valid, index_ref[r : r + 1, :], -1)
        match = (row_c == picked).astype(F32).astype(BF)
        used = jnp.where(dot_t(ones, match) > 0.5, 1.0, 0.0)
        position = dot(used.astype(BF), before)
        number = jnp.sum(used[0:1, :]).astype(I32)
        places.append(jnp.where(valid, dot(position.astype(BF), match)[0:1, :], -1.0))
        chosen = jnp.where((used[0:1, :] > 0.5) & (position[0:1, :] == place_c), 1.0, 0.0).astype(BF)
        mine = cands_ref[r]
        rows = dot(chosen, mine).astype(BF)
        pack_ref[pl.ds(pl.multiple_of(start, 16), slots), :] = dot(rows, wq_ref[...]).astype(BF)
        start = start + (((number + 15) >> 4) << 4)
        pack_ref[PRE_Q : PRE_Q + features, r * slots : (r + 1) * slots] = lax.dot_general(
            pre_wq_ref[...], mine, (((0,), (1,)), ((), ())), preferred_element_type=F32
        ).astype(BF)
    gain = gain_ref[...]
    high = gain.astype(BF).astype(F32)
    middle = (gain - high).astype(BF).astype(F32)
    per_row = width // 128
    small = [jnp.concatenate(places, axis=1), high, middle, gain - high - middle]
    for k in range(score_w_ref.shape[0] // per_row):
        lanes = [score_w_ref[i : i + 1, :].astype(F32) for i in range(k * per_row, (k + 1) * per_row)]
        small.append(jnp.concatenate(lanes, axis=1))
    small.append(jnp.zeros((PACK - SMALL - len(small), width), F32))
    pack_ref[SMALL:PACK, :] = jnp.concatenate(small, axis=0).astype(BF)
    for copy in copies[3:]:
        copy.wait()
    write = pltpu.make_async_copy(pack_ref, pack_hbm, out_sem)
    write.start()
    write.wait()


def attend(
    chunk_refs,
    pack_hbm,
    fixed_ref,
    query_ref,
    query_sem,
    keys_ref,
    values_ref,
    normed_ref,
    pre_out,
    up_copy,
):
    requests, slots = pre_out.shape
    events, width = keys_ref.shape
    half = width // 2
    head = width // HEADS
    features = chunk_refs[0].shape[-1]
    query_copy = pltpu.make_async_copy(pack_hbm.at[pl.ds(0, PRE_Q)], query_ref, query_sem)
    query_copy.start()
    up_copy.start()
    for h in range(HEADS):
        values_ref[:, (2 * h + 1) * head : (2 * h + 2) * head] = jnp.ones((events, head), BF)
    scale = LOG2E / math.sqrt(head)
    pre_w = slice(PRE_WKV - FIXED, PRE_WKV - FIXED + features)
    pre_scale = LOG2E / math.sqrt(features)
    small = fixed_ref[SMALL - FIXED : PACK - FIXED, :].astype(F32)
    gain = small[1:2, :] + small[2:3, :] + small[3:4, :]
    numbers = [jnp.max(small[0:1, r * slots : (r + 1) * slots]).astype(I32) + 1 for r in range(requests)]
    starts = [jnp.int32(0)]
    for number in numbers:
        starts.append(starts[-1] + (((number + 15) >> 4) << 4))

    def request(r, carry):
        number, start = numbers[0], starts[0]
        for k in range(1, requests):
            number, start = jnp.where(r == k, numbers[k], number), jnp.where(r == k, starts[k], start)
        parts = [ref[:, pl.ds(r, 1)].reshape(events // len(chunk_refs), features) for ref in chunk_refs]
        history = jnp.concatenate(parts, axis=0)

        def put_keys(c):
            cols = slice(c * half, (c + 1) * half)
            keys_ref[:, cols] = dot(history, fixed_ref[RANK_WK - FIXED : RANK_WV - FIXED, cols]).astype(BF)

        def put_values(c):
            part = dot(history, fixed_ref[RANK_WV - FIXED : SMALL - FIXED, c * half : (c + 1) * half]).astype(BF)
            for k in range(HEADS // 2):
                h = c * HEADS // 2 + k
                values_ref[:, 2 * h * head : (2 * h + 1) * head] = part[:, k * head : (k + 1) * head]

        pre_q = fixed_ref[PRE_Q - FIXED : PRE_Q - FIXED + features, pl.ds(pl.multiple_of(r * slots, slots), slots)]
        pre_keys = dot(history, fixed_ref[pre_w, :features]).astype(BF)
        pre_values = lax.dot_general(
            fixed_ref[pre_w, features : 2 * features],
            history,
            (((0,), (1,)), ((), ())),
            preferred_element_type=F32,
        ).astype(BF)
        put_keys(0)
        logits = dot(pre_keys, pre_q)
        put_keys(1)
        top = jnp.max(logits, axis=0, keepdims=True)
        weights = jnp.exp2((logits - top) * pre_scale)
        weights = (weights * (1.0 / jnp.sum(weights, axis=0, keepdims=True))).astype(BF)
        put_values(0)
        pooled = dot(pre_values, weights)
        put_values(1)
        query = pre_q.astype(F32)
        length = jnp.sqrt(jnp.sum(query * query, axis=0, keepdims=True))
        pre_out[pl.ds(r, 1), :] = jnp.sum(pooled * query, axis=0, keepdims=True) / (1.0 + length)
        pl.when(r == 0)(query_copy.wait)

        def tile(rows):
            at = pl.ds(pl.multiple_of(start, 16), rows)
            mixed = []
            for h in range(HEADS):
                cols = slice(h * head, (h + 1) * head)
                query = query_ref[at, cols]
                logits = dot_t(query, keys_ref[:, cols])
                top = jnp.max(logits, axis=1, keepdims=True)
                weights = jnp.exp2((logits - top) * scale).astype(BF)
                both = dot(weights, values_ref[:, 2 * h * head : (2 * h + 2) * head])
                mixed.append(query.astype(F32) + both[:, :head] / both[:, head:])
            acc = mixed[0]
            for one in mixed[1:]:
                acc = acc + one
            center = jnp.sum(acc, axis=1, keepdims=True) * (1.0 / width)
            acc = jnp.zeros((rows, head), F32)
            for one in mixed:
                acc = acc + (one - center) * (one - center)
            spread = jnp.sum(acc, axis=1, keepdims=True) * (1.0 / width)
            inverse = lax.rsqrt(spread + 1e-05)
            for h in range(HEADS):
                cols = slice(h * head, (h + 1) * head)
                normed_ref[at, cols] = ((mixed[h] - center) * inverse * gain[:, cols]).astype(BF)

        low = 0
        for rows in ROW_TILES:
            pl.when((number > low) & (number <= rows))(functools.partial(tile, rows))
            low = rows
        return carry

    lax.fori_loop(0, requests, request, 0)
    return starts, small


def rank_kernel(
    own_ref, a_ref, b_ref, c_ref, pack_hbm, fixed_ref, up_hbm,
    pre_out, rank_out,
    keys_ref, values_ref, query_ref, query_sem, normed_ref, ranked_ref, up_ref, sem,
):
    up_copy = pltpu.make_async_copy(up_hbm, up_ref, sem)
    requests, slots = rank_out.shape
    starts, small = attend(
        (own_ref, a_ref, b_ref, c_ref), pack_hbm, fixed_ref, query_ref, query_sem, keys_ref, values_ref, normed_ref,
        pre_out, up_copy,
    )
    up_copy.wait()
    width, hidden_size = up_ref.shape

    def mlp(first, count):
        at = pl.ds(pl.multiple_of(first, 16), count)
        rows = normed_ref[at, :]
        acc = jnp.zeros((count, 128), F32)
        for j in range(hidden_size // MLP_COLS):
            cols = slice(j * MLP_COLS, (j + 1) * MLP_COLS)
            x = dot(rows, up_ref[:, cols])
            x = x + x * jnp.tanh(x * (GELU_A + GELU_B * (x * x)))
            for k in range(MLP_COLS // 128):
                row, lane = divmod(j * MLP_COLS + k * 128, width)
                weight = 0.5 * small[4 + row : 5 + row, lane : lane + 128]
                acc = acc + x[:, k * 128 : (k + 1) * 128] * weight
        ranked_ref[at, :] = jnp.broadcast_to(jnp.sum(acc, axis=1, keepdims=True), acc.shape)

    def step(t, carry):
        first = t * MLP_ROWS[-1]
        left = starts[requests] - first
        low = 0
        for count in MLP_ROWS:
            high = count if count < MLP_ROWS[-1] else requests * slots
            pl.when((left > low) & (left <= high))(functools.partial(mlp, first, count))
            low = count
        return carry

    lax.fori_loop(0, (starts[requests] + MLP_ROWS[-1] - 1) // MLP_ROWS[-1], step, 0)
    row = lax.broadcasted_iota(I32, (slots, slots), 0).astype(F32)
    for r in range(requests):
        ranked = ranked_ref[pl.ds(pl.multiple_of(starts[r], 16), slots), :]
        ranked = jnp.concatenate([ranked] * (slots // 128), axis=1)
        hit = row == small[0:1, r * slots : (r + 1) * slots]
        rank_out[r : r + 1, :] = jnp.sum(jnp.where(hit, ranked, 0.0), axis=0, keepdims=True)


def select_call(surv_count, surv_index, cands, rank_wq, pre_wq, pre_wkv, rank_wkv, norm_gain, score_w):
    requests, slots = surv_index.shape
    width = rank_wq.shape[1]
    return pl.pallas_call(
        select_kernel,
        name="select",
        out_shape=jax.ShapeDtypeStruct((PACK, width), BF),
        in_specs=[SMEM, VMEM, HBM, HBM, HBM, HBM, HBM, VMEM, VMEM],
        out_specs=HBM,
        scratch_shapes=[
            pltpu.VMEM((PACK, width), BF),
            pltpu.VMEM(cands.shape, BF),
            pltpu.VMEM(rank_wq.shape, BF),
            pltpu.VMEM(pre_wq.shape, BF),
            pltpu.SemaphoreType.DMA((6,)),
            pltpu.SemaphoreType.DMA,
        ],
        compiler_params=pltpu.CompilerParams(vmem_limit_bytes=SELECT_LIMIT),
        cost_estimate=pl.CostEstimate(flops=2 * 10**9, bytes_accessed=12 * 2**20, transcendentals=0),
    )(
        surv_count.reshape(requests), surv_index, cands, rank_wq, pre_wq, pre_wkv, rank_wkv,
        norm_gain.reshape(1, -1), score_w.reshape(-1, 128),
    )


def stage_kernel(pack_hbm, fixed_ref, sem):
    copy = pltpu.make_async_copy(pack_hbm.at[pl.ds(FIXED, PACK - FIXED)], fixed_ref, sem)
    copy.start()
    copy.wait()


def stage_call(pack):
    return pl.pallas_call(
        stage_kernel,
        name="stage",
        out_shape=jax.ShapeDtypeStruct((PACK - FIXED, pack.shape[1]), BF),
        in_specs=[HBM],
        out_specs=VMEM,
        scratch_shapes=[pltpu.SemaphoreType.DMA],
        compiler_params=pltpu.CompilerParams(vmem_limit_bytes=STAGE_LIMIT),
        cost_estimate=pl.CostEstimate(flops=0, bytes_accessed=4 * 2**20, transcendentals=0),
    )(pack)


def rank_call(chunks, pack, fixed, mlp_up):
    nz, requests, here, _ = chunks[0].shape
    width = pack.shape[1]
    slots = width // requests
    events = len(chunks) * nz * here
    padded = -(-requests * slots // MLP_ROWS[-1]) * MLP_ROWS[-1]
    score = jax.ShapeDtypeStruct((requests, slots), F32)
    return pl.pallas_call(
        rank_kernel,
        name="rank",
        out_shape=(score, score),
        in_specs=[VMEM] * 4 + [HBM, VMEM, HBM],
        out_specs=(VMEM, VMEM),
        scratch_shapes=[
            pltpu.VMEM((events, width), BF),
            pltpu.VMEM((events, 2 * width), BF),
            pltpu.VMEM((PRE_Q, width), BF),
            pltpu.SemaphoreType.DMA,
            pltpu.VMEM((padded, width), BF),
            pltpu.VMEM((padded, 128), F32),
            pltpu.VMEM(mlp_up.shape, BF),
            pltpu.SemaphoreType.DMA,
        ],
        compiler_params=pltpu.CompilerParams(vmem_limit_bytes=RANK_LIMIT),
        cost_estimate=pl.CostEstimate(flops=16 * 10**9, bytes_accessed=20 * 2**20, transcendentals=4 * 10**6),
    )(*chunks, pack, fixed, mlp_up)


def body(history, cands, surv_count, surv_index, pre_wq, pre_wkv, rank_wq, rank_wkv, norm_gain, mlp_up, score_w):
    nx = 4
    nz = lax.axis_size("cand") // nx
    columns = [[z * nx + x for z in range(nz)] for x in range(nx)]

    def shift(x, by):
        pairs = [(z * nx + a, z * nx + (a + by) % nx) for z in range(nz) for a in range(nx)]
        return lax.ppermute(x, "cand", pairs)

    copies = jnp.broadcast_to(history[None], (nz,) + history.shape)
    own = lax.all_to_all(copies, "cand", split_axis=0, concat_axis=0, tiled=True, axis_index_groups=columns)
    pack = select_call(
        surv_count, surv_index, cands, rank_wq, pre_wq, pre_wkv, rank_wkv, norm_gain, score_w
    )
    chunks = [own] + [shift(own, by) for by in (1, 3, 2)]
    return rank_call(chunks, pack, stage_call(pack), mlp_up)


def solution(mesh):
    in_specs = (
        P("grp", "cand", None),
        P("grp", "cand", None),
        P("grp", "cand"),
        P("grp", "cand"),
        P(),
        P(),
        P(),
        P(),
        P(),
        P(),
        P(),
    )
    out_specs = (P("grp", "cand"), P("grp", "cand"))
    return jax.shard_map(body, mesh=mesh, in_specs=in_specs, out_specs=out_specs, check_vma=False)
```

```python
import functools
import math

import jax
import jax.numpy as jnp
from jax import lax
from jax.experimental import pallas as pl
from jax.experimental.pallas import tpu as pltpu
from jax.sharding import PartitionSpec as P

HEADS = 8
BF = jnp.bfloat16
F32 = jnp.float32
I32 = jnp.int32
LOG2E = 1.4426950408889634
GELU_A = math.sqrt(2.0 / math.pi)
GELU_B = GELU_A * 0.044715
ROW_TILES = (96, 128, 160, 176, 256)
MLP_ROWS = (128, 192, 256, 352)
MLP_COLS = 512
PRE_Q = 1024
PRE_WKV = 1280
RANK_WK = 1536
RANK_WV = 1792
SMALL = 2048
PACK = 2064
FIXED = PRE_Q
SELECT_LIMIT = 57 * 2**20
RANK_LIMIT = 50 * 2**20
STAGE_LIMIT = 50 * 2**20
VMEM = pl.BlockSpec(memory_space=pltpu.VMEM)
SMEM = pl.BlockSpec(memory_space=pltpu.SMEM)
HBM = pl.BlockSpec(memory_space=pltpu.HBM)


def dot(a, b):
    return jnp.dot(a, b, preferred_element_type=F32)


def dot_t(a, b):
    return lax.dot_general(a, b, (((1,), (1,)), ((), ())), preferred_element_type=F32)


def select_kernel(
    count_ref,
    index_ref,
    cands_hbm,
    wq_hbm,
    pre_wq_hbm,
    pre_wkv_hbm,
    wkv_hbm,
    gain_ref,
    score_w_ref,
    pack_hbm,
    pack_ref,
    cands_ref,
    wq_ref,
    pre_wq_ref,
    sems,
    out_sem,
):
    width = pack_hbm.shape[1]
    pairs = (
        (cands_hbm, cands_ref),
        (wq_hbm, wq_ref),
        (pre_wq_hbm, pre_wq_ref),
        (pre_wkv_hbm, pack_ref.at[pl.ds(PRE_WKV, pre_wkv_hbm.shape[0]), pl.ds(0, pre_wkv_hbm.shape[1])]),
        (wkv_hbm.at[:, pl.ds(0, width)], pack_ref.at[pl.ds(RANK_WK, RANK_WV - RANK_WK)]),
        (wkv_hbm.at[:, pl.ds(width, width)], pack_ref.at[pl.ds(RANK_WV, SMALL - RANK_WV)]),
    )
    copies = [pltpu.make_async_copy(a, b, sems.at[i]) for i, (a, b) in enumerate(pairs)]
    for copy in copies:
        copy.start()
    requests, slots = index_ref.shape
    _, cands, features = cands_ref.shape
    row_c = lax.broadcasted_iota(I32, (cands, slots), 0)
    lane = lax.broadcasted_iota(I32, (1, slots), 1)
    before = (
        lax.broadcasted_iota(I32, (cands, cands), 0) < lax.broadcasted_iota(I32, (cands, cands), 1)
    ).astype(BF)
    place_c = lax.broadcasted_iota(I32, (slots, cands), 0).astype(F32)
    ones = jnp.ones((8, slots), BF)
    for copy in copies[:3]:
        copy.wait()
    start = jnp.int32(0)
    places = []
    for r in range(requests):
        valid = lane < count_ref[r]
        picked = jnp.where(valid, index_ref[r : r + 1, :], -1)
        match = (row_c == picked).astype(F32).astype(BF)
        used = jnp.where(dot_t(ones, match) > 0.5, 1.0, 0.0)
        position = dot(used.astype(BF), before)
        number = jnp.sum(used[0:1, :]).astype(I32)
        places.append(jnp.where(valid, dot(position.astype(BF), match)[0:1, :], -1.0))
        chosen = jnp.where((used[0:1, :] > 0.5) & (position[0:1, :] == place_c), 1.0, 0.0).astype(BF)
        mine = cands_ref[r]
        rows = dot(chosen, mine).astype(BF)
        pack_ref[pl.ds(pl.multiple_of(start, 16), slots), :] = dot(rows, wq_ref[...]).astype(BF)
        start = start + (((number + 15) >> 4) << 4)
        pack_ref[PRE_Q : PRE_Q + features, r * slots : (r + 1) * slots] = lax.dot_general(
            pre_wq_ref[...], mine, (((0,), (1,)), ((), ())), preferred_element_type=F32
        ).astype(BF)
    gain = gain_ref[...]
    high = gain.astype(BF).astype(F32)
    middle = (gain - high).astype(BF).astype(F32)
    per_row = width // 128
    small = [jnp.concatenate(places, axis=1), high, middle, gain - high - middle]
    for k in range(score_w_ref.shape[0] // per_row):
        lanes = [score_w_ref[i : i + 1, :].astype(F32) for i in range(k * per_row, (k + 1) * per_row)]
        small.append(jnp.concatenate(lanes, axis=1))
    small.append(jnp.zeros((PACK - SMALL - len(small), width), F32))
    pack_ref[SMALL:PACK, :] = jnp.concatenate(small, axis=0).astype(BF)
    for copy in copies[3:]:
        copy.wait()
    write = pltpu.make_async_copy(pack_ref, pack_hbm, out_sem)
    write.start()
    write.wait()


def attend(
    chunk_refs,
    pack_hbm,
    fixed_ref,
    query_ref,
    query_sem,
    keys_ref,
    values_ref,
    normed_ref,
    pre_out,
    up_copy,
):
    requests, slots = pre_out.shape
    events, width = keys_ref.shape
    half = width // 2
    head = width // HEADS
    features = chunk_refs[0].shape[-1]
    query_copy = pltpu.make_async_copy(pack_hbm.at[pl.ds(0, PRE_Q)], query_ref, query_sem)
    query_copy.start()
    up_copy.start()
    for h in range(HEADS):
        values_ref[:, (2 * h + 1) * head : (2 * h + 2) * head] = jnp.ones((events, head), BF)
    scale = LOG2E / math.sqrt(head)
    pre_w = slice(PRE_WKV - FIXED, PRE_WKV - FIXED + features)
    pre_scale = LOG2E / math.sqrt(features)
    small = fixed_ref[SMALL - FIXED : PACK - FIXED, :].astype(F32)
    gain = small[1:2, :] + small[2:3, :] + small[3:4, :]
    numbers = [jnp.max(small[0:1, r * slots : (r + 1) * slots]).astype(I32) + 1 for r in range(requests)]
    starts = [jnp.int32(0)]
    for number in numbers:
        starts.append(starts[-1] + (((number + 15) >> 4) << 4))

    def request(r, carry):
        number, start = numbers[0], starts[0]
        for k in range(1, requests):
            number, start = jnp.where(r == k, numbers[k], number), jnp.where(r == k, starts[k], start)
        parts = [ref[:, pl.ds(r, 1)].reshape(events // len(chunk_refs), features) for ref in chunk_refs]
        history = jnp.concatenate(parts, axis=0)

        def put_keys(c):
            cols = slice(c * half, (c + 1) * half)
            keys_ref[:, cols] = dot(history, fixed_ref[RANK_WK - FIXED : RANK_WV - FIXED, cols]).astype(BF)

        def put_values(c):
            part = dot(history, fixed_ref[RANK_WV - FIXED : SMALL - FIXED, c * half : (c + 1) * half]).astype(BF)
            for k in range(HEADS // 2):
                h = c * HEADS // 2 + k
                values_ref[:, 2 * h * head : (2 * h + 1) * head] = part[:, k * head : (k + 1) * head]

        pre_q = fixed_ref[PRE_Q - FIXED : PRE_Q - FIXED + features, pl.ds(pl.multiple_of(r * slots, slots), slots)]
        pre_keys = dot(history, fixed_ref[pre_w, :features]).astype(BF)
        pre_values = lax.dot_general(
            fixed_ref[pre_w, features : 2 * features],
            history,
            (((0,), (1,)), ((), ())),
            preferred_element_type=F32,
        ).astype(BF)
        put_keys(0)
        logits = dot(pre_keys, pre_q)
        put_keys(1)
        top = jnp.max(logits, axis=0, keepdims=True)
        weights = jnp.exp2((logits - top) * pre_scale)
        weights = (weights * (1.0 / jnp.sum(weights, axis=0, keepdims=True))).astype(BF)
        put_values(0)
        pooled = dot(pre_values, weights)
        put_values(1)
        query = pre_q.astype(F32)
        length = jnp.sqrt(jnp.sum(query * query, axis=0, keepdims=True))
        pre_out[pl.ds(r, 1), :] = jnp.sum(pooled * query, axis=0, keepdims=True) / (1.0 + length)
        pl.when(r == 0)(query_copy.wait)

        def tile(rows):
            at = pl.ds(pl.multiple_of(start, 16), rows)
            mixed = []
            for h in range(HEADS):
                cols = slice(h * head, (h + 1) * head)
                query = query_ref[at, cols]
                logits = dot_t(query, keys_ref[:, cols])
                top = jnp.max(logits, axis=1, keepdims=True)
                weights = jnp.exp2((logits - top) * scale).astype(BF)
                both = dot(weights, values_ref[:, 2 * h * head : (2 * h + 2) * head])
                mixed.append(query.astype(F32) + both[:, :head] / both[:, head:])
            acc = mixed[0]
            for one in mixed[1:]:
                acc = acc + one
            center = jnp.sum(acc, axis=1, keepdims=True) * (1.0 / width)
            acc = jnp.zeros((rows, head), F32)
            for one in mixed:
                acc = acc + (one - center) * (one - center)
            spread = jnp.sum(acc, axis=1, keepdims=True) * (1.0 / width)
            inverse = lax.rsqrt(spread + 1e-05)
            for h in range(HEADS):
                cols = slice(h * head, (h + 1) * head)
                normed_ref[at, cols] = ((mixed[h] - center) * inverse * gain[:, cols]).astype(BF)

        low = 0
        for rows in ROW_TILES:
            pl.when((number > low) & (number <= rows))(functools.partial(tile, rows))
            low = rows
        return carry

    lax.fori_loop(0, requests, request, 0)
    return starts, small


def rank_kernel(
    own_ref, a_ref, b_ref, c_ref, pack_hbm, fixed_ref, up_hbm,
    pre_out, rank_out,
    keys_ref, values_ref, query_ref, query_sem, normed_ref, ranked_ref, up_ref, sem,
):
    up_copy = pltpu.make_async_copy(up_hbm, up_ref, sem)
    requests, slots = rank_out.shape
    starts, small = attend(
        (own_ref, a_ref, b_ref, c_ref), pack_hbm, fixed_ref, query_ref, query_sem, keys_ref, values_ref, normed_ref,
        pre_out, up_copy,
    )
    up_copy.wait()
    width, hidden_size = up_ref.shape

    def mlp(first, count):
        at = pl.ds(pl.multiple_of(first, 16), count)
        rows = normed_ref[at, :]
        acc = jnp.zeros((count, 128), F32)
        for j in range(hidden_size // MLP_COLS):
            cols = slice(j * MLP_COLS, (j + 1) * MLP_COLS)
            x = dot(rows, up_ref[:, cols])
            x = x + x * jnp.tanh(x * (GELU_A + GELU_B * (x * x)))
            for k in range(MLP_COLS // 128):
                row, lane = divmod(j * MLP_COLS + k * 128, width)
                weight = 0.5 * small[4 + row : 5 + row, lane : lane + 128]
                acc = acc + x[:, k * 128 : (k + 1) * 128] * weight
        ranked_ref[at, :] = jnp.broadcast_to(jnp.sum(acc, axis=1, keepdims=True), acc.shape)

    def step(t, carry):
        first = t * MLP_ROWS[-1]
        left = starts[requests] - first
        low = 0
        for count in MLP_ROWS:
            high = count if count < MLP_ROWS[-1] else requests * slots
            pl.when((left > low) & (left <= high))(functools.partial(mlp, first, count))
            low = count
        return carry

    lax.fori_loop(0, (starts[requests] + MLP_ROWS[-1] - 1) // MLP_ROWS[-1], step, 0)
    row = lax.broadcasted_iota(I32, (slots, slots), 0).astype(F32)
    for r in range(requests):
        ranked = ranked_ref[pl.ds(pl.multiple_of(starts[r], 16), slots), :]
        ranked = jnp.concatenate([ranked] * (slots // 128), axis=1)
        hit = row == small[0:1, r * slots : (r + 1) * slots]
        rank_out[r : r + 1, :] = jnp.sum(jnp.where(hit, ranked, 0.0), axis=0, keepdims=True)


def select_call(surv_count, surv_index, cands, rank_wq, pre_wq, pre_wkv, rank_wkv, norm_gain, score_w):
    requests, slots = surv_index.shape
    width = rank_wq.shape[1]
    return pl.pallas_call(
        select_kernel,
        name="select",
        out_shape=jax.ShapeDtypeStruct((PACK, width), BF),
        in_specs=[SMEM, VMEM, HBM, HBM, HBM, HBM, HBM, VMEM, VMEM],
        out_specs=HBM,
        scratch_shapes=[
            pltpu.VMEM((PACK, width), BF),
            pltpu.VMEM(cands.shape, BF),
            pltpu.VMEM(rank_wq.shape, BF),
            pltpu.VMEM(pre_wq.shape, BF),
            pltpu.SemaphoreType.DMA((6,)),
            pltpu.SemaphoreType.DMA,
        ],
        compiler_params=pltpu.CompilerParams(vmem_limit_bytes=SELECT_LIMIT),
        cost_estimate=pl.CostEstimate(flops=2 * 10**9, bytes_accessed=12 * 2**20, transcendentals=0),
    )(
        surv_count.reshape(requests), surv_index, cands, rank_wq, pre_wq, pre_wkv, rank_wkv,
        norm_gain.reshape(1, -1), score_w.reshape(-1, 128),
    )


def stage_kernel(pack_hbm, fixed_ref, sem):
    copy = pltpu.make_async_copy(pack_hbm.at[pl.ds(FIXED, PACK - FIXED)], fixed_ref, sem)
    copy.start()
    copy.wait()


def stage_call(pack):
    return pl.pallas_call(
        stage_kernel,
        name="stage",
        out_shape=jax.ShapeDtypeStruct((PACK - FIXED, pack.shape[1]), BF),
        in_specs=[HBM],
        out_specs=VMEM,
        scratch_shapes=[pltpu.SemaphoreType.DMA],
        compiler_params=pltpu.CompilerParams(vmem_limit_bytes=STAGE_LIMIT),
        cost_estimate=pl.CostEstimate(flops=0, bytes_accessed=4 * 2**20, transcendentals=0),
    )(pack)


def rank_call(chunks, pack, fixed, mlp_up):
    nz, requests, here, _ = chunks[0].shape
    width = pack.shape[1]
    slots = width // requests
    events = len(chunks) * nz * here
    padded = -(-requests * slots // MLP_ROWS[-1]) * MLP_ROWS[-1]
    score = jax.ShapeDtypeStruct((requests, slots), F32)
    return pl.pallas_call(
        rank_kernel,
        name="rank",
        out_shape=(score, score),
        in_specs=[VMEM] * 4 + [HBM, VMEM, HBM],
        out_specs=(VMEM, VMEM),
        scratch_shapes=[
            pltpu.VMEM((events, width), BF),
            pltpu.VMEM((events, 2 * width), BF),
            pltpu.VMEM((PRE_Q, width), BF),
            pltpu.SemaphoreType.DMA,
            pltpu.VMEM((padded, width), BF),
            pltpu.VMEM((padded, 128), F32),
            pltpu.VMEM(mlp_up.shape, BF),
            pltpu.SemaphoreType.DMA,
        ],
        compiler_params=pltpu.CompilerParams(vmem_limit_bytes=RANK_LIMIT),
        cost_estimate=pl.CostEstimate(flops=16 * 10**9, bytes_accessed=20 * 2**20, transcendentals=4 * 10**6),
    )(*chunks, pack, fixed, mlp_up)


def body(history, cands, surv_count, surv_index, pre_wq, pre_wkv, rank_wq, rank_wkv, norm_gain, mlp_up, score_w):
    nx = 4
    nz = lax.axis_size("cand") // nx
    columns = [[z * nx + x for z in range(nz)] for x in range(nx)]

    def shift(x, by):
        pairs = [(z * nx + a, z * nx + (a + by) % nx) for z in range(nz) for a in range(nx)]
        return lax.ppermute(x, "cand", pairs)

    copies = jnp.broadcast_to(history[None], (nz,) + history.shape)
    own = lax.all_to_all(copies, "cand", split_axis=0, concat_axis=0, tiled=True, axis_index_groups=columns)
    pack = select_call(
        surv_count, surv_index, cands, rank_wq, pre_wq, pre_wkv, rank_wkv, norm_gain, score_w
    )
    chunks = [own] + [shift(own, by) for by in (1, 3, 2)]
    return rank_call(chunks, pack, stage_call(pack), mlp_up)


def solution(mesh):
    in_specs = (
        P("grp", "cand", None),
        P("grp", "cand", None),
        P("grp", "cand"),
        P("grp", "cand"),
        P(),
        P(),
        P(),
        P(),
        P(),
        P(),
        P(),
    )
    out_specs = (P("grp", "cand"), P("grp", "cand"))
    return jax.shard_map(body, mesh=mesh, in_specs=in_specs, out_specs=out_specs, check_vma=False)
```
